256 devices in a mesh: dp: 64 (over y, z, core), seq: 4 (over x).
Axes of the slice: x: 4, y: 4, z: 8, core: 2. Of those that a mesh axis runs over, the one named last changes fastest.
Arguments:
- tokens: bfloat16 [64, 768, 1536], P('dp', 'seq'), may hold values from -6 to 6
- cotangent: bfloat16 [64, 768, 1536], P('dp', 'seq'), may hold values from -6 to 6
- condition: bfloat16 [64, 2, 3072], P('dp'), may hold values from -6 to 6
- per_image_rows: int32 [64, 2], replicated, may hold values from 1 to 96, as said below
- query_key_value_weight: bfloat16 [1536, 4608], P('dp'), may hold values from -1 to 1
- adapter_down: bfloat16 [1536, 64], replicated, may hold values from -0.15625 to 0.15625
- adapter_up: bfloat16 [64, 4608], replicated, may hold values from -0.75 to 0.75
- modulation_matrix: bfloat16 [3072, 3072], P('dp'), may hold values from -0.109375 to 0.109375
Outputs:
- attention: bfloat16 [64, 768, 1536], P('dp', 'seq')
- token_grad: bfloat16 [64, 768, 1536], P('dp', 'seq')
- down_grad: float32 [1536, 64], P('dp')
- up_grad: float32 [64, 4608], P(None, 'dp')
- modulation_grad: float32 [3072, 3072], P('dp')
The draws below stay inside these ranges and needn't reach their ends.
Inputs may be any that keep to these rules, and one draw needn't show every extreme that they name: Each group's two images take per_image_rows[g, 0] and per_image_rows[g, 1] rows of each of the group's 4 devices; a group fills 2 to 192 rows, the rows of all groups sum to exactly 6144, and some group fills all 192 rows.
All inputs are finite; a program needn't handle non-finite values.
Results may differ from the reference program's by a relative error of at most 0.025.
Values may be sent and summed in bfloat16 or wider, within the bound.
A program may use at most 128 MiB of HBM per device.

```python
import jax
import jax.numpy as jnp
from jax import lax

MODEL_WIDTH = 1536
LOCAL_HEADS = 12
HEAD_SIZE = 128
VEC = 3072
ADAPTER_RANK = 64
IMGS = 2
ROWS_DEV = 192
GROUPS = 64
SEQ_LEN = 768


def draw_per_image_rows(key, part):
    key = jax.random.fold_in(key, 11)
    key_order, key_pairs, key_quad, key_split = jax.random.split(key, 4)
    half_rows = ROWS_DEV // 2
    ordering = jax.random.permutation(key_order, GROUPS)
    paired = jax.random.randint(key_pairs, ((GROUPS - 4) // 2,), 2, 2 * half_rows - 1).astype(jnp.int32)
    quartet = jax.random.randint(key_quad, (2,), 2, half_rows).astype(jnp.int32)
    full_group = jnp.array([2 * half_rows], jnp.int32)
    closing = (2 * half_rows - jnp.sum(quartet)).astype(jnp.int32)[None]
    partners = jnp.stack([paired, 2 * half_rows - paired], axis=1).reshape(-1).astype(jnp.int32)
    listed = jnp.concatenate([full_group, quartet, closing, partners])
    totals = jnp.zeros((GROUPS,), jnp.int32).at[ordering].set(listed)
    lowest = jnp.maximum(1, totals - half_rows)
    highest = jnp.minimum(totals - 1, half_rows)
    first_image = jax.random.randint(key_split, (GROUPS,), lowest, highest + 1).astype(jnp.int32)
    return jnp.stack([first_image, totals - first_image], axis=1).astype(jnp.int32)


def draw_query_key_value_weight(key, part):
    key = jax.random.fold_in(key, 5)
    key_base = jax.random.fold_in(key, 0)
    att_width = LOCAL_HEADS * HEAD_SIZE
    base_draw = jax.random.normal(key_base, (MODEL_WIDTH, 3 * att_width), jnp.float32) * MODEL_WIDTH ** (-0.5)
    return base_draw.astype(jnp.bfloat16)


def block_scale(stream_key, extent, shards, least, high):
    loudness, own = 1.0, jax.random.fold_in(stream_key, 6)
    for axis_at, parts in shards:
        draws = jnp.exp(jax.random.uniform(jax.random.fold_in(own, axis_at), (parts,), jnp.float32, least / len(shards), high / len(shards)))
        loudness = loudness * jnp.repeat(draws, extent[axis_at] // parts).reshape([-1 if axis == axis_at else 1 for axis in range(len(extent))])
    return loudness


def normal_values(rng, shape, width, bound, cuts=(), held_as=jnp.bfloat16):
    values = width * jax.random.normal(rng, shape, jnp.float32)
    if cuts:
        values = values * block_scale(rng, shape, cuts, -0.22, 0.18)
    return jnp.clip(values, -bound, bound).astype(held_as)


def setup_inputs(seed: int = 0) -> dict:
    splits = jax.random.split(jax.random.key(seed), 9)
    return {
        "tokens": normal_values(splits[0], (GROUPS, SEQ_LEN, MODEL_WIDTH), 1.0, 6.0, ((0, 64), (1, 4))),
        "cotangent": normal_values(splits[1], (GROUPS, SEQ_LEN, LOCAL_HEADS * HEAD_SIZE), 1.0, 6.0, ((0, 64), (1, 4))),
        "condition": normal_values(splits[2], (GROUPS, IMGS, VEC), 1.0, 6.0, ((0, 64),)),
        "per_image_rows": draw_per_image_rows(jax.random.fold_in(splits[8], 71), 0),
        "query_key_value_weight": draw_query_key_value_weight(jax.random.fold_in(splits[8], 71), 0),
        "adapter_down": normal_values(splits[5], (MODEL_WIDTH, ADAPTER_RANK), MODEL_WIDTH ** -0.5, 0.15625),
        "adapter_up": normal_values(splits[6], (ADAPTER_RANK, 3 * LOCAL_HEADS * HEAD_SIZE), ADAPTER_RANK ** -0.5, 0.75),
        "modulation_matrix": normal_values(splits[7], (VEC, 2 * MODEL_WIDTH), VEC ** -0.5, 0.109375, ((0, 64),)),
    }


EPSILON = 1e-06
PRECISE = lax.Precision.HIGHEST
MASKED = -1e+30

def through_bf16(values):
    return lax.optimization_barrier(values.astype(jnp.bfloat16)).astype(jnp.float32)

def image_labels(row_rank, bounds):
    return lax.optimization_barrier(jnp.sum((row_rank[:, None] >= bounds[None, :]).astype(jnp.int32), axis=1)).astype(jnp.int32)

def reference(tokens, cotangent, condition, per_image_rows, query_key_value_weight, adapter_down, adapter_up, modulation_matrix):
    att_width = LOCAL_HEADS * HEAD_SIZE
    score_scale = HEAD_SIZE ** (-0.5)
    activated = jax.nn.silu(condition.astype(jnp.float32)).astype(jnp.bfloat16).reshape(GROUPS * IMGS, VEC)
    modulation = jnp.dot(activated, modulation_matrix, preferred_element_type=jnp.float32).reshape(GROUPS, IMGS, 2 * MODEL_WIDTH)

    def one_group(inputs):
        group_tokens, group_cot, group_counts, group_mod = inputs
        row_rank = (jnp.arange(SEQ_LEN, dtype=jnp.int32) % ROWS_DEV).astype(jnp.int32)
        labels = image_labels(row_rank, jnp.cumsum(group_counts).astype(jnp.int32))
        usable = labels < IMGS
        one_hot = (labels[:, None] == jnp.arange(IMGS, dtype=jnp.int32)[None, :]).astype(jnp.float32)
        shift_rows = jnp.dot(one_hot, group_mod[:, :MODEL_WIDTH], precision=PRECISE)
        scale_rows = jnp.dot(one_hot, group_mod[:, MODEL_WIDTH:], precision=PRECISE)
        inputs_wide = group_tokens.astype(jnp.float32)
        centred = inputs_wide - lax.optimization_barrier(jnp.mean(inputs_wide, axis=1, keepdims=True))
        inverse = lax.rsqrt(lax.optimization_barrier(jnp.mean(centred * centred, axis=1, keepdims=True)) + EPSILON)
        normed = centred * inverse
        modulated_input = jnp.where(usable[:, None], (1.0 + scale_rows) * normed + shift_rows, 0.0).astype(jnp.bfloat16)
        adapter_hidden = jnp.dot(modulated_input, adapter_down, preferred_element_type=jnp.float32).astype(jnp.bfloat16)
        reduced_total = jnp.dot(modulated_input, query_key_value_weight, preferred_element_type=jnp.float32) + jnp.dot(adapter_hidden, adapter_up, preferred_element_type=jnp.float32)
        head_view = through_bf16(reduced_total).reshape(SEQ_LEN, 3, LOCAL_HEADS, HEAD_SIZE)
        queries = head_view[:, 0]
        keys_all = head_view[:, 1]
        values_all = head_view[:, 2]
        allowed = (labels[:, None] == labels[None, :]) & usable[None, :]
        scores = jnp.einsum('qhd,khd->hqk', queries, keys_all) * score_scale
        scores = jnp.where(allowed[None], scores, MASKED)
        largest = lax.optimization_barrier(jnp.max(scores, axis=2, keepdims=True))
        log_total = largest + jnp.log(lax.optimization_barrier(jnp.sum(jnp.exp(scores - largest), axis=2, keepdims=True)))
        attn_probs = jnp.exp(scores - log_total)
        probs_low = through_bf16(attn_probs)
        attended = jnp.einsum('hqk,khd->qhd', probs_low, values_all).reshape(SEQ_LEN, att_width)
        attention_out = jnp.where(usable[:, None], attended, 0.0).astype(jnp.bfloat16)
        out_grad = jnp.where(usable[:, None], group_cot, jnp.zeros_like(group_cot))
        head_grads = out_grad.astype(jnp.float32).reshape(SEQ_LEN, LOCAL_HEADS, HEAD_SIZE)
        attention_wide = lax.optimization_barrier(attention_out).astype(jnp.float32).reshape(SEQ_LEN, LOCAL_HEADS, HEAD_SIZE)
        delta_sum = lax.optimization_barrier(jnp.sum(head_grads * attention_wide, axis=2))
        prob_grads = jnp.einsum('qhd,khd->hqk', head_grads, values_all)
        score_grads = through_bf16(attn_probs * (prob_grads - delta_sum.T[:, :, None]) * score_scale)
        query_grad = jnp.einsum('hqk,khd->qhd', score_grads, keys_all)
        key_grad = jnp.einsum('hqk,qhd->khd', score_grads, queries)
        value_grad = jnp.einsum('hqk,qhd->khd', probs_low, head_grads)
        projection_grad = jnp.stack([query_grad, key_grad, value_grad], axis=1).reshape(SEQ_LEN, 3 * att_width).astype(jnp.bfloat16)
        adapter_hidden_grad = jnp.dot(projection_grad, adapter_up.T, preferred_element_type=jnp.float32).astype(jnp.bfloat16)
        modulated_input_sum = jnp.dot(projection_grad, query_key_value_weight.T, preferred_element_type=jnp.float32) + jnp.dot(adapter_hidden_grad, adapter_down.T, preferred_element_type=jnp.float32)
        modded_grad = through_bf16(modulated_input_sum)
        down_part = jnp.dot(modulated_input.T, adapter_hidden_grad, preferred_element_type=jnp.float32)
        up_part = jnp.dot(adapter_hidden.T, projection_grad, preferred_element_type=jnp.float32)
        normed_grad = (1.0 + scale_rows) * modded_grad
        image_grad = jnp.concatenate([jnp.dot(one_hot.T, modded_grad, precision=PRECISE), jnp.dot(one_hot.T, modded_grad * normed, precision=PRECISE)], axis=1)
        input_grad = inverse * (normed_grad - lax.optimization_barrier(jnp.mean(normed_grad, axis=1, keepdims=True)) - normed * lax.optimization_barrier(jnp.mean(normed_grad * normed, axis=1, keepdims=True)))
        return (attention_out, input_grad.astype(jnp.bfloat16), down_part, up_part, image_grad)
    attention, token_grad, down_parts, up_parts, image_grads = lax.map(one_group, (tokens, cotangent, per_image_rows, modulation))
    down_grad = lax.optimization_barrier(jnp.sum(down_parts, axis=0))
    up_grad = lax.optimization_barrier(jnp.sum(up_parts, axis=0))
    activated_wide = lax.optimization_barrier(activated).astype(jnp.float32)
    modulation_grad = jnp.dot(activated_wide.T, image_grads.reshape(GROUPS * IMGS, 2 * MODEL_WIDTH), precision=PRECISE)
    return (attention, token_grad, down_grad, up_grad, modulation_grad)
```

```python
import jax
import jax.numpy as jnp
from jax import lax
from jax.experimental import pallas as pl
from jax.experimental.pallas import tpu as pltpu
from jax.sharding import PartitionSpec as P

HEAD_SIZE = 128
EPSILON = 1e-06
MASKED = -1e30
MESH = pl.DeviceIdType.MESH
NX, NY, NZ, NC = 4, 4, 8, 2
F32, BF16 = jnp.float32, jnp.bfloat16
ANY = pl.BlockSpec(memory_space=pl.ANY)
VM = pl.BlockSpec(memory_space=pltpu.VMEM)


def remote(src, dst, send_sem, recv_sem, device):
    return pltpu.make_async_remote_copy(
        src_ref=src,
        dst_ref=dst,
        send_sem=send_sem,
        recv_sem=recv_sem,
        device_id=device,
        device_id_type=MESH,
    )


class Place:
    def __init__(self):
        self.dp = lax.axis_index("dp")
        self.s = lax.axis_index("seq")
        self.y = self.dp // (NZ * NC)
        self.z = (self.dp // NC) % NZ
        self.c = self.dp % NC

    def at(self, dx=0, dy=0, dz=0, flip=False):
        s = (self.s + dx) % NX if dx else self.s
        y = (self.y + dy) % NY if dy else self.y
        z = (self.z + dz) % NZ if dz else self.z
        c = 1 - self.c if flip else self.c
        return (y * (NZ * NC) + z * NC + c, s)


def enter(me):
    barrier = pltpu.get_barrier_semaphore()
    peers = [me.at(dx=i) for i in range(1, NX)]
    peers += [me.at(dy=i) for i in range(1, NY)]
    peers += [me.at(dz=i) for i in range(1, NZ)]
    peers += [me.at(flip=True)]
    for peer in peers:
        pl.semaphore_signal(barrier, inc=1, device_id=peer, device_id_type=MESH)
    pl.semaphore_wait(barrier, len(peers))


class PlaneGather:
    def __init__(self, me, buf, ysend, yrecv, zsend, zrecv, csend, crecv):
        self.me, self.buf = me, buf
        self.ysend, self.yrecv = ysend, yrecv
        self.zsend, self.zrecv = zsend, zrecv
        self.csend, self.crecv = csend, crecv
        self.sent = []

    def start_y(self, own):
        me = self.me
        for i in range(1, NY):
            copy = remote(
                own, self.buf.at[me.c, me.z, me.y], self.ysend.at[i - 1], self.yrecv.at[i - 1], me.at(dy=i)
            )
            copy.start()
            self.sent.append(copy)

    def wait_y(self):
        me = self.me
        for i in range(1, NY):
            place = self.buf.at[me.c, me.z, (me.y + NY - i) % NY]
            remote(place, place, self.ysend.at[i - 1], self.yrecv.at[i - 1], me.at(dy=i)).wait_recv()

    def ring(self, way, step, part):
        me = self.me
        if way == 0:
            source, there = (me.z + NZ - step + 1) % NZ, me.at(dz=1)
        else:
            source, there = (me.z + step - 1) % NZ, me.at(dz=NZ - 1)
        block = self.buf.at[me.c, source, part]
        at = (way * 4 + step - 1) * NY + part
        return remote(block, block, self.zsend.at[at], self.zrecv.at[at], there)

    def arrive(self, way, step, part):
        me = self.me
        source = (me.z + NZ - step) % NZ if way == 0 else (me.z + step) % NZ
        block = self.buf.at[me.c, source, part]
        at = (way * 4 + step - 1) * NY + part
        there = me.at(dz=1) if way == 0 else me.at(dz=NZ - 1)
        remote(block, block, self.zsend.at[at], self.zrecv.at[at], there).wait_recv()

    def carried(self, way, step, part):
        return step < 4 or (part // 2) == way

    def step(self, step):
        for turn in range(NY):
            for way in (0, 1):
                part = turn if way == 0 else NY - 1 - turn
                if step > 1 and self.carried(way, step - 1, part):
                    self.arrive(way, step - 1, part)
                if step <= 4 and self.carried(way, step, part):
                    copy = self.ring(way, step, part)
                    copy.start()
                    self.sent.append(copy)
        if step == 1:
            self.cross(0)
        elif step == 5:
            self.cross(4)
        else:
            self.cross(step - 1)
            self.cross(NZ - step + 1)

    def cross(self, shift):
        me = self.me
        block = self.buf.at[me.c, (me.z + shift) % NZ]
        copy = remote(block, block, self.csend.at[shift], self.crecv.at[shift], me.at(flip=True))
        copy.start()
        self.sent.append(copy)

    def wait_cross(self):
        me = self.me
        for shift in range(NZ):
            block = self.buf.at[1 - me.c, (me.z + shift) % NZ]
            remote(block, block, self.csend.at[shift], self.crecv.at[shift], me.at(flip=True)).wait_recv()

    def drain(self):
        for copy in self.sent:
            copy.wait_send()


def plane_sems():
    return [
        pltpu.SemaphoreType.DMA((NY - 1,)),
        pltpu.SemaphoreType.DMA((NY - 1,)),
        pltpu.SemaphoreType.DMA((8 * NY,)),
        pltpu.SemaphoreType.DMA((8 * NY,)),
        pltpu.SemaphoreType.DMA((NZ,)),
        pltpu.SemaphoreType.DMA((NZ,)),
    ]


def exchange(me, axis, count, source, slots, send, recv):
    copies = []
    for i in range(1, count):
        copy = remote(source(i), slots.at[i - 1], send.at[i - 1], recv.at[i - 1], me.at(**{axis: i}))
        copy.start()
        copies.append(copy)
    return copies


def finish(copies):
    for copy in copies:
        copy.wait()


def gather_kernel(
    tok, cot, wsh, act, mm,
    tok_all, cot_all, w_all, mod_all, act_own,
    act_all, act_wide, part_wide, part_low, core_in, sum_core, z_in, sum_z, y_in, own_mod,
    tsend, trecv, ksend, krecv, lsem,
    wys, wyr, wzs, wzr, wcs, wcr,
    ays, ayr, azs, azr, acs, acr,
    mcs, mcr, mzs, mzr, mys, myr, mxs, mxr,
):
    me = Place()
    s = me.s
    chunk = tok.shape[0] // 4
    head_cols = cot_all.shape[2]
    act_all[me.c, me.z, me.y] = act[...]
    enter(me)
    right, left = me.at(dx=1), me.at(dx=NX - 1)
    sl, sr = (s + NX - 1) % NX, (s + 1) % NX

    acts = PlaneGather(me, act_all, ays, ayr, azs, azr, acs, acr)
    acts.start_y(act)
    weights = PlaneGather(me, w_all, wys, wyr, wzs, wzr, wcs, wcr)
    weights.start_y(wsh)

    sent = []

    def rows(i):
        return pl.ds(i * chunk, chunk)

    def token_copy(source, owner, i, slot, there):
        return remote(source, tok_all.at[owner, rows(i)], tsend.at[slot], trecv.at[slot], there)

    for i in range(4):
        j = 3 - i
        for copy in (
            token_copy(tok.at[rows(i)], s, i, i, right),
            token_copy(tok.at[rows(j)], s, j, 4 + j, left),
        ):
            copy.start()
            sent.append(copy)
    locals_ = [
        pltpu.make_async_copy(tok, tok_all.at[s], lsem.at[0]),
        pltpu.make_async_copy(
            cot.at[:, pl.ds(pl.multiple_of(s * head_cols, 128), head_cols)], cot_all.at[s], lsem.at[1]
        ),
        pltpu.make_async_copy(wsh, w_all.at[me.c, me.z, me.y], lsem.at[2]),
    ]
    for copy in locals_:
        copy.start()

    acts.wait_y()
    acts.step(1)
    weights.wait_y()
    locals_[2].wait()
    weights.step(1)
    acts.step(2)

    for i in (0, 1):
        token_copy(tok.at[rows(i)], sl, i, i, right).wait_recv()
        copy = token_copy(tok_all.at[sl, rows(i)], sl, i, 8 + i, right)
        copy.start()
        sent.append(copy)
        j = 3 - i
        token_copy(tok.at[rows(j)], sr, j, 4 + j, left).wait_recv()
        copy = token_copy(tok_all.at[sr, rows(j)], sr, j, 8 + j, left)
        copy.start()
        sent.append(copy)

    acts.step(3)
    weights.step(2)
    acts.step(4)

    cot_sent = []
    for i in range(1, NX):
        there = me.at(dx=i)
        copy = remote(
            cot.at[:, pl.ds(pl.multiple_of(there[1] * head_cols, 128), head_cols)],
            cot_all.at[s], ksend.at[i - 1], krecv.at[i - 1], there,
        )
        copy.start()
        cot_sent.append(copy)

    acts.step(5)
    acts.wait_cross()

    act_wide[...] = act_all[...].reshape(act_wide.shape).astype(F32)
    first = 48 * me.dp
    j0 = first // 128
    j1 = (j0 + 1) % 24
    offset = first - 128 * j0
    row = lax.broadcasted_iota(jnp.int32, (128, 128), 0)
    col = lax.broadcasted_iota(jnp.int32, (128, 128), 1)
    inside = col < 48
    pick0 = jnp.where((row == col + offset) & inside, 1.0, 0.0).astype(BF16)
    pick1 = jnp.where((row + 128 == col + offset) & inside, 1.0, 0.0).astype(BF16)
    for img in range(2):
        low = act_wide[pl.ds(img * 24 + j0, 64, stride=48), :].astype(BF16)
        high = act_wide[pl.ds(img * 24 + j1, 64, stride=48), :].astype(BF16)
        act_own[img * 64 : (img + 1) * 64, :] = (
            jnp.dot(low, pick0, preferred_element_type=F32)
            + jnp.dot(high, pick1, preferred_element_type=F32)
        ).astype(BF16)
    part_wide[...] = jnp.zeros_like(part_wide)
    for j in range(6):
        columns = jnp.dot(act_own[...], mm[:, j * 128 : (j + 1) * 128], preferred_element_type=F32)
        for img in range(2):
            part_wide[pl.ds(img * 6 + j, 64, stride=16), :] = columns[img * 64 : (img + 1) * 64]
    part_low[0] = part_wide[0:512].astype(BF16)
    part_low[1] = part_wide[512:1024].astype(BF16)
    crossing = remote(part_low.at[1 - me.c], core_in, mcs, mcr, me.at(flip=True))
    crossing.start()
    weights.step(3)
    crossing.wait()
    sum_core[...] = (
        (part_low[me.c].astype(F32) + core_in[...].astype(F32)).astype(BF16).reshape(sum_core.shape)
    )
    copies = exchange(me, "dz", NZ, lambda i: sum_core.at[(me.z + i) % NZ], z_in, mzs, mzr)
    finish(copies)
    total = sum_core[me.z].astype(F32)
    for i in range(NZ - 1):
        total += z_in[i].astype(F32)
    sum_z[...] = total.reshape(sum_z.shape)
    copies = exchange(me, "dy", NY, lambda i: sum_z.at[(me.y + i) % NY], y_in, mys, myr)
    finish(copies)
    own_mod[...] = sum_z[me.y] + y_in[0] + y_in[1] + y_in[2]
    mod_all[s] = own_mod[...]
    mod_sent = []
    for i in range(1, NX):
        copy = remote(own_mod, mod_all.at[s], mxs.at[i - 1], mxr.at[i - 1], me.at(dx=i))
        copy.start()
        mod_sent.append(copy)

    weights.step(4)
    weights.step(5)

    for i in (0, 1):
        opposite = (s + 2) % NX
        token_copy(tok.at[rows(i)], opposite, i, 8 + i, right).wait_recv()
        token_copy(tok.at[rows(3 - i)], opposite, 3 - i, 8 + 3 - i, left).wait_recv()
    for i in (2, 3):
        token_copy(tok.at[rows(i)], sl, i, i, right).wait_recv()
        token_copy(tok.at[rows(3 - i)], sr, 3 - i, 4 + 3 - i, left).wait_recv()
    for copy in sent:
        copy.wait_send()
    finish(cot_sent)
    finish(mod_sent)
    weights.wait_cross()
    acts.drain()
    weights.drain()
    locals_[0].wait()
    locals_[1].wait()


def gather_all(tok, cot, wsh, act, mm):
    rows, width = tok.shape
    dma = pltpu.SemaphoreType.DMA
    return pl.pallas_call(
        gather_kernel,
        out_shape=(
            jax.ShapeDtypeStruct((NX, rows, width), BF16),
            jax.ShapeDtypeStruct((NX, rows, width // NX), BF16),
            jax.ShapeDtypeStruct((NC, NZ, NY) + wsh.shape, BF16),
            jax.ShapeDtypeStruct((NX, 16, 128), F32),
            jax.ShapeDtypeStruct((128, 128), BF16),
        ),
        in_specs=[ANY, ANY, ANY, VM, VM],
        out_specs=(ANY, ANY, ANY, VM, VM),
        scratch_shapes=[
            pltpu.VMEM((NC, NZ, NY, 48, 128), BF16),
            pltpu.VMEM((3072, 128), F32),
            pltpu.VMEM((1024, 128), F32),
            pltpu.VMEM((NC, 512, 128), BF16),
            pltpu.VMEM((512, 128), BF16),
            pltpu.VMEM((NZ, 64, 128), BF16),
            pltpu.VMEM((NZ - 1, 64, 128), BF16),
            pltpu.VMEM((NY, 16, 128), F32),
            pltpu.VMEM((NY - 1, 16, 128), F32),
            pltpu.VMEM((16, 128), F32),
            dma((12,)), dma((12,)), dma((3,)), dma((3,)), dma((3,)),
            *plane_sems(),
            *plane_sems(),
            dma, dma, dma((NZ - 1,)), dma((NZ - 1,)), dma((NY - 1,)), dma((NY - 1,)), dma((3,)), dma((3,)),
        ],
        compiler_params=pltpu.CompilerParams(
            collective_id=1, has_side_effects=True, vmem_limit_bytes=24 * 1024 * 1024
        ),
        name="gather_all",
    )(tok, cot, wsh, act, mm)


def nt(a, b):
    return lax.dot_general(a, b, (((1,), (1,)), ((), ())), preferred_element_type=F32)


def tn(a, b):
    return lax.dot_general(a, b, (((0,), (0,)), ((), ())), preferred_element_type=F32)


def labels_of(rank, c0, c1):
    return (rank >= c0).astype(jnp.int32) + (rank >= c0 + c1).astype(jnp.int32)


def local_kernel(
    counts, tok, mod, cot, w, down, up,
    attn, pg, ip, up_part, down_part,
    modded, stats, low, proj, proj_grad, kv_grad, low_grad,
):
    c0, c1 = counts[0], counts[1]
    rows, width = tok.shape[1], tok.shape[2]
    heads = cot.shape[2] // HEAD_SIZE
    att = heads * HEAD_SIZE
    scale = HEAD_SIZE ** (-0.5)
    label = labels_of(lax.broadcasted_iota(jnp.int32, (rows, 1), 0), c0, c1)
    usable = label < 2
    is0 = label == 0
    lane = lax.broadcasted_iota(jnp.int32, (8, NX * rows), 1)
    for _ in range(NX - 1):
        lane = jnp.where(lane >= rows, lane - rows, lane)
    key_label = labels_of(lane, c0, c1)

    @pl.loop(0, NX)
    def _(block):
        x = tok[block].astype(F32)
        mean = jnp.mean(x, axis=1, keepdims=True)
        centred = x - mean
        inverse = lax.rsqrt(jnp.mean(centred * centred, axis=1, keepdims=True) + EPSILON)
        normed = centred * inverse
        shift = jnp.where(is0, mod[0:1, :width], mod[1:2, :width])
        gain = 1.0 + jnp.where(is0, mod[0:1, width:], mod[1:2, width:])
        value = jnp.where(usable, gain * normed + shift, 0.0).astype(BF16)
        at = pl.ds(pl.multiple_of(block * rows, rows), rows)
        modded[at, :] = value
        stats[at, 0:1] = mean
        stats[at, 1:2] = inverse

    low[...] = jnp.dot(modded[...], down[...], preferred_element_type=F32).astype(BF16)

    @pl.loop(0, 3)
    def _(n):
        at = pl.ds(pl.multiple_of(n * att, 128), att)
        proj[:, at] = (
            jnp.dot(modded[...], w[:, at], preferred_element_type=F32)
            + jnp.dot(low[...], up[:, at], preferred_element_type=F32)
        ).astype(BF16)

    kv_grad[...] = jnp.zeros_like(kv_grad)

    @pl.loop(0, NX)
    def _(block):
        at = pl.ds(pl.multiple_of(block * rows, rows), rows)
        allowed = (label == key_label[0:1]) & (key_label[0:1] < 2)
        for h in range(heads):
            c = slice(h * 128, (h + 1) * 128)
            q = proj[at, c]
            k = proj[:, att + h * 128 : att + (h + 1) * 128]
            v = proj[:, 2 * att + h * 128 : 2 * att + (h + 1) * 128]
            scores = jnp.where(allowed, nt(q, k) * scale, MASKED)
            largest = jnp.max(scores, axis=1, keepdims=True)
            raw = jnp.exp(scores - largest)
            probs = raw * (1.0 / jnp.sum(raw, axis=1, keepdims=True))
            probs_low = probs.astype(BF16)
            out = jnp.where(usable, jnp.dot(probs_low, v, preferred_element_type=F32), 0.0).astype(BF16)
            attn[block, :, c] = out
            out_grad = jnp.where(usable, cot[block, :, c].astype(F32), 0.0)
            delta = jnp.sum(out_grad * out.astype(F32), axis=1, keepdims=True)
            out_grad = out_grad.astype(BF16)
            score_grads = (probs * (nt(out_grad, v) - delta) * scale).astype(BF16)
            proj_grad[at, c] = jnp.dot(score_grads, k, preferred_element_type=F32).astype(BF16)
            kv_grad[:, h * 128 : (h + 1) * 128] += tn(score_grads, q)
            kv_grad[:, att + h * 128 : att + (h + 1) * 128] += tn(probs_low, out_grad)

    proj_grad[:, att:] = kv_grad[...].astype(BF16)
    low_grad[...] = nt(proj_grad[...], up[...]).astype(BF16)

    one_hot = jnp.where(
        key_label == lax.broadcasted_iota(jnp.int32, key_label.shape, 0), 1.0, 0.0
    )
    one_hot = jnp.where(key_label < 2, one_hot, 0.0).astype(BF16)

    for n in range(width // att):
        f = slice(n * att, (n + 1) * att)
        grad = nt(proj_grad[...], w[f, :]) + nt(low_grad[...], down[f, :])
        grad_low = grad.astype(BF16)
        for block in range(NX):
            pg[block, :, f] = grad_low[block * rows : (block + 1) * rows]
        x = tok[:, :, f].reshape(NX * rows, att).astype(F32)
        normed = (x - stats[:, 0:1]) * stats[:, 1:2]
        ip[:, f] = jnp.dot(one_hot, grad_low, preferred_element_type=F32)
        ip[:, width + n * att : width + (n + 1) * att] = jnp.dot(
            one_hot, (grad * normed).astype(BF16), preferred_element_type=F32
        )

    up_total = tn(low[...], proj_grad[...])
    for t in range(3 * heads):
        up_part[t * 64 : (t + 1) * 64, :] = up_total[:, t * 128 : (t + 1) * 128]
    down_total = tn(low_grad[...], modded[...])
    for t in range(width // 128):
        down_part[t * 64 : (t + 1) * 64, :] = down_total[:, t * 128 : (t + 1) * 128]


def local_all(counts, tok, mod, cot, w, down, up):
    _, rows, width = tok.shape
    att = cot.shape[2]
    all_rows = NX * rows
    return pl.pallas_call(
        local_kernel,
        out_shape=(
            jax.ShapeDtypeStruct((NX, rows, att), BF16),
            jax.ShapeDtypeStruct((NX, rows, width), BF16),
            jax.ShapeDtypeStruct((8, 2 * width), F32),
            jax.ShapeDtypeStruct((3 * att // 2, 128), F32),
            jax.ShapeDtypeStruct((width // 2, 128), F32),
        ),
        in_specs=[pl.BlockSpec(memory_space=pltpu.SMEM)] + [VM] * 6,
        out_specs=(VM,) * 5,
        scratch_shapes=[
            pltpu.VMEM((all_rows, width), BF16),
            pltpu.VMEM((all_rows, 128), F32),
            pltpu.VMEM((all_rows, 64), BF16),
            pltpu.VMEM((all_rows, 3 * att), BF16),
            pltpu.VMEM((all_rows, 3 * att), BF16),
            pltpu.VMEM((all_rows, 2 * att), F32),
            pltpu.VMEM((all_rows, 64), BF16),
        ],
        compiler_params=pltpu.CompilerParams(vmem_limit_bytes=56 * 1024 * 1024),
        name="local_all",
    )(counts, tok, mod, cot, w, down, up)


def scatter_kernel(
    pg, attn, ip, up_part, down_part,
    grad, attn_out, ig_all, trip,
    half_l, half_r, comb_l, comb_r, from_l, from_r,
    ip_in, own_ig, lora, down_in, y_in, plane, z_in, own_piece, core_in,
    gsend, grecv, osend, orecv, lsem,
    ips, ipr, gys, gyr, gzs, gzr, gcs, gcr,
    dxs, dxr, lys, lyr, lzs, lzr, lcs, lcr, lgs, lgr, lxs, lxr,
):
    me = Place()
    s, y, z = me.s, me.y, me.z
    rows = pg.shape[1]
    half = rows // 2
    head_cols = attn.shape[2]
    first, second = pl.ds(0, half), pl.ds(half, half)
    sl, sr, so = (s + NX - 1) % NX, (s + 1) % NX, (s + 2) % NX
    right, left = me.at(dx=1), me.at(dx=NX - 1)
    enter(me)

    ip_sent = exchange(me, "dx", NX, lambda i: ip, ip_in, ips, ipr)
    down_sent = exchange(me, "dx", NX, lambda i: down_part.at[(NX - 1) - (s + i) % NX], down_in, dxs, dxr)

    def grad_copy(src, dst, slot, there):
        copy = remote(src, dst, gsend.at[slot], grecv.at[slot], there)
        copy.start()
        return copy

    step1_r = grad_copy(pg.at[so, first], half_l, 0, right)
    step1_l = grad_copy(pg.at[so, second], half_r, 1, left)
    plain_r = grad_copy(pg.at[sr, second], from_l.at[second], 2, right)
    plain_l = grad_copy(pg.at[sl, first], from_r.at[first], 3, left)

    out_sent = []
    columns = pl.ds(pl.multiple_of(s * head_cols, 128), head_cols)
    for i in range(1, NX):
        there = me.at(dx=i)
        copy = remote(attn.at[there[1]], attn_out.at[:, columns], osend.at[i - 1], orecv.at[i - 1], there)
        copy.start()
        out_sent.append(copy)
    own_out = pltpu.make_async_copy(attn.at[s], attn_out.at[:, columns], lsem)
    own_out.start()

    finish(ip_sent)
    own_ig[...] = (ip[...] + ip_in[0] + ip_in[1] + ip_in[2]).astype(BF16)
    ig_all[me.c, z, y] = own_ig[...]
    images = PlaneGather(me, ig_all, gys, gyr, gzs, gzr, gcs, gcr)
    images.start_y(own_ig)

    finish(down_sent)
    lora[0:3] = up_part[...]
    lora[3] = down_part[(NX - 1) - s] + down_in[0] + down_in[1] + down_in[2]

    def triple(there):
        step = (s + there) % 4
        down = step // 3
        return ((3 * there + step) // 4) * (1 - down) + 3 * down

    y_sent = exchange(me, "dy", NY, lambda i: lora.at[triple((y + i) % NY)], y_in, lys, lyr)
    images.wait_y()
    images.step(1)
    finish(y_sent)
    plane[...] = (lora[triple(y)] + y_in[0] + y_in[1] + y_in[2]).reshape(plane.shape)
    z_sent = exchange(me, "dz", NZ, lambda i: plane.at[(z + i) % NZ], z_in, lzs, lzr)
    images.step(2)

    step1_r.wait_recv()
    comb_r[...] = (pg[sr, 0:half].astype(F32) + half_l[...].astype(F32)).astype(BF16)
    comb_copy_r = grad_copy(comb_r, from_l.at[first], 4, right)
    step1_l.wait_recv()
    comb_l[...] = (pg[sl, half:rows].astype(F32) + half_r[...].astype(F32)).astype(BF16)
    comb_copy_l = grad_copy(comb_l, from_r.at[second], 5, left)

    images.step(3)
    finish(z_sent)
    total = plane[z]
    for i in range(NZ - 1):
        total += z_in[i]
    own_piece[0] = total
    core_copy = remote(own_piece.at[0], core_in, lcs, lcr, me.at(flip=True))
    core_copy.start()
    images.step(4)
    core_copy.wait()
    own_piece[1] = own_piece[0] + core_in[...]
    trip[s, z] = own_piece[1]
    piece_sent = []
    for i in range(1, NZ):
        copy = remote(own_piece.at[1], trip.at[s, z], lgs.at[i - 1], lgr.at[i - 1], me.at(dz=i))
        copy.start()
        piece_sent.append(copy)
    images.step(5)
    finish(piece_sent)
    trip_sent = []
    for i in range(1, NX):
        copy = remote(trip.at[s], trip.at[s], lxs.at[i - 1], lxr.at[i - 1], me.at(dx=i))
        copy.start()
        trip_sent.append(copy)
    images.wait_cross()

    plain_r.wait_recv()
    plain_l.wait_recv()
    comb_copy_r.wait_recv()
    comb_copy_l.wait_recv()
    grad[...] = pg[s].astype(F32) + from_l[...].astype(F32) + from_r[...].astype(F32)

    for copy in (step1_r, step1_l, plain_r, plain_l, comb_copy_r, comb_copy_l):
        copy.wait_send()
    finish(out_sent)
    own_out.wait()
    finish(trip_sent)
    images.drain()


def scatter_all(pg, attn, ip, up_part, down_part):
    _, rows, width = pg.shape
    dma = pltpu.SemaphoreType.DMA
    half = rows // 2
    return pl.pallas_call(
        scatter_kernel,
        out_shape=(
            jax.ShapeDtypeStruct((rows, width), F32),
            jax.ShapeDtypeStruct((rows, width), BF16),
            jax.ShapeDtypeStruct((NC, NZ, NY, 48, 128), BF16),
            jax.ShapeDtypeStruct((NX, NZ, 24, 128), F32),
        ),
        in_specs=[VM, VM, VM, VM, VM],
        out_specs=(VM, ANY, VM, VM),
        scratch_shapes=[
            pltpu.VMEM((half, width), BF16),
            pltpu.VMEM((half, width), BF16),
            pltpu.VMEM((half, width), BF16),
            pltpu.VMEM((half, width), BF16),
            pltpu.VMEM((rows, width), BF16),
            pltpu.VMEM((rows, width), BF16),
            pltpu.VMEM((3, 48, 128), F32),
            pltpu.VMEM((48, 128), BF16),
            pltpu.VMEM((4, 192, 128), F32),
            pltpu.VMEM((3, 192, 128), F32),
            pltpu.VMEM((3, 192, 128), F32),
            pltpu.VMEM((NZ, 24, 128), F32),
            pltpu.VMEM((NZ - 1, 24, 128), F32),
            pltpu.VMEM((2, 24, 128), F32),
            pltpu.VMEM((24, 128), F32),
            dma((6,)), dma((6,)), dma((3,)), dma((3,)), dma,
            dma((3,)), dma((3,)),
            *plane_sems(),
            dma((3,)), dma((3,)), dma((3,)), dma((3,)), dma((7,)), dma((7,)),
            dma, dma, dma((7,)), dma((7,)), dma((3,)), dma((3,)),
        ],
        compiler_params=pltpu.CompilerParams(
            collective_id=2, has_side_effects=True, vmem_limit_bytes=32 * 1024 * 1024
        ),
        name="scatter_all",
    )(pg, attn, ip, up_part, down_part)


def tail_kernel(counts, grad, tok, mod, act, ig, token_grad, mod_grad, wide):
    rows, width = tok.shape
    c0, c1 = counts[0], counts[1]
    label = labels_of(lax.broadcasted_iota(jnp.int32, (rows, 1), 0), c0, c1)
    x = tok[...].astype(F32)
    centred = x - jnp.mean(x, axis=1, keepdims=True)
    inverse = lax.rsqrt(jnp.mean(centred * centred, axis=1, keepdims=True) + EPSILON)
    normed = centred * inverse
    gain = 1.0 + jnp.where(label == 0, mod[0:1, width:], mod[1:2, width:])
    g = jnp.where(label < 2, gain * grad[...], 0.0)
    token_grad[...] = (
        inverse
        * (
            g
            - jnp.mean(g, axis=1, keepdims=True)
            - normed * jnp.mean(g * normed, axis=1, keepdims=True)
        )
    ).astype(BF16)
    wide[...] = ig[...].astype(F32)
    for j in range(24):
        total = jnp.zeros((128, 128), F32)
        for img in range(2):
            part = wide[pl.ds(img * 24 + j, 64, stride=48), :].astype(BF16)
            total += tn(act[img * 64 : (img + 1) * 64], part)
        mod_grad[:, j * 128 : (j + 1) * 128] = total[0:48]


def tail_all(counts, grad, tok, mod, act, ig):
    rows, width = tok.shape
    return pl.pallas_call(
        tail_kernel,
        out_shape=(
            jax.ShapeDtypeStruct((rows, width), BF16),
            jax.ShapeDtypeStruct((48, 3072), F32),
        ),
        in_specs=[pl.BlockSpec(memory_space=pltpu.SMEM)] + [VM] * 5,
        out_specs=(VM, VM),
        scratch_shapes=[pltpu.VMEM((3072, 128), F32)],
        compiler_params=pltpu.CompilerParams(vmem_limit_bytes=32 * 1024 * 1024),
        name="tail_all",
    )(counts, grad, tok, mod, act, ig)


def body(
    tokens,
    cotangent,
    condition,
    per_image_rows,
    query_key_value_weight,
    adapter_down,
    adapter_up,
    modulation_matrix,
):
    dp = lax.axis_index("dp")
    s = lax.axis_index("seq")
    y, place = dp // (NZ * NC), dp % (NZ * NC)
    tok, cot = tokens[0], cotangent[0]
    width = tok.shape[1]
    att = cot.shape[1] // NX

    def head_columns(matrix):
        shaped = matrix.reshape(matrix.shape[0], 3, NX, att)
        return lax.dynamic_index_in_dim(shaped, s, 2, keepdims=False)

    counts = lax.dynamic_index_in_dim(per_image_rows, dp, 0, keepdims=False)
    act = jax.nn.silu(condition[0].astype(F32)).astype(BF16).reshape(48, 128)
    mm = lax.dynamic_slice_in_dim(modulation_matrix, s * 768, 768, 1)
    mm = jnp.pad(mm, ((0, 128 - mm.shape[0]), (0, 0)))
    shard_rows = query_key_value_weight.shape[0]
    wsh = head_columns(query_key_value_weight).reshape(shard_rows, 9, 128)
    wsh = wsh.transpose(1, 0, 2).reshape(9 * shard_rows, 128)
    wsh = jnp.pad(wsh, ((0, 224 - 9 * shard_rows), (0, 0)))
    up = head_columns(adapter_up).reshape(64, 3 * att)

    tok_all, cot_all, w_all, mod_all, act_own = gather_all(tok, cot, wsh, act, mm)

    w = w_all[:, :, :, : 9 * shard_rows].reshape(NC, NZ, NY, 9, shard_rows, 128)
    w = w.transpose(2, 1, 0, 4, 3, 5).reshape(width, 3 * att)
    mod = mod_all[:, :12].reshape(NX, 2, 768).transpose(1, 0, 2).reshape(2, 2 * width)
    mod = jnp.pad(mod, ((0, 6), (0, 0)))

    attn, pg, ip, up_part, down_part = local_all(counts, tok_all, mod, cot_all, w, adapter_down, up)

    grad, attention, ig_all, trip = scatter_all(
        pg,
        attn,
        ip[:2].reshape(48, 128),
        up_part.reshape(3, 192, 128),
        down_part.reshape(4, 192, 128),
    )
    token_grad, mod_grad = tail_all(counts, grad, tok, mod, act_own, ig_all.reshape(3072, 128))

    trip = trip.reshape(NX, 3, 64, 128)
    order = (3 * y + jnp.arange(3)) % 4
    slab = trip[order].reshape(9, 64, 128).transpose(1, 0, 2).reshape(64, 1152)
    up_grad = lax.dynamic_slice_in_dim(slab, place * 72, 72, 1)
    down = lax.dynamic_index_in_dim(trip, 3 - y, 0, keepdims=False)
    down = down.transpose(1, 0, 2).reshape(64, 384)
    down_grad = lax.dynamic_slice_in_dim(down, place * 24, 24, 1).T
    return attention[None], token_grad[None], down_grad, up_grad, mod_grad


def solution(mesh):
    in_specs = (
        P("dp", "seq", None),
        P("dp", "seq", None),
        P("dp", None, None),
        P(),
        P("dp", None),
        P(),
        P(),
        P("dp", None),
    )
    out_specs = (
        P("dp", "seq", None),
        P("dp", "seq", None),
        P("dp", None),
        P(None, "dp"),
        P("dp", None),
    )
    return jax.shard_map(body, mesh=mesh, in_specs=in_specs, out_specs=out_specs, check_vma=False)
```

```python
import jax
import jax.numpy as jnp
from jax import lax
from jax.experimental import pallas as pl
from jax.experimental.pallas import tpu as pltpu
from jax.sharding import PartitionSpec as P

HEAD_SIZE = 128
EPSILON = 1e-06
MASKED = -1e30
MESH = pl.DeviceIdType.MESH
NX, NY, NZ, NC = 4, 4, 8, 2
F32, BF16 = jnp.float32, jnp.bfloat16
ANY = pl.BlockSpec(memory_space=pl.ANY)
VM = pl.BlockSpec(memory_space=pltpu.VMEM)


def remote(src, dst, send_sem, recv_sem, device):
    return pltpu.make_async_remote_copy(
        src_ref=src,
        dst_ref=dst,
        send_sem=send_sem,
        recv_sem=recv_sem,
        device_id=device,
        device_id_type=MESH,
    )


class Place:
    def __init__(self):
        self.dp = lax.axis_index("dp")
        self.s = lax.axis_index("seq")
        self.y = self.dp // (NZ * NC)
        self.z = (self.dp // NC) % NZ
        self.c = self.dp % NC

    def at(self, dx=0, dy=0, dz=0, flip=False):
        s = (self.s + dx) % NX if dx else self.s
        y = (self.y + dy) % NY if dy else self.y
        z = (self.z + dz) % NZ if dz else self.z
        c = 1 - self.c if flip else self.c
        return (y * (NZ * NC) + z * NC + c, s)


def enter(me):
    barrier = pltpu.get_barrier_semaphore()
    peers = [me.at(dx=i) for i in range(1, NX)]
    peers += [me.at(dy=i) for i in range(1, NY)]
    peers += [me.at(dz=i) for i in range(1, NZ)]
    peers += [me.at(flip=True)]
    for peer in peers:
        pl.semaphore_signal(barrier, inc=1, device_id=peer, device_id_type=MESH)
    pl.semaphore_wait(barrier, len(peers))


class PlaneGather:
    def __init__(self, me, buf, ysend, yrecv, zsend, zrecv, csend, crecv):
        self.me, self.buf = me, buf
        self.ysend, self.yrecv = ysend, yrecv
        self.zsend, self.zrecv = zsend, zrecv
        self.csend, self.crecv = csend, crecv
        self.sent = []

    def start_y(self, own):
        me = self.me
        for i in range(1, NY):
            copy = remote(
                own, self.buf.at[me.c, me.z, me.y], self.ysend.at[i - 1], self.yrecv.at[i - 1], me.at(dy=i)
            )
            copy.start()
            self.sent.append(copy)

    def wait_y(self):
        me = self.me
        for i in range(1, NY):
            place = self.buf.at[me.c, me.z, (me.y + NY - i) % NY]
            remote(place, place, self.ysend.at[i - 1], self.yrecv.at[i - 1], me.at(dy=i)).wait_recv()

    def ring(self, way, step, part):
        me = self.me
        if way == 0:
            source, there = (me.z + NZ - step + 1) % NZ, me.at(dz=1)
        else:
            source, there = (me.z + step - 1) % NZ, me.at(dz=NZ - 1)
        block = self.buf.at[me.c, source, part]
        at = (way * 4 + step - 1) * NY + part
        return remote(block, block, self.zsend.at[at], self.zrecv.at[at], there)

    def arrive(self, way, step, part):
        me = self.me
        source = (me.z + NZ - step) % NZ if way == 0 else (me.z + step) % NZ
        block = self.buf.at[me.c, source, part]
        at = (way * 4 + step - 1) * NY + part
        there = me.at(dz=1) if way == 0 else me.at(dz=NZ - 1)
        remote(block, block, self.zsend.at[at], self.zrecv.at[at], there).wait_recv()

    def carried(self, way, step, part):
        return step < 4 or (part // 2) == way

    def step(self, step):
        for turn in range(NY):
            for way in (0, 1):
                part = turn if way == 0 else NY - 1 - turn
                if step > 1 and self.carried(way, step - 1, part):
                    self.arrive(way, step - 1, part)
                if step <= 4 and self.carried(way, step, part):
                    copy = self.ring(way, step, part)
                    copy.start()
                    self.sent.append(copy)
        if step == 1:
            self.cross(0)
        elif step == 5:
            self.cross(4)
        else:
            self.cross(step - 1)
            self.cross(NZ - step + 1)

    def cross(self, shift):
        me = self.me
        block = self.buf.at[me.c, (me.z + shift) % NZ]
        copy = remote(block, block, self.csend.at[shift], self.crecv.at[shift], me.at(flip=True))
        copy.start()
        self.sent.append(copy)

    def wait_cross(self):
        me = self.me
        for shift in range(NZ):
            block = self.buf.at[1 - me.c, (me.z + shift) % NZ]
            remote(block, block, self.csend.at[shift], self.crecv.at[shift], me.at(flip=True)).wait_recv()

    def drain(self):
        for copy in self.sent:
            copy.wait_send()


def plane_sems():
    return [
        pltpu.SemaphoreType.DMA((NY - 1,)),
        pltpu.SemaphoreType.DMA((NY - 1,)),
        pltpu.SemaphoreType.DMA((8 * NY,)),
        pltpu.SemaphoreType.DMA((8 * NY,)),
        pltpu.SemaphoreType.DMA((NZ,)),
        pltpu.SemaphoreType.DMA((NZ,)),
    ]


def exchange(me, axis, count, source, slots, send, recv):
    copies = []
    for i in range(1, count):
        copy = remote(source(i), slots.at[i - 1], send.at[i - 1], recv.at[i - 1], me.at(**{axis: i}))
        copy.start()
        copies.append(copy)
    return copies


def finish(copies):
    for copy in copies:
        copy.wait()


def exchange_at(me, axis, count, source, target, send, recv):
    copies = []
    for i in range(1, count):
        copy = remote(source(i), target, send.at[i - 1], recv.at[i - 1], me.at(**{axis: i}))
        copy.start()
        copies.append(copy)
    return copies


def nt(a, b):
    return lax.dot_general(a, b, (((1,), (1,)), ((), ())), preferred_element_type=F32)


def tn(a, b):
    return lax.dot_general(a, b, (((0,), (0,)), ((), ())), preferred_element_type=F32)


def nn(a, b):
    return jnp.dot(a, b, preferred_element_type=F32)


def labels_of(rank, c0, c1):
    return (rank >= c0).astype(jnp.int32) + (rank >= c0 + c1).astype(jnp.int32)


def aligned(start, size):
    return pl.ds(pl.multiple_of(start, 128), size)


class Refs:
    pass


SCRATCH = dict(
    tok_all=pltpu.VMEM((NX, 192, 1536), BF16),
    cot_all=pltpu.VMEM((NX, 192, 384), BF16),
    w_all=pltpu.VMEM((NC, NZ, NY, 224, 128), BF16),
    w=pltpu.VMEM((1536, 1152), BF16),
    up=pltpu.VMEM((64, 1152), BF16),
    down=pltpu.VMEM((64, 1536), BF16),
    mm=pltpu.VMEM((128, 768), BF16),
    a_z=pltpu.VMEM((NZ, NY, 8, 128), F32),
    a_y=pltpu.VMEM((NC, NZ, NY, 8, 128), F32),
    a_wide=pltpu.VMEM((512, 128), F32),
    a_own=pltpu.VMEM((128, 128), BF16),
    part_wide=pltpu.VMEM((1024, 128), F32),
    part_low=pltpu.VMEM((NC, NZ, NY, 16, 128), BF16),
    m_core=pltpu.VMEM((NZ, NY, 16, 128), BF16),
    m_sum=pltpu.VMEM((NZ, NY, 16, 128), BF16),
    m_y=pltpu.VMEM((NY - 1, NZ, 16, 128), BF16),
    m_plane=pltpu.VMEM((NZ, 16, 128), F32),
    m_z=pltpu.VMEM((NZ - 1, 16, 128), F32),
    m_own=pltpu.VMEM((16, 128), F32),
    m_all=pltpu.VMEM((NX, 16, 128), F32),
    mod=pltpu.VMEM((8, 3072), F32),
    modded=pltpu.VMEM((768, 1536), BF16),
    stats=pltpu.VMEM((768, 128), F32),
    low=pltpu.VMEM((768, 64), BF16),
    proj=pltpu.VMEM((768, 1152), BF16),
    proj_grad=pltpu.VMEM((768, 1152), BF16),
    kv_grad=pltpu.VMEM((768, 768), F32),
    low_grad=pltpu.VMEM((768, 64), BF16),
    attn=pltpu.VMEM((NX, 192, 384), BF16),
    pg=pltpu.VMEM((NX, 192, 1536), BF16),
    ip=pltpu.VMEM((8, 3072), F32),
    half_l=pltpu.VMEM((96, 1536), BF16),
    half_r=pltpu.VMEM((96, 1536), BF16),
    comb_l=pltpu.VMEM((96, 1536), BF16),
    comb_r=pltpu.VMEM((96, 1536), BF16),
    from_l=pltpu.VMEM((192, 1536), BF16),
    from_r=pltpu.VMEM((192, 1536), BF16),
    ip_own=pltpu.VMEM((48, 128), F32),
    ip_in=pltpu.VMEM((3, 48, 128), F32),
    ig_all=pltpu.VMEM((NC, NZ, NY, 48, 128), BF16),
    ig_wide=pltpu.VMEM((3072, 128), F32),
    lora=pltpu.VMEM((4, 192, 128), F32),
    down_part=pltpu.VMEM((4, 192, 128), F32),
    down_in=pltpu.VMEM((3, 192, 128), F32),
    l_y=pltpu.VMEM((3, 192, 128), F32),
    l_plane=pltpu.VMEM((NZ, 24, 128), F32),
    l_z=pltpu.VMEM((NZ - 1, 24, 128), F32),
    l_own=pltpu.VMEM((2, 24, 128), F32),
    l_core=pltpu.VMEM((24, 128), F32),
    trip=pltpu.VMEM((NX, NZ, 24, 128), F32),
)
PAIRS = dict(tk=12, ck=3, az=7, ay=3, ac=1, mc=1, my=3, mz=7, mx=3, gr=6, ot=3, ip=3, dx=3, ly=3, lz=7, lc=1, lg=7, lx=3)
PLANES = dict(wp=1, gp=1)
LOCAL = 8


def scratch_list():
    dma = pltpu.SemaphoreType.DMA
    out = list(SCRATCH.values())
    for count in PAIRS.values():
        out += [dma((count,)), dma((count,))]
    for _ in PLANES:
        out += plane_sems()
    return out + [dma((LOCAL,))]


def named(refs):
    r = Refs()
    refs = list(refs)
    for name in SCRATCH:
        setattr(r, name, refs.pop(0))
    for name in PAIRS:
        setattr(r, name + "_s", refs.pop(0))
        setattr(r, name + "_r", refs.pop(0))
    for name in PLANES:
        setattr(r, name, [refs.pop(0) for _ in range(6)])
    r.local = refs.pop(0)
    return r


def whole_kernel(
    rows_ref, tok, cot, act, wq, up_in, down_in, mm_in,
    attn_out, token_grad, down_out, up_out, mod_grad,
    *refs,
):
    r = named(refs)
    me = Place()
    s, y, z, c = me.s, me.y, me.z, me.c
    rows, width, att, heads = 192, 1536, 384, 3
    chunk = rows // 4
    scale = HEAD_SIZE ** (-0.5)
    right, left = me.at(dx=1), me.at(dx=NX - 1)
    sl, sr, so = (s + NX - 1) % NX, (s + 1) % NX, (s + 2) % NX
    c0, c1 = rows_ref[me.dp, 0], rows_ref[me.dp, 1]

    r.mm[...] = jnp.zeros_like(r.mm)
    locals_ = [
        pltpu.make_async_copy(tok, r.tok_all.at[s], r.local.at[0]),
        pltpu.make_async_copy(cot.at[:, aligned(s * att, att)], r.cot_all.at[s], r.local.at[1]),
        pltpu.make_async_copy(
            mm_in.at[:, aligned(s * 768, 768)], r.mm.at[pl.ds(pl.multiple_of(48 * c, 16), 48)], r.local.at[2]
        ),
        pltpu.make_async_copy(down_in, r.down, r.local.at[3]),
    ]
    for b in range(3):
        locals_.append(
            pltpu.make_async_copy(
                up_in.at[:, aligned(b * width + s * att, att)], r.up.at[:, b * att : (b + 1) * att], r.local.at[4 + b]
            )
        )
    for copy in locals_:
        copy.start()
    pieces = []
    for b in range(3):
        block = wq[:, aligned(b * width + s * att, att)].astype(F32)
        pieces += [block[:, i * 128 : (i + 1) * 128] for i in range(3)]
    pieces.append(jnp.zeros((8, 128), F32))
    r.w_all[c, z, y] = jnp.concatenate(pieces, axis=0).astype(BF16)
    r.a_z[z] = act[z]

    enter(me)

    az = exchange_at(me, "dz", NZ, lambda i: act.at[(z + i) % NZ], r.a_z.at[z], r.az_s, r.az_r)
    weights = PlaneGather(me, r.w_all, *r.wp)
    weights.start_y(r.w_all.at[c, z, y])

    def row_chunk(i):
        return pl.ds(i * chunk, chunk)

    def token_copy(source, owner, i, slot, there):
        return remote(source, r.tok_all.at[owner, row_chunk(i)], r.tk_s.at[slot], r.tk_r.at[slot], there)

    sent = []

    def launch(copy):
        copy.start()
        sent.append(copy)

    for i in range(4):
        launch(token_copy(tok.at[row_chunk(i)], s, i, i, right))
        launch(token_copy(tok.at[row_chunk(3 - i)], s, 3 - i, 4 + 3 - i, left))

    def forward(i):
        token_copy(tok.at[row_chunk(i)], sl, i, i, right).wait_recv()
        launch(token_copy(r.tok_all.at[sl, row_chunk(i)], sl, i, 8 + i, right))
        j = 3 - i
        token_copy(tok.at[row_chunk(j)], sr, j, 4 + j, left).wait_recv()
        launch(token_copy(r.tok_all.at[sr, row_chunk(j)], sr, j, 8 + j, left))

    finish(az)
    ay = exchange_at(
        me, "dy", NY, lambda i: r.a_z.at[:, (y + i) % NY], r.a_y.at[c, :, y], r.ay_s, r.ay_r
    )
    r.a_y[c, :, y] = r.a_z[:, y]
    weights.wait_y()
    weights.step(1)
    finish(ay)
    ac = remote(r.a_y.at[c], r.a_y.at[c], r.ac_s.at[0], r.ac_r.at[0], me.at(flip=True))
    ac.start()
    forward(0)
    ac.wait()
    locals_[2].wait()
    r.a_wide[...] = r.a_y[...].reshape(512, 128)
    for img in range(2):
        r.a_own[img * 64 : (img + 1) * 64, :] = r.a_wide[pl.ds(img, 64, stride=8), :].astype(BF16)
    r.part_wide[...] = jnp.zeros_like(r.part_wide)
    for j in range(6):
        columns = nn(r.a_own[...], r.mm[:, j * 128 : (j + 1) * 128])
        for img in range(2):
            r.part_wide[pl.ds(img * 6 + j, 64, stride=16), :] = columns[img * 64 : (img + 1) * 64]
    r.part_low[...] = r.part_wide[...].astype(BF16).reshape(r.part_low.shape)
    mc = remote(r.part_low.at[1 - c], r.m_core, r.mc_s.at[0], r.mc_r.at[0], me.at(flip=True))
    mc.start()
    forward(1)
    weights.step(2)
    for i in range(1, NX):
        there = me.at(dx=i)
        launch(
            remote(
                cot.at[:, aligned(there[1] * att, att)], r.cot_all.at[s], r.ck_s.at[i - 1], r.ck_r.at[i - 1], there
            )
        )
    mc.wait()
    r.m_sum[...] = (r.part_low[c].astype(F32) + r.m_core[...].astype(F32)).astype(BF16)
    my = exchange(me, "dy", NY, lambda i: r.m_sum.at[:, (y + i) % NY], r.m_y, r.my_s, r.my_r)
    finish(my)
    total = r.m_sum[:, y].astype(F32)
    for i in range(NY - 1):
        total += r.m_y[i].astype(F32)
    r.m_plane[...] = total
    mz = exchange(me, "dz", NZ, lambda i: r.m_plane.at[(z + i) % NZ], r.m_z, r.mz_s, r.mz_r)
    weights.step(3)
    finish(mz)
    total = r.m_plane[z]
    for i in range(NZ - 1):
        total += r.m_z[i]
    r.m_own[...] = total
    r.m_all[s] = total
    mx = exchange_at(me, "dx", NX, lambda i: r.m_own, r.m_all.at[s], r.mx_s, r.mx_r)
    weights.step(4)

    label = labels_of(lax.broadcasted_iota(jnp.int32, (rows, 1), 0), c0, c1)
    usable = label < 2
    is0 = label == 0
    lane = lax.broadcasted_iota(jnp.int32, (8, NX * rows), 1)
    for _ in range(NX - 1):
        lane = jnp.where(lane >= rows, lane - rows, lane)
    key_label = labels_of(lane, c0, c1)
    key_label = jnp.where(key_label < 2, key_label, 8)

    finish(mx)
    for k in range(NX):
        for img in range(2):
            for j in range(6):
                at = 768 * k + 128 * j
                r.mod[img : img + 1, at : at + 128] = r.m_all[k, img * 6 + j : img * 6 + j + 1, :]

    def normalize(block):
        x = r.tok_all[block].astype(F32)
        mean = jnp.mean(x, axis=1, keepdims=True)
        centred = x - mean
        inverse = lax.rsqrt(jnp.mean(centred * centred, axis=1, keepdims=True) + EPSILON)
        shift = jnp.where(is0, r.mod[0:1, :width], r.mod[1:2, :width])
        gain = 1.0 + jnp.where(is0, r.mod[0:1, width:], r.mod[1:2, width:])
        value = jnp.where(usable, gain * (centred * inverse) + shift, 0.0).astype(BF16)
        at = pl.ds(pl.multiple_of(block * rows, rows), rows)
        r.modded[at, :] = value
        r.stats[at, 0:1] = mean
        r.stats[at, 1:2] = inverse

    locals_[0].wait()
    normalize(s)
    for i in range(4):
        token_copy(tok.at[row_chunk(i)], sl, i, i, right).wait_recv() if i >= 2 else None
    normalize(sl)
    weights.step(5)
    for i in range(4):
        token_copy(tok.at[row_chunk(3 - i)], sr, 3 - i, 4 + 3 - i, left).wait_recv() if i >= 2 else None
    normalize(sr)
    for i in (0, 1):
        token_copy(tok.at[row_chunk(i)], so, i, 8 + i, right).wait_recv()
        token_copy(tok.at[row_chunk(3 - i)], so, 3 - i, 8 + 3 - i, left).wait_recv()
    normalize(so)
    weights.wait_cross()

    @pl.loop(0, NZ * NY)
    def _(pair):
        first = r.w_all[0, pair % NZ, pair // NZ].astype(F32)
        other = r.w_all[1, pair % NZ, pair // NZ].astype(F32)
        at = pl.ds(pl.multiple_of(48 * pair, 16), 48)
        for t in range(9):
            both = jnp.concatenate([first[24 * t : 24 * t + 24], other[24 * t : 24 * t + 24]], axis=0)
            r.w[at, t * 128 : (t + 1) * 128] = both.astype(BF16)

    for copy in locals_[3:]:
        copy.wait()
    r.low[...] = nt(r.modded[...], r.down[...]).astype(BF16)

    @pl.loop(0, 3)
    def _(n):
        at = aligned(n * att, att)
        r.proj[:, at] = (nn(r.modded[...], r.w[:, at]) + nn(r.low[...], r.up[:, at])).astype(BF16)

    r.kv_grad[...] = jnp.zeros_like(r.kv_grad)
    locals_[1].wait()
    for i in range(1, NX):
        remote(
            cot.at[:, aligned(0, att)], r.cot_all.at[(s + NX - i) % NX], r.ck_s.at[i - 1], r.ck_r.at[i - 1], me.at(dx=i)
        ).wait_recv()

    def attend(block):
        at = pl.ds(pl.multiple_of(block * rows, rows), rows)
        allowed = label == key_label[0:1]
        for h in range(heads):
            cols = slice(h * 128, (h + 1) * 128)
            q = r.proj[at, cols]
            k = r.proj[:, att + h * 128 : att + (h + 1) * 128]
            v = r.proj[:, 2 * att + h * 128 : 2 * att + (h + 1) * 128]
            scores = jnp.where(allowed, nt(q, k), MASKED)
            largest = jnp.max(scores, axis=1, keepdims=True)
            raw = jnp.exp((scores - largest) * scale)
            probs = raw * (1.0 / jnp.sum(raw, axis=1, keepdims=True))
            probs_low = probs.astype(BF16)
            out = jnp.where(usable, nn(probs_low, v), 0.0).astype(BF16)
            r.attn[block, :, cols] = out
            out_grad = jnp.where(usable, r.cot_all[block, :, cols].astype(F32), 0.0)
            delta = jnp.sum(out_grad * out.astype(F32), axis=1, keepdims=True)
            out_grad = out_grad.astype(BF16)
            score_grads = (probs * (nt(out_grad, v) - delta)).astype(BF16)
            r.proj_grad[at, cols] = (nn(score_grads, k) * scale).astype(BF16)
            r.kv_grad[:, h * 128 : (h + 1) * 128] += tn(score_grads, q)
            r.kv_grad[:, att + h * 128 : att + (h + 1) * 128] += tn(probs_low, out_grad)

    mine = aligned(s * att, att)

    @pl.loop(0, NX - 1)
    def _(i):
        block = (s + 1 + i) % NX
        attend(block)
        remote(r.attn.at[block], attn_out.at[:, mine], r.ot_s.at[i], r.ot_r.at[i], (me.dp, block)).start()

    attend(s)
    own_out = pltpu.make_async_copy(r.attn.at[s], attn_out.at[:, mine], r.local.at[7])
    own_out.start()

    r.proj_grad[:, att : 2 * att] = (r.kv_grad[:, :att] * scale).astype(BF16)
    r.proj_grad[:, 2 * att :] = r.kv_grad[:, att:].astype(BF16)
    r.low_grad[...] = nt(r.proj_grad[...], r.up[...]).astype(BF16)

    down_total = tn(r.low_grad[...], r.modded[...])
    for t in range(12):
        r.down_part[t // 3, (t % 3) * 64 : (t % 3 + 1) * 64, :] = down_total[:, t * 128 : (t + 1) * 128]
    dx = exchange(me, "dx", NX, lambda i: r.down_part.at[(NX - 1) - (s + i) % NX], r.down_in, r.dx_s, r.dx_r)

    one_hot = jnp.where(
        key_label == lax.broadcasted_iota(jnp.int32, key_label.shape, 0), 1.0, 0.0
    ).astype(BF16)[:, :rows]

    def grads(block):
        at = pl.ds(pl.multiple_of(block * rows, rows), rows)

        @pl.loop(0, width // att)
        def _(n):
            f = aligned(n * att, att)
            grad = nt(r.proj_grad[at, :], r.w[f, :]) + nn(r.low_grad[at, :], r.down[:, f])
            grad_low = grad.astype(BF16)
            r.pg[block, :, f] = grad_low
            normed = (r.tok_all[block, :, f].astype(F32) - r.stats[at, 0:1]) * r.stats[at, 1:2]
            r.ip[:, f] += nn(one_hot, grad_low)
            r.ip[:, aligned(width + n * att, att)] += nn(one_hot, (grad * normed).astype(BF16))

    def grad_copy(src, dst, slot, there):
        return remote(src, dst, r.gr_s.at[slot], r.gr_r.at[slot], there)

    half = rows // 2
    first, second = pl.ds(0, half), pl.ds(half, half)
    r.ip[...] = jnp.zeros_like(r.ip)
    grads(so)
    step1_r = grad_copy(r.pg.at[so, first], r.half_l, 0, right)
    step1_l = grad_copy(r.pg.at[so, second], r.half_r, 1, left)
    launch(step1_r)
    launch(step1_l)

    up_total = tn(r.low[...], r.proj_grad[...])
    for t in range(9):
        r.lora[t // 3, (t % 3) * 64 : (t % 3 + 1) * 64, :] = up_total[:, t * 128 : (t + 1) * 128]
    finish(dx)
    r.lora[3] = r.down_part[(NX - 1) - s] + r.down_in[0] + r.down_in[1] + r.down_in[2]

    def triple(there):
        step = (s + there) % 4
        down = step // 3
        return ((3 * there + step) // 4) * (1 - down) + 3 * down

    ly = exchange(me, "dy", NY, lambda i: r.lora.at[triple((y + i) % NY)], r.l_y, r.ly_s, r.ly_r)

    grads(sr)
    plain_r = grad_copy(r.pg.at[sr, second], r.from_l.at[second], 2, right)
    launch(plain_r)
    grads(sl)
    plain_l = grad_copy(r.pg.at[sl, first], r.from_r.at[first], 3, left)
    launch(plain_l)
    step1_r.wait_recv()
    r.comb_r[...] = (r.pg[sr, 0:half].astype(F32) + r.half_l[...].astype(F32)).astype(BF16)
    comb_copy_r = grad_copy(r.comb_r, r.from_l.at[first], 4, right)
    launch(comb_copy_r)
    step1_l.wait_recv()
    r.comb_l[...] = (r.pg[sl, half:rows].astype(F32) + r.half_r[...].astype(F32)).astype(BF16)
    comb_copy_l = grad_copy(r.comb_l, r.from_r.at[second], 5, left)
    launch(comb_copy_l)

    finish(ly)
    r.l_plane[...] = (r.lora[triple(y)] + r.l_y[0] + r.l_y[1] + r.l_y[2]).reshape(r.l_plane.shape)
    lz = exchange(me, "dz", NZ, lambda i: r.l_plane.at[(z + i) % NZ], r.l_z, r.lz_s, r.lz_r)

    grads(s)
    for img in range(2):
        for j in range(24):
            r.ip_own[img * 24 + j : img * 24 + j + 1, :] = r.ip[img : img + 1, j * 128 : (j + 1) * 128]
    ip = exchange(me, "dx", NX, lambda i: r.ip_own, r.ip_in, r.ip_s, r.ip_r)
    finish(lz)
    total = r.l_plane[z]
    for i in range(NZ - 1):
        total += r.l_z[i]
    r.l_own[0] = total
    lc = remote(r.l_own.at[0], r.l_core, r.lc_s.at[0], r.lc_r.at[0], me.at(flip=True))
    lc.start()

    finish(ip)
    r.ig_all[c, z, y] = (r.ip_own[...] + r.ip_in[0] + r.ip_in[1] + r.ip_in[2]).astype(BF16)
    images = PlaneGather(me, r.ig_all, *r.gp)
    images.start_y(r.ig_all.at[c, z, y])

    lc.wait()
    r.l_own[1] = r.l_own[0] + r.l_core[...]
    r.trip[s, z] = r.l_own[1]
    lg = exchange_at(me, "dz", NZ, lambda i: r.l_own.at[1], r.trip.at[s, z], r.lg_s, r.lg_r)
    images.wait_y()
    images.step(1)
    finish(lg)
    lx = exchange_at(me, "dx", NX, lambda i: r.trip.at[s], r.trip.at[s], r.lx_s, r.lx_r)
    images.step(2)

    def prepare():
        x = tok_own()
        mean, inverse = own_stats()
        gain = 1.0 + jnp.where(is0, r.mod[0:1, width:], r.mod[1:2, width:])
        return (x - mean) * inverse, inverse, jnp.where(usable, gain, 0.0)

    def own_stats():
        at = pl.ds(pl.multiple_of(s * rows, rows), rows)
        return r.stats[at, 0:1], r.stats[at, 1:2]

    def tok_own():
        return r.tok_all[s].astype(F32)

    images.step(3)
    images.step(4)
    plain_r.wait_recv()
    plain_l.wait_recv()
    comb_copy_r.wait_recv()
    comb_copy_l.wait_recv()
    normed, inverse, gain = prepare()
    g = gain * (r.pg[s].astype(F32) + r.from_l[...].astype(F32) + r.from_r[...].astype(F32))
    token_grad[...] = (
        inverse
        * (g - jnp.mean(g, axis=1, keepdims=True) - normed * jnp.mean(g * normed, axis=1, keepdims=True))
    ).astype(BF16)

    finish(lx)
    start = 72 * (z * NC + c)
    row = lax.broadcasted_iota(jnp.int32, (128, 128), 0)
    col = lax.broadcasted_iota(jnp.int32, (128, 128), 1)

    def picked(tiles, first_column):
        total = jnp.zeros((64, 128), F32)
        for i, tile in enumerate(tiles):
            pick = jnp.where(row + 128 * i == col + first_column, 1.0, 0.0).astype(BF16)
            large = tile.astype(BF16)
            rest = (tile - large.astype(F32)).astype(BF16)
            total += nn(large, pick) + nn(rest, pick)
        return total

    def tiles_of(index):
        flat = r.trip[index].reshape(192, 128)
        return [flat[i * 64 : (i + 1) * 64] for i in range(3)]

    up_tiles = tiles_of((3 * y) % 4) + tiles_of((3 * y + 1) % 4) + tiles_of((3 * y + 2) % 4)
    up_out[...] = picked(up_tiles, 72 * (z * NC + c))[:, :72]
    down_out[...] = picked(tiles_of(3 - y), 24 * (z * NC + c))[:, :24]

    images.step(5)
    images.wait_cross()
    r.ig_wide[...] = r.ig_all[...].reshape(3072, 128).astype(F32)
    for j in range(24):
        total = jnp.zeros((128, 128), F32)
        for img in range(2):
            part = r.ig_wide[pl.ds(img * 24 + j, 64, stride=48), :].astype(BF16)
            total += tn(r.a_own[img * 64 : (img + 1) * 64], part)
        r.part_wide[0:128, :] = total
        mod_grad[:, j * 128 : (j + 1) * 128] = r.part_wide[pl.ds(pl.multiple_of(48 * c, 8), 48), :]

    for copy in sent:
        copy.wait_send()
    for i in range(NX - 1):
        remote(
            r.attn.at[0], attn_out.at[:, aligned(((s + 3 - i) % NX) * att, att)], r.ot_s.at[i], r.ot_r.at[i], right
        ).wait()
    own_out.wait()
    weights.drain()
    images.drain()


def whole(per_image_rows, tok, cot, act, wq, up, down, mm):
    return pl.pallas_call(
        whole_kernel,
        out_shape=(
            jax.ShapeDtypeStruct((192, 1536), BF16),
            jax.ShapeDtypeStruct((192, 1536), BF16),
            jax.ShapeDtypeStruct((64, 24), F32),
            jax.ShapeDtypeStruct((64, 72), F32),
            jax.ShapeDtypeStruct((48, 3072), F32),
        ),
        in_specs=[pl.BlockSpec(memory_space=pltpu.SMEM), ANY, ANY, VM, VM, ANY, ANY, ANY],
        out_specs=(ANY, VM, VM, VM, VM),
        scratch_shapes=scratch_list(),
        compiler_params=pltpu.CompilerParams(
            collective_id=1, has_side_effects=True, vmem_limit_bytes=60 * 1024 * 1024
        ),
        name="whole",
    )(per_image_rows, tok, cot, act, wq, up, down, mm)


def body(
    tokens,
    cotangent,
    condition,
    per_image_rows,
    query_key_value_weight,
    adapter_down,
    adapter_up,
    modulation_matrix,
):
    act = jax.nn.silu(condition[0].astype(F32)).astype(BF16).astype(F32)
    act = act.reshape(2, NY, NZ, 96).transpose(2, 1, 0, 3)
    act = jnp.pad(act, ((0, 0), (0, 0), (0, 6), (0, 32)))
    attention, token_grad, down_grad, up_grad, mod_grad = whole(
        per_image_rows,
        tokens[0],
        cotangent[0],
        act,
        query_key_value_weight,
        adapter_up,
        adapter_down.T,
        modulation_matrix,
    )
    return attention[None], token_grad[None], down_grad.T, up_grad, mod_grad


def solution(mesh):
    in_specs = (
        P("dp", "seq", None),
        P("dp", "seq", None),
        P("dp", None, None),
        P(),
        P("dp", None),
        P(),
        P(),
        P("dp", None),
    )
    out_specs = (
        P("dp", "seq", None),
        P("dp", "seq", None),
        P("dp", None),
        P(None, "dp"),
        P("dp", None),
    )
    return jax.shard_map(body, mesh=mesh, in_specs=in_specs, out_specs=out_specs, check_vma=False)
```

```python
import jax
import jax.numpy as jnp
from jax import lax
from jax.experimental import pallas as pl
from jax.experimental.pallas import tpu as pltpu
from jax.sharding import PartitionSpec as P

HEAD_SIZE = 128
EPSILON = 1e-06
MASKED = -1e30
MESH = pl.DeviceIdType.MESH
NX, NY, NZ, NC = 4, 4, 8, 2
F32, BF16 = jnp.float32, jnp.bfloat16
ANY = pl.BlockSpec(memory_space=pl.ANY)
VM = pl.BlockSpec(memory_space=pltpu.VMEM)


def remote(src, dst, send_sem, recv_sem, device):
    return pltpu.make_async_remote_copy(
        src_ref=src,
        dst_ref=dst,
        send_sem=send_sem,
        recv_sem=recv_sem,
        device_id=device,
        device_id_type=MESH,
    )


class Place:
    def __init__(self):
        self.dp = lax.axis_index("dp")
        self.s = lax.axis_index("seq")
        self.y = self.dp // (NZ * NC)
        self.z = (self.dp // NC) % NZ
        self.c = self.dp % NC

    def at(self, dx=0, dy=0, dz=0, flip=False):
        s = (self.s + dx) % NX if dx else self.s
        y = (self.y + dy) % NY if dy else self.y
        z = (self.z + dz) % NZ if dz else self.z
        c = 1 - self.c if flip else self.c
        return (y * (NZ * NC) + z * NC + c, s)


def enter(me):
    barrier = pltpu.get_barrier_semaphore()
    peers = [me.at(dx=i) for i in range(1, NX)]
    peers += [me.at(dy=i) for i in range(1, NY)]
    peers += [me.at(dz=i) for i in range(1, NZ)]
    peers += [me.at(flip=True)]
    for peer in peers:
        pl.semaphore_signal(barrier, inc=1, device_id=peer, device_id_type=MESH)
    pl.semaphore_wait(barrier, len(peers))


class PlaneGather:
    def __init__(self, me, buf, ysend, yrecv, zsend, zrecv, csend, crecv):
        self.me, self.buf = me, buf
        self.ysend, self.yrecv = ysend, yrecv
        self.zsend, self.zrecv = zsend, zrecv
        self.csend, self.crecv = csend, crecv
        self.sent = []

    def start_y(self, own):
        me = self.me
        for i in range(1, NY):
            copy = remote(
                own, self.buf.at[me.c, me.z, me.y], self.ysend.at[i - 1], self.yrecv.at[i - 1], me.at(dy=i)
            )
            copy.start()
            self.sent.append(copy)

    def wait_y(self):
        me = self.me
        for i in range(1, NY):
            place = self.buf.at[me.c, me.z, (me.y + NY - i) % NY]
            remote(place, place, self.ysend.at[i - 1], self.yrecv.at[i - 1], me.at(dy=i)).wait_recv()

    def ring(self, way, step, part):
        me = self.me
        if way == 0:
            source, there = (me.z + NZ - step + 1) % NZ, me.at(dz=1)
        else:
            source, there = (me.z + step - 1) % NZ, me.at(dz=NZ - 1)
        block = self.buf.at[me.c, source, part]
        at = (way * 4 + step - 1) * NY + part
        return remote(block, block, self.zsend.at[at], self.zrecv.at[at], there)

    def arrive(self, way, step, part):
        me = self.me
        source = (me.z + NZ - step) % NZ if way == 0 else (me.z + step) % NZ
        block = self.buf.at[me.c, source, part]
        at = (way * 4 + step - 1) * NY + part
        there = me.at(dz=1) if way == 0 else me.at(dz=NZ - 1)
        remote(block, block, self.zsend.at[at], self.zrecv.at[at], there).wait_recv()

    def carried(self, way, step, part):
        return step < 4 or (part // 2) == way

    def step(self, step):
        for turn in range(NY):
            for way in (0, 1):
                part = turn if way == 0 else NY - 1 - turn
                if step > 1 and self.carried(way, step - 1, part):
                    self.arrive(way, step - 1, part)
                if step <= 4 and self.carried(way, step, part):
                    copy = self.ring(way, step, part)
                    copy.start()
                    self.sent.append(copy)
        if step == 1:
            self.cross(0)
        elif step == 5:
            self.cross(4)
        else:
            self.cross(step - 1)
            self.cross(NZ - step + 1)

    def cross(self, shift):
        me = self.me
        block = self.buf.at[me.c, (me.z + shift) % NZ]
        copy = remote(block, block, self.csend.at[shift], self.crecv.at[shift], me.at(flip=True))
        copy.start()
        self.sent.append(copy)

    def wait_cross(self, shift):
        me = self.me
        block = self.buf.at[1 - me.c, (me.z + shift) % NZ]
        remote(block, block, self.csend.at[shift], self.crecv.at[shift], me.at(flip=True)).wait_recv()

    def drain(self):
        for copy in self.sent:
            copy.wait_send()


def plane_sems():
    return [
        pltpu.SemaphoreType.DMA((NY - 1,)),
        pltpu.SemaphoreType.DMA((NY - 1,)),
        pltpu.SemaphoreType.DMA((8 * NY,)),
        pltpu.SemaphoreType.DMA((8 * NY,)),
        pltpu.SemaphoreType.DMA((NZ,)),
        pltpu.SemaphoreType.DMA((NZ,)),
    ]


def exchange(me, axis, count, source, slots, send, recv):
    copies = []
    for i in range(1, count):
        copy = remote(source(i), slots.at[i - 1], send.at[i - 1], recv.at[i - 1], me.at(**{axis: i}))
        copy.start()
        copies.append(copy)
    return copies


def exchange_at(me, axis, count, source, target, send, recv):
    copies = []
    for i in range(1, count):
        copy = remote(source(i), target, send.at[i - 1], recv.at[i - 1], me.at(**{axis: i}))
        copy.start()
        copies.append(copy)
    return copies


def nt(a, b):
    return lax.dot_general(a, b, (((1,), (1,)), ((), ())), preferred_element_type=F32)


def tn(a, b):
    return lax.dot_general(a, b, (((0,), (0,)), ((), ())), preferred_element_type=F32)


def nn(a, b):
    return jnp.dot(a, b, preferred_element_type=F32)


def labels_of(rank, c0, c1):
    return (rank >= c0).astype(jnp.int32) + (rank >= c0 + c1).astype(jnp.int32)


def aligned(start, size):
    return pl.ds(pl.multiple_of(start, 128), size)


class Refs:
    pass


SCRATCH = dict(
    tok_all=pltpu.VMEM((NX, 192, 1536), BF16),
    cot_all=pltpu.VMEM((NX, 192, 384), BF16),
    w_all=pltpu.VMEM((NC, NZ, NY, 224, 128), BF16),
    w=pltpu.VMEM((1536, 1152), BF16),
    up=pltpu.VMEM((64, 1152), BF16),
    down=pltpu.VMEM((64, 1536), BF16),
    mm=pltpu.VMEM((256, 768), BF16),
    a_src=pltpu.VMEM((NZ, NY, 8, 128), F32),
    a_z=pltpu.VMEM((NZ, NY, 8, 128), F32),
    a_y=pltpu.VMEM((NC, NY, NZ, 8, 128), F32),
    a_wide=pltpu.VMEM((512, 128), F32),
    a_pair=pltpu.VMEM((128, 256), BF16),
    part_wide=pltpu.VMEM((1024, 128), F32),
    part_low=pltpu.VMEM((NC, NY, NZ, 16, 128), BF16),
    m_core=pltpu.VMEM((NY, NZ, 16, 128), BF16),
    m_sum=pltpu.VMEM((NY, NZ, 16, 128), BF16),
    m_y=pltpu.VMEM((NY - 1, NZ, 16, 128), BF16),
    m_plane=pltpu.VMEM((NZ, 16, 128), F32),
    m_z=pltpu.VMEM((NZ - 1, 16, 128), F32),
    m_own=pltpu.VMEM((16, 128), F32),
    m_all=pltpu.VMEM((NX, 16, 128), F32),
    modded=pltpu.VMEM((768, 1536), BF16),
    stats=pltpu.VMEM((768, 128), F32),
    low=pltpu.VMEM((768, 64), BF16),
    proj=pltpu.VMEM((768, 1152), BF16),
    proj_grad=pltpu.VMEM((768, 1152), BF16),
    kv_grad=pltpu.VMEM((768, 768), F32),
    low_grad=pltpu.VMEM((768, 64), BF16),
    attn=pltpu.VMEM((NX, 192, 384), BF16),
    pg=pltpu.VMEM((NX, 192, 1536), BF16),
    ip=pltpu.VMEM((8, 3072), F32),
    half_l=pltpu.VMEM((96, 1536), BF16),
    half_r=pltpu.VMEM((96, 1536), BF16),
    comb_l=pltpu.VMEM((96, 1536), BF16),
    comb_r=pltpu.VMEM((96, 1536), BF16),
    from_l=pltpu.VMEM((192, 1536), BF16),
    from_r=pltpu.VMEM((192, 1536), BF16),
    ip_own=pltpu.VMEM((48, 128), F32),
    ip_in=pltpu.VMEM((3, 48, 128), F32),
    lo=pltpu.VMEM((NY, 2, 192, 128), BF16),
    l_y=pltpu.VMEM((NY - 1, 2, 192, 128), BF16),
    l_plane=pltpu.VMEM((NZ, 48, 128), BF16),
    l_z=pltpu.VMEM((NZ - 1, 48, 128), BF16),
    l_own=pltpu.VMEM((48, 128), F32),
    l_core=pltpu.VMEM((48, 128), F32),
    l_piece=pltpu.VMEM((48, 128), BF16),
    l_x=pltpu.VMEM((NX, 48, 128), BF16),
)
PAIRS = dict(tk=12, ck=3, az=7, ay=3, ac=1, mc=1, my=3, mz=7, mx=3, gr=6, ot=3, ip=3, iz=7, iy=3, ic=1, ly=3, lz=7, lc=1, lx=3, lg=7)
PLANES = dict(wp=1)
LOCAL = 8


def scratch_list():
    dma = pltpu.SemaphoreType.DMA
    out = list(SCRATCH.values())
    for count in PAIRS.values():
        out += [dma((count,)), dma((count,))]
    for _ in PLANES:
        out += plane_sems()
    return out + [dma((LOCAL,))]


def named(refs):
    r = Refs()
    refs = list(refs)
    for name in SCRATCH:
        setattr(r, name, refs.pop(0))
    for name in PAIRS:
        setattr(r, name + "_s", refs.pop(0))
        setattr(r, name + "_r", refs.pop(0))
    for name in PLANES:
        setattr(r, name, [refs.pop(0) for _ in range(6)])
    r.local = refs.pop(0)
    return r


def whole_kernel(
    rows_ref, tok, cot, cond, wq, up_in, down_in, mm_in,
    attn_out, grad_out, mod, a_own, ig_all, f_all,
    *refs,
):
    r = named(refs)
    me = Place()
    s, y, z, c = me.s, me.y, me.z, me.c
    rows, width, att, heads = 192, 1536, 384, 3
    chunk = rows // 4
    scale = HEAD_SIZE ** (-0.5)
    right, left = me.at(dx=1), me.at(dx=NX - 1)
    sl, sr, so = (s + NX - 1) % NX, (s + 1) % NX, (s + 2) % NX
    c0, c1 = rows_ref[0, me.dp], rows_ref[1, me.dp]

    offset = 48 * me.dp - 128 * ((96 * (me.dp // 2)) // 128)
    r.mm[...] = jnp.zeros_like(r.mm)
    locals_ = [
        pltpu.make_async_copy(tok, r.tok_all.at[s], r.local.at[0]),
        pltpu.make_async_copy(cot.at[:, aligned(s * att, att)], r.cot_all.at[s], r.local.at[1]),
        pltpu.make_async_copy(
            mm_in.at[:, aligned(s * 768, 768)], r.mm.at[pl.ds(pl.multiple_of(offset, 16), 48)], r.local.at[2]
        ),
        pltpu.make_async_copy(down_in, r.down, r.local.at[3]),
    ]
    for b in range(3):
        locals_.append(
            pltpu.make_async_copy(
                up_in.at[:, aligned(b * width + s * att, att)], r.up.at[:, b * att : (b + 1) * att], r.local.at[4 + b]
            )
        )
    for copy in locals_:
        copy.start()
    pieces = []
    for b in range(3):
        block = wq[:, aligned(b * width + s * att, att)].astype(F32)
        pieces += [block[:, i * 128 : (i + 1) * 128] for i in range(3)]
    pieces.append(jnp.zeros((8, 128), F32))
    r.w_all[c, z, y] = jnp.concatenate(pieces, axis=0).astype(BF16)
    wide = cond[...].astype(F32)
    wide = (wide / (1.0 + jnp.exp(-wide))).astype(BF16).astype(F32)
    r.a_src[...] = jnp.zeros_like(r.a_src)
    for p in range(NZ * NY):
        j = (96 * p) // 128
        for img in range(2):
            for t in range(2):
                if j + t < 24:
                    r.a_src[p % NZ, p // NZ, 2 * img + t : 2 * img + t + 1, :] = wide[
                        img : img + 1, (j + t) * 128 : (j + t + 1) * 128
                    ]
    r.a_z[z] = r.a_src[z]

    enter(me)

    sent = []

    def arrived(copies):
        for copy in copies:
            copy.wait_recv()
            sent.append(copy)

    az = exchange_at(me, "dz", NZ, lambda i: r.a_src.at[(z + i) % NZ], r.a_z.at[z], r.az_s, r.az_r)
    weights = PlaneGather(me, r.w_all, *r.wp)
    weights.start_y(r.w_all.at[c, z, y])

    def row_chunk(i):
        return pl.ds(i * chunk, chunk)

    def token_copy(source, owner, i, slot, there):
        return remote(source, r.tok_all.at[owner, row_chunk(i)], r.tk_s.at[slot], r.tk_r.at[slot], there)

    def launch(copy):
        copy.start()
        sent.append(copy)

    for i in range(4):
        launch(token_copy(tok.at[row_chunk(i)], s, i, i, right))
        launch(token_copy(tok.at[row_chunk(3 - i)], s, 3 - i, 4 + 3 - i, left))

    def forward(i):
        token_copy(tok.at[row_chunk(i)], sl, i, i, right).wait_recv()
        launch(token_copy(r.tok_all.at[sl, row_chunk(i)], sl, i, 8 + i, right))
        j = 3 - i
        token_copy(tok.at[row_chunk(j)], sr, j, 4 + j, left).wait_recv()
        launch(token_copy(r.tok_all.at[sr, row_chunk(j)], sr, j, 8 + j, left))

    arrived(az)
    ay = exchange_at(
        me, "dy", NY, lambda i: r.a_z.at[:, (y + i) % NY], r.a_y.at[c, y], r.ay_s, r.ay_r
    )
    r.a_y[c, y] = r.a_z[:, y]
    weights.wait_y()
    weights.step(1)
    arrived(ay)
    ac = remote(r.a_y.at[c], r.a_y.at[c], r.ac_s.at[0], r.ac_r.at[0], me.at(flip=True))
    ac.start()
    forward(0)
    arrived([ac])
    locals_[2].wait()
    r.a_wide[...] = r.a_y[...].reshape(512, 128)
    for img in range(2):
        for t in range(2):
            r.a_pair[img * 64 : (img + 1) * 64, t * 128 : (t + 1) * 128] = r.a_wide[
                pl.ds(2 * img + t, 64, stride=8), :
            ].astype(BF16)
    r.part_wide[...] = jnp.zeros_like(r.part_wide)
    for j in range(6):
        columns = nn(r.a_pair[...], r.mm[:, j * 128 : (j + 1) * 128])
        for img in range(2):
            r.part_wide[pl.ds(img * 6 + j, 64, stride=16), :] = columns[img * 64 : (img + 1) * 64]
    r.part_low[...] = r.part_wide[...].astype(BF16).reshape(r.part_low.shape)
    mc = remote(r.part_low.at[1 - c], r.m_core, r.mc_s.at[0], r.mc_r.at[0], me.at(flip=True))
    mc.start()
    row = lax.broadcasted_iota(jnp.int32, (256, 128), 0)
    col = lax.broadcasted_iota(jnp.int32, (256, 128), 1)
    pick = jnp.where((row == col + offset) & (col < 48), 1.0, 0.0).astype(BF16)
    a_own[...] = nn(r.a_pair[...], pick).astype(BF16)
    r.kv_grad[...] = jnp.zeros_like(r.kv_grad)
    forward(1)
    weights.step(2)
    for i in range(1, NX):
        there = me.at(dx=i)
        launch(
            remote(
                cot.at[:, aligned(there[1] * att, att)], r.cot_all.at[s], r.ck_s.at[i - 1], r.ck_r.at[i - 1], there
            )
        )
    arrived([mc])
    r.m_sum[...] = (r.part_low[c].astype(F32) + r.m_core[...].astype(F32)).astype(BF16)
    my = exchange(me, "dy", NY, lambda i: r.m_sum.at[(y + i) % NY], r.m_y, r.my_s, r.my_r)
    arrived(my)
    total = r.m_sum[y].astype(F32)
    for i in range(NY - 1):
        total += r.m_y[i].astype(F32)
    r.m_plane[...] = total
    mz = exchange(me, "dz", NZ, lambda i: r.m_plane.at[(z + i) % NZ], r.m_z, r.mz_s, r.mz_r)
    weights.step(3)
    arrived(mz)
    total = r.m_plane[z]
    for i in range(NZ - 1):
        total += r.m_z[i]
    r.m_own[...] = total
    r.m_all[s] = total
    mx = exchange_at(me, "dx", NX, lambda i: r.m_own, r.m_all.at[s], r.mx_s, r.mx_r)
    weights.step(4)

    def place(shift):
        weights.wait_cross(shift)
        at_z = (z + shift) % NZ

        @pl.loop(0, NY)
        def _(at_y):
            first = r.w_all[0, at_z, at_y].astype(F32)
            other = r.w_all[1, at_z, at_y].astype(F32)
            at = pl.ds(pl.multiple_of(48 * (NZ * at_y + at_z), 16), 48)
            for t in range(9):
                both = jnp.concatenate([first[24 * t : 24 * t + 24], other[24 * t : 24 * t + 24]], axis=0)
                r.w[at, t * 128 : (t + 1) * 128] = both.astype(BF16)

    label = labels_of(lax.broadcasted_iota(jnp.int32, (rows, 1), 0), c0, c1)
    usable = label < 2
    is0 = label == 0
    lane = lax.broadcasted_iota(jnp.int32, (8, NX * rows), 1)
    for _ in range(NX - 1):
        lane = jnp.where(lane >= rows, lane - rows, lane)
    key_label = labels_of(lane, c0, c1)
    key_label = jnp.where(key_label < 2, key_label, 8)

    place(0)
    place(1)
    place(NZ - 1)
    arrived(mx)
    mod[...] = jnp.zeros_like(mod)
    for k in range(NX):
        for img in range(2):
            for j in range(6):
                at = 768 * k + 128 * j
                mod[img : img + 1, at : at + 128] = r.m_all[k, img * 6 + j : img * 6 + j + 1, :]

    def normalize(block):
        x = r.tok_all[block].astype(F32)
        mean = jnp.mean(x, axis=1, keepdims=True)
        centred = x - mean
        inverse = lax.rsqrt(jnp.mean(centred * centred, axis=1, keepdims=True) + EPSILON)
        shift = jnp.where(is0, mod[0:1, :width], mod[1:2, :width])
        gain = 1.0 + jnp.where(is0, mod[0:1, width:], mod[1:2, width:])
        value = jnp.where(usable, gain * (centred * inverse) + shift, 0.0).astype(BF16)
        at = pl.ds(pl.multiple_of(block * rows, rows), rows)
        r.modded[at, :] = value
        r.stats[at, 0:1] = mean
        r.stats[at, 1:2] = inverse

    locals_[0].wait()
    normalize(s)
    for i in range(4):
        token_copy(tok.at[row_chunk(i)], sl, i, i, right).wait_recv() if i >= 2 else None
    normalize(sl)
    weights.step(5)
    place(2)
    place(NZ - 2)
    for i in range(4):
        token_copy(tok.at[row_chunk(3 - i)], sr, 3 - i, 4 + 3 - i, left).wait_recv() if i >= 2 else None
    normalize(sr)
    for i in (0, 1):
        token_copy(tok.at[row_chunk(i)], so, i, 8 + i, right).wait_recv()
        token_copy(tok.at[row_chunk(3 - i)], so, 3 - i, 8 + 3 - i, left).wait_recv()
    normalize(so)
    place(3)
    place(5)
    place(4)
    for copy in locals_[3:]:
        copy.wait()
    r.low[...] = nt(r.modded[...], r.down[...]).astype(BF16)

    @pl.loop(0, 3)
    def _(n):
        at = aligned(n * att, att)
        r.proj[:, at] = (nn(r.modded[...], r.w[:, at]) + nn(r.low[...], r.up[:, at])).astype(BF16)

    locals_[1].wait()
    for i in range(1, NX):
        remote(
            cot.at[:, aligned(0, att)], r.cot_all.at[(s + NX - i) % NX], r.ck_s.at[i - 1], r.ck_r.at[i - 1], me.at(dx=i)
        ).wait_recv()

    def attend(block):
        at = pl.ds(pl.multiple_of(block * rows, rows), rows)
        allowed = label == key_label[0:1]
        for h in range(heads):
            cols = slice(h * 128, (h + 1) * 128)
            q = r.proj[at, cols]
            k = r.proj[:, att + h * 128 : att + (h + 1) * 128]
            v = r.proj[:, 2 * att + h * 128 : 2 * att + (h + 1) * 128]
            scores = jnp.where(allowed, nt(q, k), MASKED)
            largest = jnp.max(scores, axis=1, keepdims=True)
            raw = jnp.exp((scores - largest) * scale)
            probs = raw * (1.0 / jnp.sum(raw, axis=1, keepdims=True))
            probs_low = probs.astype(BF16)
            out = jnp.where(usable, nn(probs_low, v), 0.0).astype(BF16)
            r.attn[block, :, cols] = out
            out_grad = jnp.where(usable, r.cot_all[block, :, cols].astype(F32), 0.0)
            delta = jnp.sum(out_grad * out.astype(F32), axis=1, keepdims=True)
            out_grad = out_grad.astype(BF16)
            score_grads = (probs * (nt(out_grad, v) - delta)).astype(BF16)
            r.proj_grad[at, cols] = (nn(score_grads, k) * scale).astype(BF16)
            r.kv_grad[h * 128 : (h + 1) * 128, :] += tn(q, score_grads)
            r.kv_grad[att + h * 128 : att + (h + 1) * 128, :] += tn(out_grad, probs_low)

    mine = aligned(s * att, att)

    @pl.loop(0, NX - 1)
    def _(i):
        block = (s + 1 + i) % NX
        attend(block)
        remote(r.attn.at[block], attn_out.at[:, mine], r.ot_s.at[i], r.ot_r.at[i], (me.dp, block)).start()

    attend(s)
    own_out = pltpu.make_async_copy(r.attn.at[s], attn_out.at[:, mine], r.local.at[7])
    own_out.start()

    for h in range(2 * heads):
        turned = r.kv_grad[h * 128 : (h + 1) * 128, :].T
        if h < heads:
            turned = turned * scale
        r.proj_grad[:, att + h * 128 : att + (h + 1) * 128] = turned.astype(BF16)
    r.low_grad[...] = nt(r.proj_grad[...], r.up[...]).astype(BF16)

    one_hot = jnp.where(
        key_label == lax.broadcasted_iota(jnp.int32, key_label.shape, 0), 1.0, 0.0
    ).astype(BF16)[:, :rows]

    def grads(block):
        at = pl.ds(pl.multiple_of(block * rows, rows), rows)

        @pl.loop(0, width // att)
        def _(n):
            f = aligned(n * att, att)
            grad = nt(r.proj_grad[at, :], r.w[f, :]) + nn(r.low_grad[at, :], r.down[:, f])
            grad_low = grad.astype(BF16)
            r.pg[block, :, f] = grad_low
            normed = (r.tok_all[block, :, f].astype(F32) - r.stats[at, 0:1]) * r.stats[at, 1:2]
            r.ip[:, f] += nn(one_hot, grad_low)
            r.ip[:, aligned(width + n * att, att)] += nn(one_hot, (grad * normed).astype(BF16))

    def grad_copy(src, dst, slot, there):
        return remote(src, dst, r.gr_s.at[slot], r.gr_r.at[slot], there)

    half = rows // 2
    first, second = pl.ds(0, half), pl.ds(half, half)
    r.ip[...] = jnp.zeros_like(r.ip)
    grads(so)
    step1_r = grad_copy(r.pg.at[so, first], r.half_l, 0, right)
    step1_l = grad_copy(r.pg.at[so, second], r.half_r, 1, left)
    launch(step1_r)
    launch(step1_l)

    grads(sr)
    plain_r = grad_copy(r.pg.at[sr, second], r.from_l.at[second], 2, right)
    launch(plain_r)
    grads(sl)
    plain_l = grad_copy(r.pg.at[sl, first], r.from_r.at[first], 3, left)
    launch(plain_l)

    r.lo[NX - 1 - s, 0] = jnp.zeros((192, 128), BF16)
    up_total = tn(r.low[...], r.proj_grad[...]).astype(BF16)
    for t in range(9):
        r.lo[(4 * (t // 3) + s) // 3, 0, (t % 3) * 64 : (t % 3 + 1) * 64, :] = up_total[:, t * 128 : (t + 1) * 128]
    down_total = tn(r.low_grad[...], r.modded[...]).astype(BF16)
    for t in range(12):
        r.lo[t // 3, 1, (t % 3) * 64 : (t % 3 + 1) * 64, :] = down_total[:, t * 128 : (t + 1) * 128]
    ly = exchange(me, "dy", NY, lambda i: r.lo.at[(y + i) % NY], r.l_y, r.ly_s, r.ly_r)

    step1_r.wait_recv()
    r.comb_r[...] = (r.pg[sr, 0:half].astype(F32) + r.half_l[...].astype(F32)).astype(BF16)
    comb_copy_r = grad_copy(r.comb_r, r.from_l.at[first], 4, right)
    launch(comb_copy_r)
    step1_l.wait_recv()
    r.comb_l[...] = (r.pg[sl, half:rows].astype(F32) + r.half_r[...].astype(F32)).astype(BF16)
    comb_copy_l = grad_copy(r.comb_l, r.from_r.at[second], 5, left)
    launch(comb_copy_l)

    grads(s)
    for img in range(2):
        for j in range(24):
            r.ip_own[img * 24 + j : img * 24 + j + 1, :] = r.ip[img : img + 1, j * 128 : (j + 1) * 128]
    ip = exchange(me, "dx", NX, lambda i: r.ip_own, r.ip_in, r.ip_s, r.ip_r)

    arrived(ly)
    total = r.lo[y].astype(F32)
    for i in range(NY - 1):
        total += r.l_y[i].astype(F32)
    for i in range(NZ):
        at = slice(24 * i, 24 * i + 24)
        r.l_plane[i] = jnp.concatenate([total[0, at], total[1, at]], axis=0).astype(BF16)
    lz = exchange(me, "dz", NZ, lambda i: r.l_plane.at[(z + i) % NZ], r.l_z, r.lz_s, r.lz_r)

    arrived(ip)
    ig_all[c, y, z] = (r.ip_own[...] + r.ip_in[0] + r.ip_in[1] + r.ip_in[2]).astype(BF16)
    own_ig = ig_all.at[c, y, z]
    iz = exchange_at(me, "dz", NZ, lambda i: own_ig, own_ig, r.iz_s, r.iz_r)

    arrived(lz)
    total = r.l_plane[z].astype(F32)
    for i in range(NZ - 1):
        total += r.l_z[i].astype(F32)
    r.l_own[...] = total
    lc = remote(r.l_own, r.l_core, r.lc_s.at[0], r.lc_r.at[0], me.at(flip=True))
    lc.start()

    arrived(iz)
    column = ig_all.at[c, y]
    iy = exchange_at(me, "dy", NY, lambda i: column, column, r.iy_s, r.iy_r)

    arrived([lc])
    r.l_piece[...] = (r.l_own[...] + r.l_core[...]).astype(BF16)
    r.l_x[s] = r.l_piece[...]
    lx = exchange_at(me, "dx", NX, lambda i: r.l_piece, r.l_x.at[s], r.lx_s, r.lx_r)

    arrived(iy)
    ic = remote(ig_all.at[c], ig_all.at[c], r.ic_s.at[0], r.ic_r.at[0], me.at(flip=True))
    ic.start()

    arrived(lx)
    pieces = [r.l_x[(3 * y + i) % 4].astype(F32)[0:24] for i in range(3)]
    total = r.l_x[0].astype(F32)[24:48]
    for i in range(1, NX):
        total += r.l_x[i].astype(F32)[24:48]
    f_all[z] = jnp.concatenate(pieces + [total], axis=0).astype(BF16)
    lg = exchange_at(me, "dz", NZ, lambda i: f_all.at[z], f_all.at[z], r.lg_s, r.lg_r)

    plain_r.wait_recv()
    plain_l.wait_recv()
    comb_copy_r.wait_recv()
    comb_copy_l.wait_recv()
    grad_out[...] = (r.pg[s].astype(F32) + r.from_l[...].astype(F32) + r.from_r[...].astype(F32)).astype(BF16)
    arrived([ic])
    arrived(lg)

    for copy in sent:
        copy.wait_send()
    for i in range(NX - 1):
        remote(
            r.attn.at[0], attn_out.at[:, aligned(((s + 3 - i) % NX) * att, att)], r.ot_s.at[i], r.ot_r.at[i], right
        ).wait()
    own_out.wait()
    weights.drain()


def whole(counts, tok, cot, cond, wq, up, down, mm):
    return pl.pallas_call(
        whole_kernel,
        out_shape=(
            jax.ShapeDtypeStruct((192, 1536), BF16),
            jax.ShapeDtypeStruct((192, 1536), BF16),
            jax.ShapeDtypeStruct((8, 3072), F32),
            jax.ShapeDtypeStruct((128, 128), BF16),
            jax.ShapeDtypeStruct((NC, NY, NZ, 48, 128), BF16),
            jax.ShapeDtypeStruct((NZ, 96, 128), BF16),
        ),
        in_specs=[pl.BlockSpec(memory_space=pltpu.SMEM), ANY, ANY, VM, VM, ANY, ANY, ANY],
        out_specs=(ANY, VM, VM, VM, VM, VM),
        scratch_shapes=scratch_list(),
        compiler_params=pltpu.CompilerParams(
            collective_id=1, has_side_effects=True, vmem_limit_bytes=60 * 1024 * 1024
        ),
        name="whole",
    )(counts, tok, cot, cond, wq, up, down, mm)


def tail_kernel(
    counts, attn, grad, tok, mod, act, ig, pieces,
    attn_out, token_grad, down_out, up_out, mod_grad,
    ig_wide, sem,
):
    copy = pltpu.make_async_copy(attn, attn_out, sem)
    copy.start()
    rows, width = tok.shape
    dp = lax.axis_index("dp")
    c0, c1 = counts[0, dp], counts[1, dp]
    label = labels_of(lax.broadcasted_iota(jnp.int32, (rows, 1), 0), c0, c1)
    x = tok[...].astype(F32)
    centred = x - jnp.mean(x, axis=1, keepdims=True)
    inverse = lax.rsqrt(jnp.mean(centred * centred, axis=1, keepdims=True) + EPSILON)
    normed = centred * inverse
    gain = 1.0 + jnp.where(label == 0, mod[0:1, width:], mod[1:2, width:])
    g = jnp.where(label < 2, gain * grad[...].astype(F32), 0.0)
    token_grad[...] = (
        inverse
        * (g - jnp.mean(g, axis=1, keepdims=True) - normed * jnp.mean(g * normed, axis=1, keepdims=True))
    ).astype(BF16)

    ig_wide[...] = ig[...].reshape(3072, 128).astype(F32)
    for j in range(24):
        total = jnp.zeros((128, 128), F32)
        for img in range(2):
            part = ig_wide[pl.ds(img * 24 + j, 64, stride=48), :].astype(BF16)
            total += tn(act[img * 64 : (img + 1) * 64], part)
        mod_grad[:, j * 128 : (j + 1) * 128] = total[0:48]

    place = dp % (NZ * NC)
    flat = pieces[...].astype(F32)

    def tiles(i):
        triple = jnp.concatenate([flat[k, 24 * i : 24 * i + 24] for k in range(NZ)], axis=0).astype(BF16)
        return [triple[j * 64 : (j + 1) * 64] for j in range(3)]

    row = lax.broadcasted_iota(jnp.int32, (128, 128), 0)
    col = lax.broadcasted_iota(jnp.int32, (128, 128), 1)
    total = jnp.zeros((64, 128), F32)
    for i, tile in enumerate(tiles(0) + tiles(1) + tiles(2)):
        total += nn(tile, jnp.where(row + 128 * i == col + 72 * place, 1.0, 0.0).astype(BF16))
    up_out[...] = total[:, :72]
    total = jnp.zeros((128, 64), F32)
    for i, tile in enumerate(tiles(3)):
        total += nt(jnp.where(col + 128 * i == row + 24 * place, 1.0, 0.0).astype(BF16), tile)
    down_out[...] = total[:24]
    copy.wait()


def tail(counts, attn, grad, tok, mod, act, ig, pieces):
    return pl.pallas_call(
        tail_kernel,
        out_shape=(
            jax.ShapeDtypeStruct((192, 1536), BF16),
            jax.ShapeDtypeStruct((192, 1536), BF16),
            jax.ShapeDtypeStruct((24, 64), F32),
            jax.ShapeDtypeStruct((64, 72), F32),
            jax.ShapeDtypeStruct((48, 3072), F32),
        ),
        in_specs=[pl.BlockSpec(memory_space=pltpu.SMEM), ANY] + [VM] * 6,
        out_specs=(ANY, VM, VM, VM, VM),
        scratch_shapes=[pltpu.VMEM((3072, 128), F32), pltpu.SemaphoreType.DMA],
        compiler_params=pltpu.CompilerParams(vmem_limit_bytes=32 * 1024 * 1024),
        name="tail",
    )(counts, attn, grad, tok, mod, act, ig, pieces)


def body(
    tokens,
    cotangent,
    condition,
    per_image_rows,
    query_key_value_weight,
    adapter_down,
    adapter_up,
    modulation_matrix,
):
    counts = per_image_rows.T
    attn, grad, mod, act, ig, pieces = whole(
        counts,
        tokens[0],
        cotangent[0],
        condition[0],
        query_key_value_weight,
        adapter_up,
        adapter_down.T,
        modulation_matrix,
    )
    attention, token_grad, down_grad, up_grad, mod_grad = tail(
        counts, attn, grad, tokens[0], mod, act, ig, pieces
    )
    return attention[None], token_grad[None], down_grad, up_grad, mod_grad


def solution(mesh):
    in_specs = (
        P("dp", "seq", None),
        P("dp", "seq", None),
        P("dp", None, None),
        P(),
        P("dp", None),
        P(),
        P(),
        P("dp", None),
    )
    out_specs = (
        P("dp", "seq", None),
        P("dp", "seq", None),
        P("dp", None),
        P(None, "dp"),
        P("dp", None),
    )
    return jax.shard_map(body, mesh=mesh, in_specs=in_specs, out_specs=out_specs, check_vma=False)
```

```python
import jax
import jax.numpy as jnp
from jax import lax
from jax.experimental import pallas as pl
from jax.experimental.pallas import tpu as pltpu
from jax.sharding import PartitionSpec as P

HEAD_SIZE = 128
EPSILON = 1e-06
MASKED = -1e30
MESH = pl.DeviceIdType.MESH
NX, NY, NZ, NC = 4, 4, 8, 2
F32, BF16 = jnp.float32, jnp.bfloat16
ANY = pl.BlockSpec(memory_space=pl.ANY)
VM = pl.BlockSpec(memory_space=pltpu.VMEM)


def remote(src, dst, send_sem, recv_sem, device):
    return pltpu.make_async_remote_copy(
        src_ref=src,
        dst_ref=dst,
        send_sem=send_sem,
        recv_sem=recv_sem,
        device_id=device,
        device_id_type=MESH,
    )


class Place:
    def __init__(self):
        self.dp = lax.axis_index("dp")
        self.s = lax.axis_index("seq")
        self.y = self.dp // (NZ * NC)
        self.z = (self.dp // NC) % NZ
        self.c = self.dp % NC

    def at(self, dx=0, dy=0, dz=0, flip=False):
        s = (self.s + dx) % NX if dx else self.s
        y = (self.y + dy) % NY if dy else self.y
        z = (self.z + dz) % NZ if dz else self.z
        c = 1 - self.c if flip else self.c
        return (y * (NZ * NC) + z * NC + c, s)


def enter(me):
    barrier = pltpu.get_barrier_semaphore()
    peers = [me.at(dx=i) for i in range(1, NX)]
    peers += [me.at(dy=i) for i in range(1, NY)]
    peers += [me.at(dz=i) for i in range(1, NZ)]
    peers += [me.at(dy=i, flip=True) for i in range(NY)]
    for peer in peers:
        pl.semaphore_signal(barrier, inc=1, device_id=peer, device_id_type=MESH)
    pl.semaphore_wait(barrier, len(peers))


HALF = 112


class RowGather:
    def __init__(self, me, buf, ysend, yrecv, zsend, zrecv):
        self.me, self.buf = me, buf
        self.ysend, self.yrecv = ysend, yrecv
        self.zsend, self.zrecv = zsend, zrecv
        self.sent = []

    def block(self, at_z, at_y):
        return self.buf.at[self.me.c, at_z, at_y, pl.ds(0, HALF)]

    def launch(self, copy):
        copy.start()
        self.sent.append(copy)

    def start_y(self):
        me = self.me
        own = self.block(me.z, me.y)
        for i in range(1, NY):
            self.launch(remote(own, own, self.ysend.at[i - 1], self.yrecv.at[i - 1], me.at(dy=i)))

    def wait_y(self):
        me = self.me
        for i in range(1, NY):
            block = self.block(me.z, (me.y + NY - i) % NY)
            remote(block, block, self.ysend.at[i - 1], self.yrecv.at[i - 1], me.at(dy=i)).wait_recv()

    def ring(self, way, step, part, arriving):
        me = self.me
        far = step if arriving else step - 1
        source = (me.z + NZ - far) % NZ if way == 0 else (me.z + far) % NZ
        block = self.block(source, part)
        at = (way * 4 + step - 1) * NY + part
        there = me.at(dz=1) if way == 0 else me.at(dz=NZ - 1)
        return remote(block, block, self.zsend.at[at], self.zrecv.at[at], there)

    def carried(self, way, step, part):
        return step < 4 or (part // 2) == way

    def step(self, step):
        for turn in range(NY):
            for way in (0, 1):
                part = turn if way == 0 else NY - 1 - turn
                if step > 1 and self.carried(way, step - 1, part):
                    self.ring(way, step - 1, part, True).wait_recv()
                if step <= 4 and self.carried(way, step, part):
                    self.launch(self.ring(way, step, part, False))


class ColumnGather:
    def __init__(self, me, buf, zsend, zrecv, ysend, yrecv):
        self.me, self.buf = me, buf
        self.ysend, self.yrecv = ysend, yrecv
        self.zsend, self.zrecv = zsend, zrecv
        self.sent = []

    def block(self, shift, at_y):
        return self.buf.at[self.me.c, (self.me.z + shift) % NZ, at_y, pl.ds(HALF, HALF)]

    def launch(self, copy):
        copy.start()
        self.sent.append(copy)

    def ring(self, way, step, arriving):
        far = step if arriving else step - 1
        block = self.block((NZ - far) % NZ if way == 0 else far, self.me.y)
        at = way * 4 + step - 1
        there = self.me.at(dz=1) if way == 0 else self.me.at(dz=NZ - 1)
        return remote(block, block, self.zsend.at[at], self.zrecv.at[at], there)

    def spread(self, shift):
        block = self.block(shift, self.me.y)
        for i in range(1, NY):
            at = shift * (NY - 1) + i - 1
            self.launch(remote(block, block, self.ysend.at[at], self.yrecv.at[at], self.me.at(dy=i)))

    def wait_spread(self, shift):
        for i in range(1, NY):
            block = self.block(shift, (self.me.y + NY - i) % NY)
            at = shift * (NY - 1) + i - 1
            remote(block, block, self.ysend.at[at], self.yrecv.at[at], self.me.at(dy=i)).wait_recv()

    def step(self, step):
        for way in (0, 1):
            last = 4 - way
            if 1 < step <= last + 1:
                self.ring(way, step - 1, True).wait_recv()
            if step <= last:
                self.launch(self.ring(way, step, False))
        if step == 1:
            self.spread(0)
        else:
            self.spread(NZ - step + 1)
            if step < 5:
                self.spread(step - 1)


class CoreSwap:
    def __init__(self, me, buf, send, recv):
        self.me, self.buf, self.send, self.recv = me, buf, send, recv
        self.sent = []

    def copy(self, at_c, shift):
        block = self.buf.at[at_c, (self.me.z + shift) % NZ]
        return remote(block, block, self.send.at[shift], self.recv.at[shift], self.me.at(flip=True))

    def start(self, shift):
        copy = self.copy(self.me.c, shift)
        copy.start()
        self.sent.append(copy)

    def wait(self, shift):
        self.copy(1 - self.me.c, shift).wait_recv()


def exchange(me, axis, count, source, slots, send, recv):
    copies = []
    for i in range(1, count):
        copy = remote(source(i), slots.at[i - 1], send.at[i - 1], recv.at[i - 1], me.at(**{axis: i}))
        copy.start()
        copies.append(copy)
    return copies


def exchange_at(me, axis, count, source, target, send, recv):
    copies = []
    for i in range(1, count):
        copy = remote(source(i), target, send.at[i - 1], recv.at[i - 1], me.at(**{axis: i}))
        copy.start()
        copies.append(copy)
    return copies


def nt(a, b):
    return lax.dot_general(a, b, (((1,), (1,)), ((), ())), preferred_element_type=F32)


def tn(a, b):
    return lax.dot_general(a, b, (((0,), (0,)), ((), ())), preferred_element_type=F32)


def nn(a, b):
    return jnp.dot(a, b, preferred_element_type=F32)


def sorting(c0, c1, rows):
    here = lax.broadcasted_iota(jnp.int32, (rows, rows), 0)
    source = lax.broadcasted_iota(jnp.int32, (rows, rows), 1)
    later = here >= rows // 2
    rank = jnp.where(later, here - rows // 2, here)
    live = rank < jnp.where(later, c1, c0)
    return jnp.where((source == rank + jnp.where(later, c0, 0)) & live, 1.0, 0.0).astype(BF16)


def aligned(start, size):
    return pl.ds(pl.multiple_of(start, 128), size)


class Refs:
    pass


SCRATCH = dict(
    tok_all=pltpu.VMEM((NX, 192, 1536), BF16),
    cot_all=pltpu.VMEM((NX, 192, 384), BF16),
    w_all=pltpu.VMEM((NC, NZ, NY, 224, 128), BF16),
    w=pltpu.VMEM((1536, 1152), BF16),
    up=pltpu.VMEM((64, 1152), BF16),
    down=pltpu.VMEM((64, 1536), BF16),
    mm=pltpu.VMEM((256, 768), BF16),
    a_rows=pltpu.VMEM((NZ, 16, 128), F32),
    a_src=pltpu.VMEM((NZ, 16, 128), BF16),
    a_z=pltpu.VMEM((NZ, 16, 128), BF16),
    a_turn=pltpu.VMEM((NY, 32, 128), F32),
    a_low=pltpu.VMEM((NY, 32, 128), BF16),
    a_y=pltpu.VMEM((NC, NY, 32, 128), BF16),
    a_wide=pltpu.VMEM((256, 128), F32),
    a_pair=pltpu.VMEM((128, 256), BF16),
    part_wide=pltpu.VMEM((768, 128), F32),
    part_low=pltpu.VMEM((NC, NY, 96, 128), BF16),
    m_in=pltpu.VMEM((7, 96, 128), BF16),
    m_plane=pltpu.VMEM((NZ, 16, 128), F32),
    m_z=pltpu.VMEM((NZ - 1, 16, 128), F32),
    m_own=pltpu.VMEM((16, 128), F32),
    m_all=pltpu.VMEM((NX, 16, 128), F32),
    modded=pltpu.VMEM((768, 1536), BF16),
    stats=pltpu.VMEM((768, 128), F32),
    low=pltpu.VMEM((768, 64), BF16),
    proj=pltpu.VMEM((768, 1152), BF16),
    proj_grad=pltpu.VMEM((768, 1152), BF16),
    low_grad=pltpu.VMEM((768, 64), BF16),
    cot_own=pltpu.VMEM((192, 1536), BF16),
    attn=pltpu.VMEM((NX, 2, 96, 384), BF16),
    pg=pltpu.VMEM((2, NX, 96, 1536), BF16),
    ip=pltpu.VMEM((8, 3072), F32),
    half_l=pltpu.VMEM((2, 48, 1536), BF16),
    half_r=pltpu.VMEM((2, 48, 1536), BF16),
    comb_l=pltpu.VMEM((2, 48, 1536), BF16),
    comb_r=pltpu.VMEM((2, 48, 1536), BF16),
    from_l=pltpu.VMEM((2, 96, 1536), BF16),
    from_r=pltpu.VMEM((2, 96, 1536), BF16),
    ip_own=pltpu.VMEM((48, 128), F32),
    ip_in=pltpu.VMEM((3, 48, 128), F32),
    lo=pltpu.VMEM((NY, 2, 192, 128), BF16),
    l_y=pltpu.VMEM((NY - 1, 2, 192, 128), BF16),
    l_plane=pltpu.VMEM((NZ, 48, 128), BF16),
    l_z=pltpu.VMEM((NZ - 1, 48, 128), BF16),
    l_own=pltpu.VMEM((48, 128), F32),
    l_core=pltpu.VMEM((48, 128), F32),
    l_piece=pltpu.VMEM((48, 128), BF16),
    l_x=pltpu.VMEM((NX, 48, 128), BF16),
)
PAIRS = dict(tk=12, ck=6, az=7, ay=7, my=7, mz=7, mx=3, gr=12, ot=6, ip=3, iz=7, iy=3, ic=1, ly=3, lz=7, lc=1, lx=3, lg=7)
PLANES = dict(wy=3, wz=32, vz=8, vy=24, wc=8)
LOCAL = 8


def scratch_list():
    dma = pltpu.SemaphoreType.DMA
    out = list(SCRATCH.values())
    for count in PAIRS.values():
        out += [dma((count,)), dma((count,))]
    for count in PLANES.values():
        out += [dma((count,)), dma((count,))]
    return out + [dma((LOCAL,))]


def named(refs):
    r = Refs()
    refs = list(refs)
    for name in SCRATCH:
        setattr(r, name, refs.pop(0))
    for name in PAIRS:
        setattr(r, name + "_s", refs.pop(0))
        setattr(r, name + "_r", refs.pop(0))
    for name in PLANES:
        setattr(r, name, [refs.pop(0), refs.pop(0)])
    r.local = refs.pop(0)
    return r


def whole_kernel(
    rows_ref, tok, cot, cond, wq, up_in, down_in, mm_in,
    attn_out, grad_out, mod, a_own, ig_all, f_all,
    *refs,
):
    r = named(refs)
    me = Place()
    s, y, z, c = me.s, me.y, me.z, me.c
    rows, width, att, heads = 192, 1536, 384, 3
    part = rows // 2
    image_rows = NX * part
    chunk = rows // 4
    scale = HEAD_SIZE ** (-0.5)
    right, left = me.at(dx=1), me.at(dx=NX - 1)
    sl, sr, so = (s + NX - 1) % NX, (s + 1) % NX, (s + 2) % NX
    c0, c1 = rows_ref[0, me.dp], rows_ref[1, me.dp]

    offset = 48 * me.dp - 128 * ((96 * (me.dp // 2)) // 128)
    r.mm[...] = jnp.zeros_like(r.mm)
    locals_ = [
        pltpu.make_async_copy(
            mm_in.at[:, aligned(s * 768, 768)], r.mm.at[pl.ds(pl.multiple_of(offset, 16), 48)], r.local.at[0]
        ),
        pltpu.make_async_copy(down_in, r.down, r.local.at[1]),
    ]
    for b in range(3):
        locals_.append(
            pltpu.make_async_copy(
                up_in.at[:, aligned(b * width + s * att, att)], r.up.at[:, b * att : (b + 1) * att], r.local.at[2 + b]
            )
        )
    for copy in locals_:
        copy.start()
    pieces = []
    for b in range(3):
        block = wq[:, aligned(b * width + s * att, att)].astype(F32)
        pieces += [block[:, i * 128 : (i + 1) * 128] for i in range(3)]
    pieces.append(jnp.zeros((8, 128), F32))
    r.w_all[c, z, y] = jnp.concatenate(pieces, axis=0).astype(BF16)
    wide = cond[...].astype(F32)
    wide = (wide / (1.0 + jnp.exp(-wide))).astype(BF16).astype(F32)
    r.a_rows[...] = jnp.zeros_like(r.a_rows)
    for p in range(NZ * NY):
        j = (96 * p) // 128
        for img in range(2):
            for t in range(2):
                if j + t < 24:
                    at = 4 * (p // NZ) + 2 * img + t
                    r.a_rows[p % NZ, at : at + 1, :] = wide[img : img + 1, (j + t) * 128 : (j + t + 1) * 128]
    r.a_src[...] = r.a_rows[...].astype(BF16)
    r.a_z[z] = r.a_src[z]
    r.m_plane[...] = jnp.zeros_like(r.m_plane)
    perm = sorting(c0, c1, rows)
    r.tok_all[s] = nn(perm, tok[...]).astype(BF16)

    enter(me)

    sent = []

    def arrived(copies):
        for copy in copies:
            copy.wait_recv()
            sent.append(copy)

    az = exchange_at(me, "dz", NZ, lambda i: r.a_src.at[(z + i) % NZ], r.a_z.at[z], r.az_s, r.az_r)
    weights = RowGather(me, r.w_all, *r.wy, *r.wz)
    weights.start_y()
    others = ColumnGather(me, r.w_all, *r.vz, *r.vy)
    others.step(1)
    swap = CoreSwap(me, r.w_all, *r.wc)

    def row_chunk(i):
        return pl.ds(i * chunk, chunk)

    def token_copy(source, owner, i, slot, there):
        return remote(source, r.tok_all.at[owner, row_chunk(i)], r.tk_s.at[slot], r.tk_r.at[slot], there)

    def launch(copy):
        copy.start()
        sent.append(copy)

    def own_tokens(img):
        i = 2 * img
        launch(token_copy(r.tok_all.at[s, row_chunk(i)], s, i, i, right))
        launch(token_copy(r.tok_all.at[s, row_chunk(i + 1)], s, i + 1, 4 + i + 1, left))
        launch(token_copy(r.tok_all.at[s, row_chunk(i + 1)], s, i + 1, i + 1, right))
        launch(token_copy(r.tok_all.at[s, row_chunk(i)], s, i, 4 + i, left))

    def forward(img):
        i = 2 * img
        token_copy(r.tok_all.at[s, row_chunk(i)], sl, i, i, right).wait_recv()
        launch(token_copy(r.tok_all.at[sl, row_chunk(i)], sl, i, 8 + i, right))
        i = i + 1
        token_copy(r.tok_all.at[s, row_chunk(i)], sr, i, 4 + i, left).wait_recv()
        launch(token_copy(r.tok_all.at[sr, row_chunk(i)], sr, i, 8 + i, left))

    def wait_tokens(img):
        i = 2 * img
        own = r.tok_all.at[s, row_chunk(i)]
        token_copy(own, sl, i + 1, i + 1, right).wait_recv()
        token_copy(own, sr, i, 4 + i, left).wait_recv()
        token_copy(own, so, i, 8 + i, right).wait_recv()
        token_copy(own, so, i + 1, 8 + i + 1, left).wait_recv()

    def cot_copy(img, i, columns, source):
        at = pl.ds(img * part, part)
        return remote(
            r.cot_own.at[at, columns], r.cot_all.at[source, at],
            r.ck_s.at[3 * img + i - 1], r.ck_r.at[3 * img + i - 1], me.at(dx=i),
        )

    def own_cotangent(img):
        for i in range(1, NX):
            launch(cot_copy(img, i, aligned(((s + i) % NX) * att, att), s))

    def wait_cotangent(img):
        for i in range(1, NX):
            cot_copy(img, i, aligned(0, att), (s + NX - i) % NX).wait_recv()

    own_tokens(0)
    r.cot_own[...] = nn(perm, cot[...]).astype(BF16)
    arrived(az)
    turned = r.a_z[...].astype(F32)
    for at_y in range(NY):
        for at_z in range(NZ):
            r.a_turn[at_y, 4 * at_z : 4 * at_z + 4, :] = turned[at_z, 4 * at_y : 4 * at_y + 4]
    r.a_low[...] = r.a_turn[...].astype(BF16)
    r.a_y[c, y] = r.a_low[y]

    def plane_exchange(source, target, send, recv):
        copies = []
        for i in range(1, 2 * NY):
            dy, flip = i // 2, i % 2 == 1
            there = (y + dy) % NY
            at = (1 - c) if flip else c
            copy = remote(
                source(at, there), target(i - 1), send.at[i - 1], recv.at[i - 1], me.at(dy=dy, flip=flip)
            )
            copy.start()
            copies.append(copy)
        return copies

    ay = plane_exchange(lambda at, there: r.a_low.at[there], lambda i: r.a_y.at[c, y], r.ay_s, r.ay_r)
    weights.wait_y()
    weights.step(1)
    others.step(2)
    arrived(ay)
    locals_[0].wait()
    r.a_wide[...] = r.a_y[...].reshape(256, 128).astype(F32)
    for img in range(2):
        for t in range(2):
            r.a_pair[img * 64 : (img + 1) * 64, t * 128 : (t + 1) * 128] = r.a_wide[
                pl.ds(2 * img + t, 64, stride=4), :
            ].astype(BF16)
    for j in range(6):
        columns = nn(r.a_pair[...], r.mm[:, j * 128 : (j + 1) * 128])
        for img in range(2):
            r.part_wide[pl.ds(img * 6 + j, 64, stride=12), :] = columns[img * 64 : (img + 1) * 64]
    r.part_low[...] = r.part_wide[...].astype(BF16).reshape(r.part_low.shape)
    my = plane_exchange(lambda at, there: r.part_low.at[at, there], lambda i: r.m_in.at[i], r.my_s, r.my_r)
    forward(0)
    own_cotangent(0)
    own_tokens(1)
    others.step(3)
    row = lax.broadcasted_iota(jnp.int32, (256, 128), 0)
    col = lax.broadcasted_iota(jnp.int32, (256, 128), 1)
    pick = jnp.where((row == col + offset) & (col < 48), 1.0, 0.0).astype(BF16)
    a_own[...] = nn(r.a_pair[...], pick).astype(BF16)
    weights.step(2)
    r.cot_all[s] = r.cot_own[:, aligned(s * att, att)]
    arrived(my)
    total = r.part_low[c, y].astype(F32)
    for i in range(7):
        total += r.m_in[i].astype(F32)
    for at_z in range(NZ):
        r.m_plane[at_z, 0:12, :] = total[12 * at_z : 12 * at_z + 12]
    mz = exchange(me, "dz", NZ, lambda i: r.m_plane.at[(z + i) % NZ], r.m_z, r.mz_s, r.mz_r)
    others.step(4)
    weights.step(3)
    arrived(mz)
    total = r.m_plane[z]
    for i in range(NZ - 1):
        total += r.m_z[i]
    r.m_own[...] = total
    r.m_all[s] = total
    mx = exchange_at(me, "dx", NX, lambda i: r.m_own, r.m_all.at[s], r.mx_s, r.mx_r)
    others.step(5)
    weights.step(4)
    for shift in (0, 1, NZ - 1, 2, NZ - 2):
        others.wait_spread(shift)
        swap.start(shift)

    def place(shift):
        swap.wait(shift)
        at_z = (z + shift) % NZ

        @pl.loop(0, NY)
        def _(at_y):
            first = r.w_all[0, at_z, at_y].astype(F32)
            other = r.w_all[1, at_z, at_y].astype(F32)
            at = pl.ds(pl.multiple_of(48 * (NZ * at_y + at_z), 16), 48)
            for t in range(9):
                both = jnp.concatenate([first[24 * t : 24 * t + 24], other[24 * t : 24 * t + 24]], axis=0)
                r.w[at, t * 128 : (t + 1) * 128] = both.astype(BF16)

    arrived(mx)
    mod[...] = jnp.zeros_like(mod)
    for k in range(NX):
        for img in range(2):
            for j in range(6):
                at = 768 * k + 128 * j
                mod[img : img + 1, at : at + 128] = r.m_all[k, img * 6 + j : img * 6 + j + 1, :]

    def normalize(img):
        @pl.loop(0, NX)
        def _(block):
            x = r.tok_all[block, img * part : (img + 1) * part, :].astype(F32)
            mean = jnp.mean(x, axis=1, keepdims=True)
            centred = x - mean
            inverse = lax.rsqrt(jnp.mean(centred * centred, axis=1, keepdims=True) + EPSILON)
            rank = lax.broadcasted_iota(jnp.int32, (part, 1), 0)
            gain = 1.0 + mod[img : img + 1, width:]
            value = gain * (centred * inverse) + mod[img : img + 1, :width]
            at = pl.ds(pl.multiple_of(img * image_rows + block * part, 32), part)
            r.modded[at, :] = jnp.where(rank < (c0, c1)[img], value, 0.0).astype(BF16)
            r.stats[at, 0:1] = mean
            r.stats[at, 1:2] = inverse

    weights.step(5)
    for shift in (3, 5, 4):
        others.wait_spread(shift)
        swap.start(shift)
    wait_tokens(0)
    normalize(0)
    forward(1)
    own_cotangent(1)
    for shift in (0, 1, NZ - 1, 2, NZ - 2, 3, 5, 4):
        place(shift)
    for copy in locals_[1:]:
        copy.wait()

    def project(img):
        at = slice(img * image_rows, (img + 1) * image_rows)
        r.low[at, :] = nt(r.modded[at, :], r.down[...]).astype(BF16)

        @pl.loop(0, 3)
        def _(n):
            cols = aligned(n * att, att)
            r.proj[at, cols] = (nn(r.modded[at, :], r.w[:, cols]) + nn(r.low[at, :], r.up[:, cols])).astype(BF16)

    lane = lax.broadcasted_iota(jnp.int32, (1, image_rows), 1)
    for _ in range(NX - 1):
        lane = jnp.where(lane >= part, lane - part, lane)

    def attend(img):
        at = slice(img * image_rows, (img + 1) * image_rows)
        allowed = lane < (c0, c1)[img]
        for h in range(heads):
            cols = slice(h * 128, (h + 1) * 128)
            key_cols = slice(att + h * 128, att + (h + 1) * 128)
            value_cols = slice(2 * att + h * 128, 2 * att + (h + 1) * 128)
            q, k, v = r.proj[at, cols], r.proj[at, key_cols], r.proj[at, value_cols]
            scores = jnp.where(allowed, nt(q, k), MASKED)
            largest = jnp.max(scores, axis=1, keepdims=True)
            raw = jnp.exp((scores - largest) * scale)
            probs = raw * (1.0 / jnp.sum(raw, axis=1, keepdims=True))
            probs_low = probs.astype(BF16)
            out = nn(probs_low, v).astype(BF16)
            r.attn[:, img, :, cols] = out.reshape(NX, part, 128)
            out_grad = r.cot_all[:, img * part : (img + 1) * part, cols].reshape(image_rows, 128)
            delta = jnp.sum(out_grad.astype(F32) * out.astype(F32), axis=1, keepdims=True)
            score_grads = (probs * (nt(out_grad, v) - delta)).astype(BF16)
            r.proj_grad[at, cols] = (nn(score_grads, k) * scale).astype(BF16)
            r.proj_grad[at, key_cols] = (tn(q, score_grads) * scale).T.astype(BF16)
            r.proj_grad[at, value_cols] = tn(out_grad, probs_low).T.astype(BF16)

    mine = aligned(s * att, att)

    def give(img):
        for i in range(1, NX):
            there = me.at(dx=i)
            launch(
                remote(
                    r.attn.at[there[1], img],
                    attn_out.at[img * part : (img + 1) * part, mine],
                    r.ot_s.at[3 * img + i - 1], r.ot_r.at[3 * img + i - 1], there,
                )
            )
        attn_out[img * part : (img + 1) * part, mine] = r.attn[s, img]

    def grads(img):
        at = slice(img * image_rows, (img + 1) * image_rows)
        r.low_grad[at, :] = nt(r.proj_grad[at, :], r.up[...]).astype(BF16)

        @pl.loop(0, width // att)
        def _(n):
            f = aligned(n * att, att)
            grad = nt(r.proj_grad[at, :], r.w[f, :]) + nn(r.low_grad[at, :], r.down[:, f])
            r.pg[img, :, :, f] = grad.astype(BF16).reshape(NX, part, att)
            x = r.tok_all[:, img * part : (img + 1) * part, f].reshape(image_rows, att).astype(F32)
            normed = (x - r.stats[at, 0:1]) * r.stats[at, 1:2]
            r.ip[img : img + 1, f] = jnp.sum(grad, axis=0, keepdims=True)
            r.ip[img : img + 1, aligned(width + n * att, att)] = jnp.sum(grad * normed, axis=0, keepdims=True)

    half = part // 2
    first, second = pl.ds(0, half), pl.ds(half, half)

    def grad_copy(img, slot):
        src, dst, there = (
            (r.pg.at[img, so, first], r.half_l.at[img], right),
            (r.pg.at[img, so, second], r.half_r.at[img], left),
            (r.pg.at[img, sr, second], r.from_l.at[img, second], right),
            (r.pg.at[img, sl, first], r.from_r.at[img, first], left),
            (r.comb_r.at[img], r.from_l.at[img, first], right),
            (r.comb_l.at[img], r.from_r.at[img, second], left),
        )[slot]
        return remote(src, dst, r.gr_s.at[6 * img + slot], r.gr_r.at[6 * img + slot], there)

    def reduce_first(img):
        for slot in range(4):
            launch(grad_copy(img, slot))

    def reduce_second(img):
        grad_copy(img, 0).wait_recv()
        r.comb_r[img] = (r.pg[img, sr, 0:half].astype(F32) + r.half_l[img].astype(F32)).astype(BF16)
        launch(grad_copy(img, 4))
        grad_copy(img, 1).wait_recv()
        r.comb_l[img] = (r.pg[img, sl, half:part].astype(F32) + r.half_r[img].astype(F32)).astype(BF16)
        launch(grad_copy(img, 5))

    project(0)
    wait_cotangent(0)
    attend(0)
    give(0)
    grads(0)
    reduce_first(0)
    wait_tokens(1)
    normalize(1)
    project(1)
    wait_cotangent(1)
    attend(1)
    give(1)
    reduce_second(0)
    grads(1)
    reduce_first(1)

    for img in range(2):
        for j in range(24):
            r.ip_own[img * 24 + j : img * 24 + j + 1, :] = r.ip[img : img + 1, j * 128 : (j + 1) * 128]
    ip = exchange(me, "dx", NX, lambda i: r.ip_own, r.ip_in, r.ip_s, r.ip_r)

    r.lo[NX - 1 - s, 0] = jnp.zeros((192, 128), BF16)
    up_total = tn(r.low[...], r.proj_grad[...]).astype(BF16)
    for t in range(9):
        r.lo[(4 * (t // 3) + s) // 3, 0, (t % 3) * 64 : (t % 3 + 1) * 64, :] = up_total[:, t * 128 : (t + 1) * 128]
    down_total = tn(r.low_grad[...], r.modded[...]).astype(BF16)
    for t in range(12):
        r.lo[t // 3, 1, (t % 3) * 64 : (t % 3 + 1) * 64, :] = down_total[:, t * 128 : (t + 1) * 128]
    ly = exchange(me, "dy", NY, lambda i: r.lo.at[(y + i) % NY], r.l_y, r.ly_s, r.ly_r)

    reduce_second(1)

    arrived(ly)
    total = r.lo[y].astype(F32)
    for i in range(NY - 1):
        total += r.l_y[i].astype(F32)
    for i in range(NZ):
        at = slice(24 * i, 24 * i + 24)
        r.l_plane[i] = jnp.concatenate([total[0, at], total[1, at]], axis=0).astype(BF16)
    lz = exchange(me, "dz", NZ, lambda i: r.l_plane.at[(z + i) % NZ], r.l_z, r.lz_s, r.lz_r)

    arrived(ip)
    ig_all[c, y, z] = (r.ip_own[...] + r.ip_in[0] + r.ip_in[1] + r.ip_in[2]).astype(BF16)
    own_ig = ig_all.at[c, y, z]
    iz = exchange_at(me, "dz", NZ, lambda i: own_ig, own_ig, r.iz_s, r.iz_r)

    arrived(lz)
    total = r.l_plane[z].astype(F32)
    for i in range(NZ - 1):
        total += r.l_z[i].astype(F32)
    r.l_own[...] = total
    lc = remote(r.l_own, r.l_core, r.lc_s.at[0], r.lc_r.at[0], me.at(flip=True))
    lc.start()

    arrived(iz)
    column = ig_all.at[c, y]
    iy = exchange_at(me, "dy", NY, lambda i: column, column, r.iy_s, r.iy_r)

    arrived([lc])
    r.l_piece[...] = (r.l_own[...] + r.l_core[...]).astype(BF16)
    r.l_x[s] = r.l_piece[...]
    lx = exchange_at(me, "dx", NX, lambda i: r.l_piece, r.l_x.at[s], r.lx_s, r.lx_r)

    arrived(iy)
    ic = remote(ig_all.at[c], ig_all.at[c], r.ic_s.at[0], r.ic_r.at[0], me.at(flip=True))
    ic.start()

    arrived(lx)
    pieces = [r.l_x[(3 * y + i) % 4].astype(F32)[0:24] for i in range(3)]
    total = r.l_x[0].astype(F32)[24:48]
    for i in range(1, NX):
        total += r.l_x[i].astype(F32)[24:48]
    f_all[z] = jnp.concatenate(pieces + [total], axis=0).astype(BF16)
    lg = exchange_at(me, "dz", NZ, lambda i: f_all.at[z], f_all.at[z], r.lg_s, r.lg_r)

    for img in range(2):
        for slot in range(2, 6):
            grad_copy(img, slot).wait_recv()
        grad_out[img * part : (img + 1) * part, :] = (
            r.pg[img, s].astype(F32) + r.from_l[img].astype(F32) + r.from_r[img].astype(F32)
        ).astype(BF16)
    arrived([ic])
    arrived(lg)

    for copy in sent:
        copy.wait_send()
    for img in range(2):
        for i in range(1, NX):
            remote(
                r.attn.at[0, img],
                attn_out.at[img * part : (img + 1) * part, aligned(((s + NX - i) % NX) * att, att)],
                r.ot_s.at[3 * img + i - 1], r.ot_r.at[3 * img + i - 1], right,
            ).wait_recv()
    for copy in weights.sent + others.sent + swap.sent:
        copy.wait_send()


def whole(counts, tok, cot, cond, wq, up, down, mm):
    return pl.pallas_call(
        whole_kernel,
        out_shape=(
            jax.ShapeDtypeStruct((192, 1536), BF16),
            jax.ShapeDtypeStruct((192, 1536), BF16),
            jax.ShapeDtypeStruct((8, 3072), F32),
            jax.ShapeDtypeStruct((128, 128), BF16),
            jax.ShapeDtypeStruct((NC, NY, NZ, 48, 128), BF16),
            jax.ShapeDtypeStruct((NZ, 96, 128), BF16),
        ),
        in_specs=[pl.BlockSpec(memory_space=pltpu.SMEM), VM, VM, VM, VM, ANY, ANY, ANY],
        out_specs=(VM, VM, VM, VM, VM, VM),
        scratch_shapes=scratch_list(),
        compiler_params=pltpu.CompilerParams(
            collective_id=1, has_side_effects=True, vmem_limit_bytes=60 * 1024 * 1024
        ),
        name="whole",
    )(counts, tok, cot, cond, wq, up, down, mm)


def tail_kernel(
    counts, attn, grad, tok, mod, act, ig, pieces,
    attn_out, token_grad, down_out, up_out, mod_grad,
    ig_wide, sorted_grad,
):
    rows, width = tok.shape
    part = rows // 2
    dp = lax.axis_index("dp")
    perm = sorting(counts[0, dp], counts[1, dp], rows)
    attn_out[...] = tn(perm, attn[...]).astype(BF16)
    for img in range(2):
        at = slice(img * part, (img + 1) * part)
        x = nn(perm[at], tok[...])
        centred = x - jnp.mean(x, axis=1, keepdims=True)
        inverse = lax.rsqrt(jnp.mean(centred * centred, axis=1, keepdims=True) + EPSILON)
        normed = centred * inverse
        g = (1.0 + mod[img : img + 1, width:]) * grad[at, :].astype(F32)
        sorted_grad[at, :] = (
            inverse
            * (g - jnp.mean(g, axis=1, keepdims=True) - normed * jnp.mean(g * normed, axis=1, keepdims=True))
        ).astype(BF16)
    token_grad[...] = tn(perm, sorted_grad[...]).astype(BF16)

    ig_wide[...] = ig[...].reshape(3072, 128).astype(F32)
    for j in range(24):
        total = jnp.zeros((128, 128), F32)
        for img in range(2):
            part = ig_wide[pl.ds(img * 24 + j, 64, stride=48), :].astype(BF16)
            total += tn(act[img * 64 : (img + 1) * 64], part)
        mod_grad[:, j * 128 : (j + 1) * 128] = total[0:48]

    place = dp % (NZ * NC)
    flat = pieces[...].astype(F32)

    def tiles(i):
        triple = jnp.concatenate([flat[k, 24 * i : 24 * i + 24] for k in range(NZ)], axis=0).astype(BF16)
        return [triple[j * 64 : (j + 1) * 64] for j in range(3)]

    row = lax.broadcasted_iota(jnp.int32, (128, 128), 0)
    col = lax.broadcasted_iota(jnp.int32, (128, 128), 1)
    total = jnp.zeros((64, 128), F32)
    for i, tile in enumerate(tiles(0) + tiles(1) + tiles(2)):
        total += nn(tile, jnp.where(row + 128 * i == col + 72 * place, 1.0, 0.0).astype(BF16))
    up_out[...] = total[:, :72]
    total = jnp.zeros((128, 64), F32)
    for i, tile in enumerate(tiles(3)):
        total += nt(jnp.where(col + 128 * i == row + 24 * place, 1.0, 0.0).astype(BF16), tile)
    down_out[...] = total[:24]


def tail(counts, attn, grad, tok, mod, act, ig, pieces):
    return pl.pallas_call(
        tail_kernel,
        out_shape=(
            jax.ShapeDtypeStruct((192, 1536), BF16),
            jax.ShapeDtypeStruct((192, 1536), BF16),
            jax.ShapeDtypeStruct((24, 64), F32),
            jax.ShapeDtypeStruct((64, 72), F32),
            jax.ShapeDtypeStruct((48, 3072), F32),
        ),
        in_specs=[pl.BlockSpec(memory_space=pltpu.SMEM)] + [VM] * 7,
        out_specs=(VM, VM, VM, VM, VM),
        scratch_shapes=[pltpu.VMEM((3072, 128), F32), pltpu.VMEM((192, 1536), BF16)],
        compiler_params=pltpu.CompilerParams(vmem_limit_bytes=60 * 1024 * 1024),
        name="tail",
    )(counts, attn, grad, tok, mod, act, ig, pieces)


def body(
    tokens,
    cotangent,
    condition,
    per_image_rows,
    query_key_value_weight,
    adapter_down,
    adapter_up,
    modulation_matrix,
):
    counts = per_image_rows.T
    attn, grad, mod, act, ig, pieces = whole(
        counts,
        tokens[0],
        cotangent[0],
        condition[0],
        query_key_value_weight,
        adapter_up,
        adapter_down.T,
        modulation_matrix,
    )
    attention, token_grad, down_grad, up_grad, mod_grad = tail(
        counts, attn, grad, tokens[0], mod, act, ig, pieces
    )
    return attention[None], token_grad[None], down_grad, up_grad, mod_grad


def solution(mesh):
    in_specs = (
        P("dp", "seq", None),
        P("dp", "seq", None),
        P("dp", None, None),
        P(),
        P("dp", None),
        P(),
        P(),
        P("dp", None),
    )
    out_specs = (
        P("dp", "seq", None),
        P("dp", "seq", None),
        P("dp", None),
        P(None, "dp"),
        P("dp", None),
    )
    return jax.shard_map(body, mesh=mesh, in_specs=in_specs, out_specs=out_specs, check_vma=False)
```

```python
import jax
import jax.numpy as jnp
from jax import lax
from jax.experimental import pallas as pl
from jax.experimental.pallas import tpu as pltpu
from jax.sharding import PartitionSpec as P

HEAD_SIZE = 128
EPSILON = 1e-06
MASKED = -1e30
MESH = pl.DeviceIdType.MESH
NX, NY, NZ, NC = 4, 4, 8, 2
F32, BF16 = jnp.float32, jnp.bfloat16
ANY = pl.BlockSpec(memory_space=pl.ANY)
VM = pl.BlockSpec(memory_space=pltpu.VMEM)


def remote(src, dst, send_sem, recv_sem, device):
    return pltpu.make_async_remote_copy(
        src_ref=src,
        dst_ref=dst,
        send_sem=send_sem,
        recv_sem=recv_sem,
        device_id=device,
        device_id_type=MESH,
    )


class Place:
    def __init__(self):
        self.dp = lax.axis_index("dp")
        self.s = lax.axis_index("seq")
        self.y = self.dp // (NZ * NC)
        self.z = (self.dp // NC) % NZ
        self.c = self.dp % NC

    def at(self, dx=0, dy=0, dz=0, flip=False):
        s = (self.s + dx) % NX if dx else self.s
        y = (self.y + dy) % NY if dy else self.y
        z = (self.z + dz) % NZ if dz else self.z
        c = 1 - self.c if flip else self.c
        return (y * (NZ * NC) + z * NC + c, s)


def peers_of(me):
    peers = [me.at(dx=i) for i in range(1, NX)]
    peers += [me.at(dx=i, flip=True) for i in range(1, NX)]
    peers += [me.at(dy=i) for i in range(1, NY)]
    peers += [me.at(dz=i) for i in range(1, NZ)]
    peers += [me.at(dy=i, flip=True) for i in range(NY)]
    return peers


def greet(me):
    for peer in peers_of(me):
        pl.semaphore_signal(pltpu.get_barrier_semaphore(), inc=1, device_id=peer, device_id_type=MESH)


def enter(me):
    pl.semaphore_wait(pltpu.get_barrier_semaphore(), len(peers_of(me)))


HALF = 112


class RowGather:
    def __init__(self, me, buf, ysend, yrecv, zsend, zrecv):
        self.me, self.buf = me, buf
        self.ysend, self.yrecv = ysend, yrecv
        self.zsend, self.zrecv = zsend, zrecv
        self.sent = []

    def block(self, at_z, at_y):
        return self.buf.at[self.me.c, at_z, at_y, pl.ds(0, HALF)]

    def launch(self, copy):
        copy.start()
        self.sent.append(copy)

    def start_y(self):
        me = self.me
        own = self.block(me.z, me.y)
        for i in range(1, NY):
            self.launch(remote(own, own, self.ysend.at[i - 1], self.yrecv.at[i - 1], me.at(dy=i)))

    def wait_y(self):
        me = self.me
        for i in range(1, NY):
            block = self.block(me.z, (me.y + NY - i) % NY)
            remote(block, block, self.ysend.at[i - 1], self.yrecv.at[i - 1], me.at(dy=i)).wait_recv()

    def ring(self, way, step, part, arriving):
        me = self.me
        far = step if arriving else step - 1
        source = (me.z + NZ - far) % NZ if way == 0 else (me.z + far) % NZ
        block = self.block(source, part)
        at = (way * 4 + step - 1) * NY + part
        there = me.at(dz=1) if way == 0 else me.at(dz=NZ - 1)
        return remote(block, block, self.zsend.at[at], self.zrecv.at[at], there)

    def carried(self, way, step, part):
        return step < 4 or (part // 2) == way

    def step(self, step):
        for turn in range(NY):
            for way in (0, 1):
                part = turn if way == 0 else NY - 1 - turn
                if step > 1 and self.carried(way, step - 1, part):
                    self.ring(way, step - 1, part, True).wait_recv()
                if step <= 4 and self.carried(way, step, part):
                    self.launch(self.ring(way, step, part, False))


class ColumnGather:
    def __init__(self, me, buf, zsend, zrecv, ysend, yrecv):
        self.me, self.buf = me, buf
        self.ysend, self.yrecv = ysend, yrecv
        self.zsend, self.zrecv = zsend, zrecv
        self.sent = []

    def block(self, shift, at_y):
        return self.buf.at[self.me.c, (self.me.z + shift) % NZ, at_y, pl.ds(HALF, HALF)]

    def launch(self, copy):
        copy.start()
        self.sent.append(copy)

    def ring(self, way, step, arriving):
        far = step if arriving else step - 1
        block = self.block((NZ - far) % NZ if way == 0 else far, self.me.y)
        at = way * 4 + step - 1
        there = self.me.at(dz=1) if way == 0 else self.me.at(dz=NZ - 1)
        return remote(block, block, self.zsend.at[at], self.zrecv.at[at], there)

    def spread(self, shift):
        block = self.block(shift, self.me.y)
        for i in range(1, NY):
            at = shift * (NY - 1) + i - 1
            self.launch(remote(block, block, self.ysend.at[at], self.yrecv.at[at], self.me.at(dy=i)))

    def wait_spread(self, shift):
        for i in range(1, NY):
            block = self.block(shift, (self.me.y + NY - i) % NY)
            at = shift * (NY - 1) + i - 1
            remote(block, block, self.ysend.at[at], self.yrecv.at[at], self.me.at(dy=i)).wait_recv()

    def step(self, step):
        for way in (0, 1):
            last = 4 - way
            if 1 < step <= last + 1:
                self.ring(way, step - 1, True).wait_recv()
            if step <= last:
                self.launch(self.ring(way, step, False))
        if step == 1:
            self.spread(0)
        else:
            self.spread(NZ - step + 1)
            if step < 5:
                self.spread(step - 1)


class CoreSwap:
    def __init__(self, me, buf, send, recv):
        self.me, self.buf, self.send, self.recv = me, buf, send, recv
        self.sent = []

    def copy(self, at_c, shift):
        block = self.buf.at[at_c, (self.me.z + shift) % NZ]
        return remote(block, block, self.send.at[shift], self.recv.at[shift], self.me.at(flip=True))

    def start(self, shift):
        copy = self.copy(self.me.c, shift)
        copy.start()
        self.sent.append(copy)

    def wait(self, shift):
        self.copy(1 - self.me.c, shift).wait_recv()


def exchange(me, axis, count, source, slots, send, recv):
    copies = []
    for i in range(1, count):
        copy = remote(source(i), slots.at[i - 1], send.at[i - 1], recv.at[i - 1], me.at(**{axis: i}))
        copy.start()
        copies.append(copy)
    return copies


def exchange_at(me, axis, count, source, target, send, recv):
    copies = []
    for i in range(1, count):
        copy = remote(source(i), target, send.at[i - 1], recv.at[i - 1], me.at(**{axis: i}))
        copy.start()
        copies.append(copy)
    return copies


def nt(a, b):
    return lax.dot_general(a, b, (((1,), (1,)), ((), ())), preferred_element_type=F32)


def tn(a, b):
    return lax.dot_general(a, b, (((0,), (0,)), ((), ())), preferred_element_type=F32)


def nn(a, b):
    return jnp.dot(a, b, preferred_element_type=F32)


def sorting(c0, c1, rows):
    here = lax.broadcasted_iota(jnp.int32, (rows, rows), 0)
    source = lax.broadcasted_iota(jnp.int32, (rows, rows), 1)
    later = here >= rows // 2
    rank = jnp.where(later, here - rows // 2, here)
    live = rank < jnp.where(later, c1, c0)
    return jnp.where((source == rank + jnp.where(later, c0, 0)) & live, 1.0, 0.0).astype(BF16)


def aligned(start, size):
    return pl.ds(pl.multiple_of(start, 128), size)


class Refs:
    pass


SCRATCH = dict(
    tok_raw=pltpu.VMEM((192, 1536), BF16),
    cot_raw=pltpu.VMEM((192, 1536), BF16),
    tok_all=pltpu.VMEM((NX, 192, 1536), BF16),
    cot_all=pltpu.VMEM((NX, 192, 384), BF16),
    w_all=pltpu.VMEM((NC, NZ, NY, 224, 128), BF16),
    w=pltpu.VMEM((1536, 1152), BF16),
    up=pltpu.VMEM((64, 1152), BF16),
    down=pltpu.VMEM((64, 1536), BF16),
    mm=pltpu.VMEM((256, 768), BF16),
    a_rows=pltpu.VMEM((NZ, 16, 128), F32),
    a_src=pltpu.VMEM((NZ, 16, 128), BF16),
    a_z=pltpu.VMEM((NZ, 16, 128), BF16),
    a_turn=pltpu.VMEM((NY, 32, 128), F32),
    a_low=pltpu.VMEM((NY, 32, 128), BF16),
    a_y=pltpu.VMEM((NC, NY, 32, 128), BF16),
    a_wide=pltpu.VMEM((256, 128), F32),
    a_pair=pltpu.VMEM((128, 256), BF16),
    part_wide=pltpu.VMEM((768, 128), F32),
    part_low=pltpu.VMEM((NC, NY, 96, 128), BF16),
    m_in=pltpu.VMEM((7, 96, 128), BF16),
    m_plane=pltpu.VMEM((NZ, 16, 128), F32),
    m_z=pltpu.VMEM((NZ - 1, 16, 128), F32),
    m_own=pltpu.VMEM((16, 128), F32),
    m_all=pltpu.VMEM((NX, 16, 128), F32),
    modded=pltpu.VMEM((768, 1536), BF16),
    stats=pltpu.VMEM((768, 128), F32),
    low=pltpu.VMEM((768, 64), BF16),
    proj=pltpu.VMEM((768, 1152), BF16),
    proj_grad=pltpu.VMEM((768, 1152), BF16),
    low_grad=pltpu.VMEM((768, 64), BF16),
    cot_own=pltpu.VMEM((192, 1536), BF16),
    attn=pltpu.VMEM((NX, 2, 96, 384), BF16),
    pg=pltpu.VMEM((2, NX, 96, 1536), BF16),
    ip=pltpu.VMEM((8, 3072), F32),
    half_l=pltpu.VMEM((2, 48, 1536), BF16),
    half_r=pltpu.VMEM((2, 48, 1536), BF16),
    comb_l=pltpu.VMEM((2, 48, 1536), BF16),
    comb_r=pltpu.VMEM((2, 48, 1536), BF16),
    from_l=pltpu.VMEM((2, 96, 1536), BF16),
    from_r=pltpu.VMEM((2, 96, 1536), BF16),
    ip_own=pltpu.VMEM((2, 24, 128), F32),
    ip_in=pltpu.VMEM((2, 3, 24, 128), F32),
    lo=pltpu.VMEM((NY, 2, 192, 128), BF16),
    l_y=pltpu.VMEM((NY - 1, 2, 192, 128), BF16),
    l_plane=pltpu.VMEM((NZ, 48, 128), BF16),
    l_z=pltpu.VMEM((NZ - 1, 48, 128), BF16),
    l_piece=pltpu.VMEM((48, 128), BF16),
    l_x=pltpu.VMEM((NC, NX, 48, 128), BF16),
)
PAIRS = dict(tk=12, ck=6, az=7, ay=7, my=7, mz=7, mx=3, gr=12, ot=6, ip=6, iz=14, iy=6, ic=2, ly=3, lz=7, lx=7, lg=7)
PLANES = dict(wy=3, wz=32, vz=8, vy=24, wc=8)
LOCAL = 8


def scratch_list():
    dma = pltpu.SemaphoreType.DMA
    out = list(SCRATCH.values())
    for count in PAIRS.values():
        out += [dma((count,)), dma((count,))]
    for count in PLANES.values():
        out += [dma((count,)), dma((count,))]
    return out + [dma((LOCAL,))]


def named(refs):
    r = Refs()
    refs = list(refs)
    for name in SCRATCH:
        setattr(r, name, refs.pop(0))
    for name in PAIRS:
        setattr(r, name + "_s", refs.pop(0))
        setattr(r, name + "_r", refs.pop(0))
    for name in PLANES:
        setattr(r, name, [refs.pop(0), refs.pop(0)])
    r.local = refs.pop(0)
    return r


def whole_kernel(
    rows_ref, tok, cot, cond, wq, up_in, down_in, mm_in,
    attn_out, grad_out, mod, a_own, ig_all, f_all,
    *refs,
):
    r = named(refs)
    me = Place()
    s, y, z, c = me.s, me.y, me.z, me.c
    rows, width, att, heads = 192, 1536, 384, 3
    part = rows // 2
    image_rows = NX * part
    chunk = rows // 4
    scale = HEAD_SIZE ** (-0.5)
    right, left = me.at(dx=1), me.at(dx=NX - 1)
    sl, sr, so = (s + NX - 1) % NX, (s + 1) % NX, (s + 2) % NX
    c0, c1 = rows_ref[0, me.dp], rows_ref[1, me.dp]

    greet(me)
    offset = 48 * me.dp - 128 * ((96 * (me.dp // 2)) // 128)
    r.mm[...] = jnp.zeros_like(r.mm)
    raw_tok = pltpu.make_async_copy(tok, r.tok_raw, r.local.at[5])
    raw_tok.start()
    raw_cot = pltpu.make_async_copy(cot, r.cot_raw, r.local.at[6])
    raw_cot.start()
    locals_ = [
        pltpu.make_async_copy(
            mm_in.at[:, aligned(s * 768, 768)], r.mm.at[pl.ds(pl.multiple_of(offset, 16), 48)], r.local.at[0]
        ),
        pltpu.make_async_copy(down_in, r.down, r.local.at[1]),
    ]
    for b in range(3):
        locals_.append(
            pltpu.make_async_copy(
                up_in.at[:, aligned(b * width + s * att, att)], r.up.at[:, b * att : (b + 1) * att], r.local.at[2 + b]
            )
        )
    for copy in locals_:
        copy.start()
    pieces = []
    for b in range(3):
        block = wq[:, aligned(b * width + s * att, att)].astype(F32)
        pieces += [block[:, i * 128 : (i + 1) * 128] for i in range(3)]
    pieces.append(jnp.zeros((8, 128), F32))
    r.w_all[c, z, y] = jnp.concatenate(pieces, axis=0).astype(BF16)
    wide = cond[...].astype(F32)
    wide = (wide / (1.0 + jnp.exp(-wide))).astype(BF16).astype(F32)
    r.a_rows[...] = jnp.zeros_like(r.a_rows)
    for p in range(NZ * NY):
        j = (96 * p) // 128
        for img in range(2):
            for t in range(2):
                if j + t < 24:
                    at = 4 * (p // NZ) + 2 * img + t
                    r.a_rows[p % NZ, at : at + 1, :] = wide[img : img + 1, (j + t) * 128 : (j + t + 1) * 128]
    r.a_src[...] = r.a_rows[...].astype(BF16)
    r.a_z[z] = r.a_src[z]
    r.m_plane[...] = jnp.zeros_like(r.m_plane)
    perm = sorting(c0, c1, rows)
    raw_tok.wait()
    r.tok_all[s] = nn(perm, r.tok_raw[...]).astype(BF16)

    enter(me)

    sent = []

    def arrived(copies):
        for copy in copies:
            copy.wait_recv()
            sent.append(copy)

    def row_chunk(i):
        return pl.ds(i * chunk, chunk)

    def token_copy(source, owner, i, slot, there):
        return remote(source, r.tok_all.at[owner, row_chunk(i)], r.tk_s.at[slot], r.tk_r.at[slot], there)

    def launch(copy):
        copy.start()
        sent.append(copy)

    def own_tokens(img):
        i = 2 * img
        launch(token_copy(r.tok_all.at[s, row_chunk(i)], s, i, i, right))
        launch(token_copy(r.tok_all.at[s, row_chunk(i + 1)], s, i + 1, 4 + i + 1, left))
        launch(token_copy(r.tok_all.at[s, row_chunk(i + 1)], s, i + 1, i + 1, right))
        launch(token_copy(r.tok_all.at[s, row_chunk(i)], s, i, 4 + i, left))

    def forward(img):
        i = 2 * img
        token_copy(r.tok_all.at[s, row_chunk(i)], sl, i, i, right).wait_recv()
        launch(token_copy(r.tok_all.at[sl, row_chunk(i)], sl, i, 8 + i, right))
        i = i + 1
        token_copy(r.tok_all.at[s, row_chunk(i)], sr, i, 4 + i, left).wait_recv()
        launch(token_copy(r.tok_all.at[sr, row_chunk(i)], sr, i, 8 + i, left))

    def wait_tokens(img):
        i = 2 * img
        own = r.tok_all.at[s, row_chunk(i)]
        token_copy(own, sl, i + 1, i + 1, right).wait_recv()
        token_copy(own, sr, i, 4 + i, left).wait_recv()
        token_copy(own, so, i, 8 + i, right).wait_recv()
        token_copy(own, so, i + 1, 8 + i + 1, left).wait_recv()

    def cot_copy(img, i, columns, source):
        at = pl.ds(img * part, part)
        return remote(
            r.cot_own.at[at, columns], r.cot_all.at[source, at],
            r.ck_s.at[3 * img + i - 1], r.ck_r.at[3 * img + i - 1], me.at(dx=i),
        )

    def own_cotangent(img):
        for i in range(1, NX):
            launch(cot_copy(img, i, aligned(((s + i) % NX) * att, att), s))

    def wait_cotangent(img):
        for i in range(1, NX):
            cot_copy(img, i, aligned(0, att), (s + NX - i) % NX).wait_recv()

    own_tokens(0)
    az = exchange_at(me, "dz", NZ, lambda i: r.a_src.at[(z + i) % NZ], r.a_z.at[z], r.az_s, r.az_r)
    weights = RowGather(me, r.w_all, *r.wy, *r.wz)
    weights.start_y()
    others = ColumnGather(me, r.w_all, *r.vz, *r.vy)
    others.step(1)
    swap = CoreSwap(me, r.w_all, *r.wc)
    raw_cot.wait()
    r.cot_own[...] = nn(perm, r.cot_raw[...]).astype(BF16)
    arrived(az)
    turned = r.a_z[...].astype(F32)
    for at_y in range(NY):
        for at_z in range(NZ):
            r.a_turn[at_y, 4 * at_z : 4 * at_z + 4, :] = turned[at_z, 4 * at_y : 4 * at_y + 4]
    r.a_low[...] = r.a_turn[...].astype(BF16)
    r.a_y[c, y] = r.a_low[y]

    def plane_exchange(source, target, send, recv):
        copies = []
        for i in range(1, 2 * NY):
            dy, flip = i // 2, i % 2 == 1
            there = (y + dy) % NY
            at = (1 - c) if flip else c
            copy = remote(
                source(at, there), target(i - 1), send.at[i - 1], recv.at[i - 1], me.at(dy=dy, flip=flip)
            )
            copy.start()
            copies.append(copy)
        return copies

    ay = plane_exchange(lambda at, there: r.a_low.at[there], lambda i: r.a_y.at[c, y], r.ay_s, r.ay_r)
    weights.wait_y()
    weights.step(1)
    others.step(2)
    arrived(ay)
    locals_[0].wait()
    r.a_wide[...] = r.a_y[...].reshape(256, 128).astype(F32)
    for img in range(2):
        for t in range(2):
            r.a_pair[img * 64 : (img + 1) * 64, t * 128 : (t + 1) * 128] = r.a_wide[
                pl.ds(2 * img + t, 64, stride=4), :
            ].astype(BF16)
    for j in range(6):
        columns = nn(r.a_pair[...], r.mm[:, j * 128 : (j + 1) * 128])
        for img in range(2):
            r.part_wide[pl.ds(img * 6 + j, 64, stride=12), :] = columns[img * 64 : (img + 1) * 64]
    r.part_low[...] = r.part_wide[...].astype(BF16).reshape(r.part_low.shape)
    my = plane_exchange(lambda at, there: r.part_low.at[at, there], lambda i: r.m_in.at[i], r.my_s, r.my_r)
    forward(0)
    own_cotangent(0)
    own_tokens(1)
    others.step(3)
    row = lax.broadcasted_iota(jnp.int32, (256, 128), 0)
    col = lax.broadcasted_iota(jnp.int32, (256, 128), 1)
    pick = jnp.where((row == col + offset) & (col < 48), 1.0, 0.0).astype(BF16)
    a_own[...] = nn(r.a_pair[...], pick).astype(BF16)
    weights.step(2)
    r.cot_all[s] = r.cot_own[:, aligned(s * att, att)]
    arrived(my)
    total = r.part_low[c, y].astype(F32)
    for i in range(7):
        total += r.m_in[i].astype(F32)
    for at_z in range(NZ):
        r.m_plane[at_z, 0:12, :] = total[12 * at_z : 12 * at_z + 12]
    mz = exchange(me, "dz", NZ, lambda i: r.m_plane.at[(z + i) % NZ], r.m_z, r.mz_s, r.mz_r)
    others.step(4)
    weights.step(3)
    arrived(mz)
    total = r.m_plane[z]
    for i in range(NZ - 1):
        total += r.m_z[i]
    r.m_own[...] = total
    r.m_all[s] = total
    mx = exchange_at(me, "dx", NX, lambda i: r.m_own, r.m_all.at[s], r.mx_s, r.mx_r)
    others.step(5)
    weights.step(4)
    for shift in (0, 1, NZ - 1, 2, NZ - 2):
        others.wait_spread(shift)
        swap.start(shift)

    def place(shift):
        swap.wait(shift)
        at_z = (z + shift) % NZ

        @pl.loop(0, NY)
        def _(at_y):
            first = r.w_all[0, at_z, at_y].astype(F32)
            other = r.w_all[1, at_z, at_y].astype(F32)
            at = pl.ds(pl.multiple_of(48 * (NZ * at_y + at_z), 16), 48)
            for t in range(9):
                both = jnp.concatenate([first[24 * t : 24 * t + 24], other[24 * t : 24 * t + 24]], axis=0)
                r.w[at, t * 128 : (t + 1) * 128] = both.astype(BF16)

    arrived(mx)
    mod[...] = jnp.zeros_like(mod)
    for k in range(NX):
        for img in range(2):
            for j in range(6):
                at = 768 * k + 128 * j
                mod[img : img + 1, at : at + 128] = r.m_all[k, img * 6 + j : img * 6 + j + 1, :]

    def normalize(img):
        @pl.loop(0, NX)
        def _(block):
            x = r.tok_all[block, img * part : (img + 1) * part, :].astype(F32)
            mean = jnp.mean(x, axis=1, keepdims=True)
            centred = x - mean
            inverse = lax.rsqrt(jnp.mean(centred * centred, axis=1, keepdims=True) + EPSILON)
            rank = lax.broadcasted_iota(jnp.int32, (part, 1), 0)
            gain = 1.0 + mod[img : img + 1, width:]
            value = gain * (centred * inverse) + mod[img : img + 1, :width]
            at = pl.ds(pl.multiple_of(img * image_rows + block * part, 32), part)
            r.modded[at, :] = jnp.where(rank < (c0, c1)[img], value, 0.0).astype(BF16)
            r.stats[at, 0:1] = mean
            r.stats[at, 1:2] = inverse

    wait_tokens(0)
    normalize(0)
    for shift in (0, 1, NZ - 1):
        place(shift)
    weights.step(5)
    for shift in (3, 5, 4):
        others.wait_spread(shift)
        swap.start(shift)
    forward(1)
    own_cotangent(1)
    for shift in (2, NZ - 2, 3, 5, 4):
        place(shift)
    for copy in locals_[1:]:
        copy.wait()

    def project(img):
        at = slice(img * image_rows, (img + 1) * image_rows)
        r.low[at, :] = nt(r.modded[at, :], r.down[...]).astype(BF16)

        @pl.loop(0, 3)
        def _(n):
            cols = aligned(n * att, att)
            r.proj[at, cols] = (nn(r.modded[at, :], r.w[:, cols]) + nn(r.low[at, :], r.up[:, cols])).astype(BF16)

    lane = lax.broadcasted_iota(jnp.int32, (1, image_rows), 1)
    for _ in range(NX - 1):
        lane = jnp.where(lane >= part, lane - part, lane)

    def attend(img):
        at = slice(img * image_rows, (img + 1) * image_rows)
        allowed = lane < (c0, c1)[img]
        for h in range(heads):
            cols = slice(h * 128, (h + 1) * 128)
            key_cols = slice(att + h * 128, att + (h + 1) * 128)
            value_cols = slice(2 * att + h * 128, 2 * att + (h + 1) * 128)
            q, k, v = r.proj[at, cols], r.proj[at, key_cols], r.proj[at, value_cols]
            scores = jnp.where(allowed, nt(q, k), MASKED)
            largest = jnp.max(scores, axis=1, keepdims=True)
            raw = jnp.exp((scores - largest) * scale)
            probs = raw * (1.0 / jnp.sum(raw, axis=1, keepdims=True))
            probs_low = probs.astype(BF16)
            out = nn(probs_low, v).astype(BF16)
            r.attn[:, img, :, cols] = out.reshape(NX, part, 128)
            out_grad = r.cot_all[:, img * part : (img + 1) * part, cols].reshape(image_rows, 128)
            delta = jnp.sum(out_grad.astype(F32) * out.astype(F32), axis=1, keepdims=True)
            score_grads = (probs * (nt(out_grad, v) - delta)).astype(BF16)
            r.proj_grad[at, cols] = (nn(score_grads, k) * scale).astype(BF16)
            r.proj_grad[at, key_cols] = (tn(q, score_grads) * scale).T.astype(BF16)
            r.proj_grad[at, value_cols] = tn(out_grad, probs_low).T.astype(BF16)

    mine = aligned(s * att, att)

    def give(img):
        for i in range(1, NX):
            there = me.at(dx=i)
            launch(
                remote(
                    r.attn.at[there[1], img],
                    attn_out.at[img * part : (img + 1) * part, mine],
                    r.ot_s.at[3 * img + i - 1], r.ot_r.at[3 * img + i - 1], there,
                )
            )
        attn_out[img * part : (img + 1) * part, mine] = r.attn[s, img]

    def low_grads(img):
        at = slice(img * image_rows, (img + 1) * image_rows)
        r.low_grad[at, :] = nt(r.proj_grad[at, :], r.up[...]).astype(BF16)

    def grads(img):
        at = slice(img * image_rows, (img + 1) * image_rows)

        @pl.loop(0, width // att)
        def _(n):
            f = aligned(n * att, att)
            grad = nt(r.proj_grad[at, :], r.w[f, :]) + nn(r.low_grad[at, :], r.down[:, f])
            r.pg[img, :, :, f] = grad.astype(BF16).reshape(NX, part, att)
            x = r.tok_all[:, img * part : (img + 1) * part, f].reshape(image_rows, att).astype(F32)
            normed = (x - r.stats[at, 0:1]) * r.stats[at, 1:2]
            r.ip[img : img + 1, f] = jnp.sum(grad, axis=0, keepdims=True)
            r.ip[img : img + 1, aligned(width + n * att, att)] = jnp.sum(grad * normed, axis=0, keepdims=True)

    half = part // 2
    first, second = pl.ds(0, half), pl.ds(half, half)

    def grad_copy(img, slot):
        src, dst, there = (
            (r.pg.at[img, so, first], r.half_l.at[img], right),
            (r.pg.at[img, so, second], r.half_r.at[img], left),
            (r.pg.at[img, sr, second], r.from_l.at[img, second], right),
            (r.pg.at[img, sl, first], r.from_r.at[img, first], left),
            (r.comb_r.at[img], r.from_l.at[img, first], right),
            (r.comb_l.at[img], r.from_r.at[img, second], left),
        )[slot]
        return remote(src, dst, r.gr_s.at[6 * img + slot], r.gr_r.at[6 * img + slot], there)

    def reduce_first(img):
        for slot in range(4):
            launch(grad_copy(img, slot))

    def reduce_second(img):
        grad_copy(img, 0).wait_recv()
        r.comb_r[img] = (r.pg[img, sr, 0:half].astype(F32) + r.half_l[img].astype(F32)).astype(BF16)
        launch(grad_copy(img, 4))
        grad_copy(img, 1).wait_recv()
        r.comb_l[img] = (r.pg[img, sl, half:part].astype(F32) + r.half_r[img].astype(F32)).astype(BF16)
        launch(grad_copy(img, 5))

    project(0)
    wait_cotangent(0)
    attend(0)
    give(0)
    low_grads(0)
    grads(0)
    reduce_first(0)

    def image_x(img):
        for j in range(24):
            r.ip_own[img, j : j + 1, :] = r.ip[img : img + 1, j * 128 : (j + 1) * 128]
        return [
            remote(
                r.ip_own.at[img], r.ip_in.at[img, i - 1], r.ip_s.at[3 * img + i - 1], r.ip_r.at[3 * img + i - 1],
                me.at(dx=i),
            )
            for i in range(1, NX)
        ]

    def image_z(img):
        total = r.ip_own[img] + r.ip_in[img, 0] + r.ip_in[img, 1] + r.ip_in[img, 2]
        ig_all[img, c, y, z] = jnp.concatenate([total, jnp.zeros((8, 128), F32)], axis=0).astype(BF16)
        own = ig_all.at[img, c, y, z]
        return [
            remote(own, own, r.iz_s.at[7 * img + i - 1], r.iz_r.at[7 * img + i - 1], me.at(dz=i))
            for i in range(1, NZ)
        ]

    def image_y(img):
        own = ig_all.at[img, c, y]
        return [
            remote(own, own, r.iy_s.at[3 * img + i - 1], r.iy_r.at[3 * img + i - 1], me.at(dy=i))
            for i in range(1, NY)
        ]

    def image_core(img):
        own = ig_all.at[img, c]
        return [remote(own, own, r.ic_s.at[img], r.ic_r.at[img], me.at(flip=True))]

    def go(copies):
        for copy in copies:
            copy.start()
        return copies

    ix = go(image_x(0))
    wait_tokens(1)
    normalize(1)
    project(1)
    arrived(ix)
    iz = go(image_z(0))
    reduce_second(0)
    wait_cotangent(1)
    attend(1)
    give(1)
    arrived(iz)
    iy = go(image_y(0))
    low_grads(1)

    r.lo[NX - 1 - s, 0] = jnp.zeros((192, 128), BF16)
    up_total = tn(r.low[...], r.proj_grad[...]).astype(BF16)
    for t in range(9):
        r.lo[(4 * (t // 3) + s) // 3, 0, (t % 3) * 64 : (t % 3 + 1) * 64, :] = up_total[:, t * 128 : (t + 1) * 128]
    down_total = tn(r.low_grad[...], r.modded[...]).astype(BF16)
    for t in range(12):
        r.lo[t // 3, 1, (t % 3) * 64 : (t % 3 + 1) * 64, :] = down_total[:, t * 128 : (t + 1) * 128]
    ly = exchange(me, "dy", NY, lambda i: r.lo.at[(y + i) % NY], r.l_y, r.ly_s, r.ly_r)

    grads(1)
    reduce_first(1)
    ix = go(image_x(1))
    arrived(iy)
    ic0 = go(image_core(0))

    arrived(ly)
    total = r.lo[y].astype(F32)
    for i in range(NY - 1):
        total += r.l_y[i].astype(F32)
    for i in range(NZ):
        at = slice(24 * i, 24 * i + 24)
        r.l_plane[i] = jnp.concatenate([total[0, at], total[1, at]], axis=0).astype(BF16)
    lz = exchange(me, "dz", NZ, lambda i: r.l_plane.at[(z + i) % NZ], r.l_z, r.lz_s, r.lz_r)

    arrived(ix)
    iz = go(image_z(1))
    arrived(lz)
    total = r.l_plane[z].astype(F32)
    for i in range(NZ - 1):
        total += r.l_z[i].astype(F32)
    r.l_piece[...] = total.astype(BF16)
    r.l_x[c, s] = r.l_piece[...]
    lx = [
        remote(
            r.l_piece, r.l_x.at[c, s], r.lx_s.at[i - 1], r.lx_r.at[i - 1], me.at(dx=i // 2, flip=i % 2 == 1)
        )
        for i in range(1, 2 * NX)
    ]
    go(lx)
    arrived(iz)
    iy = go(image_y(1))
    reduce_second(1)

    arrived(lx)
    sums = [r.l_x[0, i].astype(F32) + r.l_x[1, i].astype(F32) for i in range(NX)]
    pieces = []
    for i in range(3):
        k = (3 * y + i) % 4
        pieces.append((r.l_x[0, k].astype(F32) + r.l_x[1, k].astype(F32))[0:24])
    pieces.append((sums[0] + sums[1] + sums[2] + sums[3])[24:48])
    f_all[z] = jnp.concatenate(pieces, axis=0).astype(BF16)
    lg = exchange_at(me, "dz", NZ, lambda i: f_all.at[z], f_all.at[z], r.lg_s, r.lg_r)

    arrived(iy)
    ic1 = go(image_core(1))
    for img in range(2):
        for slot in range(2, 6):
            grad_copy(img, slot).wait_recv()
        grad_out[img * part : (img + 1) * part, :] = (
            r.pg[img, s].astype(F32) + r.from_l[img].astype(F32) + r.from_r[img].astype(F32)
        ).astype(BF16)
    arrived(ic0)
    arrived(ic1)
    arrived(lg)

    for copy in sent:
        copy.wait_send()
    for img in range(2):
        for i in range(1, NX):
            remote(
                r.attn.at[0, img],
                attn_out.at[img * part : (img + 1) * part, aligned(((s + NX - i) % NX) * att, att)],
                r.ot_s.at[3 * img + i - 1], r.ot_r.at[3 * img + i - 1], right,
            ).wait_recv()
    for copy in weights.sent + others.sent + swap.sent:
        copy.wait_send()


def whole(counts, tok, cot, cond, wq, up, down, mm):
    return pl.pallas_call(
        whole_kernel,
        out_shape=(
            jax.ShapeDtypeStruct((192, 1536), BF16),
            jax.ShapeDtypeStruct((192, 1536), BF16),
            jax.ShapeDtypeStruct((8, 3072), F32),
            jax.ShapeDtypeStruct((128, 128), BF16),
            jax.ShapeDtypeStruct((2, NC, NY, NZ, 32, 128), BF16),
            jax.ShapeDtypeStruct((NZ, 96, 128), BF16),
        ),
        in_specs=[pl.BlockSpec(memory_space=pltpu.SMEM), ANY, ANY, VM, VM, ANY, ANY, ANY],
        out_specs=(VM, VM, VM, VM, VM, VM),
        scratch_shapes=scratch_list(),
        compiler_params=pltpu.CompilerParams(
            collective_id=1, has_side_effects=True, vmem_limit_bytes=60 * 1024 * 1024
        ),
        name="whole",
    )(counts, tok, cot, cond, wq, up, down, mm)


def tail_kernel(
    counts, attn, grad, tok, mod, act, ig, pieces,
    attn_out, token_grad, down_out, up_out, mod_grad,
    ig_wide, sorted_grad,
):
    rows, width = tok.shape
    part = rows // 2
    dp = lax.axis_index("dp")
    perm = sorting(counts[0, dp], counts[1, dp], rows)
    attn_out[...] = tn(perm, attn[...]).astype(BF16)
    for img in range(2):
        at = slice(img * part, (img + 1) * part)
        x = nn(perm[at], tok[...])
        centred = x - jnp.mean(x, axis=1, keepdims=True)
        inverse = lax.rsqrt(jnp.mean(centred * centred, axis=1, keepdims=True) + EPSILON)
        normed = centred * inverse
        g = (1.0 + mod[img : img + 1, width:]) * grad[at, :].astype(F32)
        sorted_grad[at, :] = (
            inverse
            * (g - jnp.mean(g, axis=1, keepdims=True) - normed * jnp.mean(g * normed, axis=1, keepdims=True))
        ).astype(BF16)
    token_grad[...] = tn(perm, sorted_grad[...]).astype(BF16)

    ig_wide[...] = ig[...].reshape(4096, 128).astype(F32)
    for j in range(24):
        total = jnp.zeros((128, 128), F32)
        for img in range(2):
            part = ig_wide[pl.ds(img * 2048 + j, 64, stride=32), :].astype(BF16)
            total += tn(act[img * 64 : (img + 1) * 64], part)
        mod_grad[:, j * 128 : (j + 1) * 128] = total[0:48]

    place = dp % (NZ * NC)
    flat = pieces[...].astype(F32)

    def tiles(i):
        triple = jnp.concatenate([flat[k, 24 * i : 24 * i + 24] for k in range(NZ)], axis=0).astype(BF16)
        return [triple[j * 64 : (j + 1) * 64] for j in range(3)]

    row = lax.broadcasted_iota(jnp.int32, (128, 128), 0)
    col = lax.broadcasted_iota(jnp.int32, (128, 128), 1)
    total = jnp.zeros((64, 128), F32)
    for i, tile in enumerate(tiles(0) + tiles(1) + tiles(2)):
        total += nn(tile, jnp.where(row + 128 * i == col + 72 * place, 1.0, 0.0).astype(BF16))
    up_out[...] = total[:, :72]
    total = jnp.zeros((128, 64), F32)
    for i, tile in enumerate(tiles(3)):
        total += nt(jnp.where(col + 128 * i == row + 24 * place, 1.0, 0.0).astype(BF16), tile)
    down_out[...] = total[:24]


def tail(counts, attn, grad, tok, mod, act, ig, pieces):
    return pl.pallas_call(
        tail_kernel,
        out_shape=(
            jax.ShapeDtypeStruct((192, 1536), BF16),
            jax.ShapeDtypeStruct((192, 1536), BF16),
            jax.ShapeDtypeStruct((24, 64), F32),
            jax.ShapeDtypeStruct((64, 72), F32),
            jax.ShapeDtypeStruct((48, 3072), F32),
        ),
        in_specs=[pl.BlockSpec(memory_space=pltpu.SMEM)] + [VM] * 7,
        out_specs=(VM, VM, VM, VM, VM),
        scratch_shapes=[pltpu.VMEM((4096, 128), F32), pltpu.VMEM((192, 1536), BF16)],
        compiler_params=pltpu.CompilerParams(vmem_limit_bytes=60 * 1024 * 1024),
        name="tail",
    )(counts, attn, grad, tok, mod, act, ig, pieces)


def body(
    tokens,
    cotangent,
    condition,
    per_image_rows,
    query_key_value_weight,
    adapter_down,
    adapter_up,
    modulation_matrix,
):
    counts = per_image_rows.T
    attn, grad, mod, act, ig, pieces = whole(
        counts,
        tokens[0],
        cotangent[0],
        condition[0],
        query_key_value_weight,
        adapter_up,
        adapter_down.T,
        modulation_matrix,
    )
    attention, token_grad, down_grad, up_grad, mod_grad = tail(
        counts, attn, grad, tokens[0], mod, act, ig, pieces
    )
    return attention[None], token_grad[None], down_grad, up_grad, mod_grad


def solution(mesh):
    in_specs = (
        P("dp", "seq", None),
        P("dp", "seq", None),
        P("dp", None, None),
        P(),
        P("dp", None),
        P(),
        P(),
        P("dp", None),
    )
    out_specs = (
        P("dp", "seq", None),
        P("dp", "seq", None),
        P("dp", None),
        P(None, "dp"),
        P("dp", None),
    )
    return jax.shard_map(body, mesh=mesh, in_specs=in_specs, out_specs=out_specs, check_vma=False)
```

```python
import jax
import jax.numpy as jnp
from jax import lax
from jax.experimental import pallas as pl
from jax.experimental.pallas import tpu as pltpu
from jax.sharding import PartitionSpec as P

HEAD_SIZE = 128
EPSILON = 1e-06
MASKED = -1e30
MESH = pl.DeviceIdType.MESH
NX, NY, NZ, NC = 4, 4, 8, 2
F32, BF16 = jnp.float32, jnp.bfloat16
ANY = pl.BlockSpec(memory_space=pl.ANY)
VM = pl.BlockSpec(memory_space=pltpu.VMEM)


def remote(src, dst, send_sem, recv_sem, device):
    return pltpu.make_async_remote_copy(
        src_ref=src,
        dst_ref=dst,
        send_sem=send_sem,
        recv_sem=recv_sem,
        device_id=device,
        device_id_type=MESH,
    )


class Place:
    def __init__(self):
        self.dp = lax.axis_index("dp")
        self.s = lax.axis_index("seq")
        self.y = self.dp // (NZ * NC)
        self.z = (self.dp // NC) % NZ
        self.c = self.dp % NC

    def at(self, dx=0, dy=0, dz=0, flip=False):
        s = (self.s + dx) % NX if dx else self.s
        y = (self.y + dy) % NY if dy else self.y
        z = (self.z + dz) % NZ if dz else self.z
        c = 1 - self.c if flip else self.c
        return (y * (NZ * NC) + z * NC + c, s)


def peers_of(me):
    peers = [me.at(dx=i) for i in range(1, NX)]
    peers += [me.at(dx=i, flip=True) for i in range(1, NX)]
    peers += [me.at(dy=i) for i in range(1, NY)]
    peers += [me.at(dz=i) for i in range(1, NZ)]
    peers += [me.at(dy=i, flip=True) for i in range(NY)]
    return peers


def greet(me):
    for peer in peers_of(me):
        pl.semaphore_signal(pltpu.get_barrier_semaphore(), inc=1, device_id=peer, device_id_type=MESH)


def enter(me):
    pl.semaphore_wait(pltpu.get_barrier_semaphore(), len(peers_of(me)))


HALF = 112


class Batch:
    def __init__(self, me, copies, sample, send, recv):
        self.all = remote(sample, sample, send, recv, me.at(dx=1))
        for copy in copies:
            copy.start()

    def arrived(self):
        self.all.wait_recv()

    def left(self):
        self.all.wait_send()


class RowGather:
    def __init__(self, me, buf, ysend, yrecv, zsend, zrecv):
        self.me, self.buf = me, buf
        self.ysend, self.yrecv = ysend.at[0], yrecv.at[0]
        self.zsend, self.zrecv = zsend.at[0], zrecv

    def start_y(self):
        me = self.me
        own = self.buf.at[me.c, me.z, me.y, pl.ds(0, HALF)]
        copies = [remote(own, own, self.ysend, self.yrecv, me.at(dy=i)) for i in range(1, NY)]
        sample = self.buf.at[me.c, me.z, pl.ds(0, 3), pl.ds(0, HALF)]
        self.first = Batch(me, copies, sample, self.ysend, self.yrecv)

    def ring(self, way, step, arriving):
        me = self.me
        far = step if arriving else step - 1
        source = (me.z + NZ - far) % NZ if way == 0 else (me.z + far) % NZ
        ys = pl.ds(0, NY) if step < 4 else pl.ds(2 * way, 2)
        block = self.buf.at[me.c, source, ys, pl.ds(0, HALF)]
        there = me.at(dz=1) if way == 0 else me.at(dz=NZ - 1)
        return remote(block, block, self.zsend, self.zrecv.at[way * 4 + step - 1], there)

    def step(self, step):
        for way in (0, 1):
            if step > 1:
                self.ring(way, step - 1, True).wait_recv()
            if step <= 4:
                self.ring(way, step, False).start()

    def left(self):
        me = self.me
        self.first.left()
        sample = self.buf.at[me.c, pl.ds(0, 7), pl.ds(0, NY), pl.ds(0, HALF)]
        remote(sample, sample, self.zsend, self.zrecv.at[0], me.at(dz=1)).wait_send()


class ColumnGather:
    def __init__(self, me, buf, zsend, zrecv, ysend, yrecv):
        self.me, self.buf = me, buf
        self.ysend, self.yrecv = ysend.at[0], yrecv
        self.zsend, self.zrecv = zsend.at[0], zrecv

    def block(self, shift, ys):
        return self.buf.at[self.me.c, (self.me.z + shift) % NZ, ys, pl.ds(HALF, HALF)]

    def ring(self, way, step, arriving):
        far = step if arriving else step - 1
        block = self.block((NZ - far) % NZ if way == 0 else far, self.me.y)
        there = self.me.at(dz=1) if way == 0 else self.me.at(dz=NZ - 1)
        return remote(block, block, self.zsend, self.zrecv.at[way * 4 + step - 1], there)

    def spread(self, shift):
        block = self.block(shift, self.me.y)
        for i in range(1, NY):
            remote(block, block, self.ysend, self.yrecv.at[shift], self.me.at(dy=i)).start()

    def wait_spread(self, shift):
        sample = self.block(shift, pl.ds(0, 3))
        remote(sample, sample, self.ysend, self.yrecv.at[shift], self.me.at(dy=1)).wait_recv()

    def step(self, step):
        for way in (0, 1):
            last = 4 - way
            if 1 < step <= last + 1:
                self.ring(way, step - 1, True).wait_recv()
            if step <= last:
                self.ring(way, step, False).start()
        if step == 1:
            self.spread(0)
        else:
            self.spread(NZ - step + 1)
            if step < 5:
                self.spread(step - 1)

    def left(self):
        me = self.me
        sample = self.buf.at[me.c, pl.ds(0, 7), 0, pl.ds(HALF, HALF)]
        remote(sample, sample, self.zsend, self.zrecv.at[0], me.at(dz=1)).wait_send()
        sample = self.buf.at[me.c, pl.ds(0, NZ), pl.ds(0, 3), pl.ds(HALF, HALF)]
        remote(sample, sample, self.ysend, self.yrecv.at[0], me.at(dy=1)).wait_send()


class CoreSwap:
    def __init__(self, me, buf, send, recv):
        self.me, self.buf, self.send, self.recv = me, buf, send.at[0], recv

    def copy(self, at_c, shift):
        block = self.buf.at[at_c, (self.me.z + shift) % NZ]
        return remote(block, block, self.send, self.recv.at[shift], self.me.at(flip=True))

    def start(self, shift):
        self.copy(self.me.c, shift).start()

    def wait(self, shift):
        self.copy(1 - self.me.c, shift).wait_recv()

    def left(self):
        block = self.buf.at[self.me.c]
        remote(block, block, self.send, self.recv.at[0], self.me.at(flip=True)).wait_send()


def exchange(me, axis, count, source, target, sample, send, recv):
    copies = [
        remote(source(i), target(i), send.at[0], recv.at[0], me.at(**{axis: i})) for i in range(1, count)
    ]
    return Batch(me, copies, sample, send.at[0], recv.at[0])

def nt(a, b):
    return lax.dot_general(a, b, (((1,), (1,)), ((), ())), preferred_element_type=F32)


def tn(a, b):
    return lax.dot_general(a, b, (((0,), (0,)), ((), ())), preferred_element_type=F32)


def nn(a, b):
    return jnp.dot(a, b, preferred_element_type=F32)


def sorting(c0, c1, rows):
    here = lax.broadcasted_iota(jnp.int32, (rows, rows), 0)
    source = lax.broadcasted_iota(jnp.int32, (rows, rows), 1)
    later = here >= rows // 2
    rank = jnp.where(later, here - rows // 2, here)
    live = rank < jnp.where(later, c1, c0)
    return jnp.where((source == rank + jnp.where(later, c0, 0)) & live, 1.0, 0.0).astype(BF16)


def aligned(start, size):
    return pl.ds(pl.multiple_of(start, 128), size)


class Refs:
    pass


SCRATCH = dict(
    tok_raw=pltpu.VMEM((192, 1536), BF16),
    cot_raw=pltpu.VMEM((192, 1536), BF16),
    tok_all=pltpu.VMEM((NX, 192, 1536), BF16),
    cot_all=pltpu.VMEM((NX, 192, 384), BF16),
    w_all=pltpu.VMEM((NC, NZ, NY, 224, 128), BF16),
    w=pltpu.VMEM((1536, 1152), BF16),
    up=pltpu.VMEM((64, 1152), BF16),
    down=pltpu.VMEM((64, 1536), BF16),
    mm=pltpu.VMEM((256, 768), BF16),
    a_rows=pltpu.VMEM((NZ, 16, 128), F32),
    a_src=pltpu.VMEM((NZ, 16, 128), BF16),
    a_z=pltpu.VMEM((NZ, 16, 128), BF16),
    a_turn=pltpu.VMEM((NY, 32, 128), F32),
    a_low=pltpu.VMEM((NY, 32, 128), BF16),
    a_y=pltpu.VMEM((NC * NY, 32, 128), BF16),
    a_wide=pltpu.VMEM((256, 128), F32),
    a_pair=pltpu.VMEM((128, 256), BF16),
    part_wide=pltpu.VMEM((768, 128), F32),
    part_low=pltpu.VMEM((NC, NY, 96, 128), BF16),
    m_in=pltpu.VMEM((7, 96, 128), BF16),
    m_plane=pltpu.VMEM((NZ, 16, 128), F32),
    m_z=pltpu.VMEM((NZ - 1, 16, 128), F32),
    m_own=pltpu.VMEM((16, 128), F32),
    m_all=pltpu.VMEM((NX, 16, 128), F32),
    modded=pltpu.VMEM((768, 1536), BF16),
    stats=pltpu.VMEM((768, 128), F32),
    low=pltpu.VMEM((768, 64), BF16),
    proj=pltpu.VMEM((768, 1152), BF16),
    proj_grad=pltpu.VMEM((768, 1152), BF16),
    low_grad=pltpu.VMEM((768, 64), BF16),
    cot_own=pltpu.VMEM((192, 1536), BF16),
    attn=pltpu.VMEM((NX, 2, 96, 384), BF16),
    pg=pltpu.VMEM((2, NX, 96, 1536), BF16),
    ip=pltpu.VMEM((8, 3072), F32),
    half_l=pltpu.VMEM((2, 48, 1536), BF16),
    half_r=pltpu.VMEM((2, 48, 1536), BF16),
    comb_l=pltpu.VMEM((2, 48, 1536), BF16),
    comb_r=pltpu.VMEM((2, 48, 1536), BF16),
    from_l=pltpu.VMEM((2, 96, 1536), BF16),
    from_r=pltpu.VMEM((2, 96, 1536), BF16),
    ip_own=pltpu.VMEM((48, 128), F32),
    ip_in=pltpu.VMEM((3, 48, 128), F32),
    lo=pltpu.VMEM((NY, 2, 192, 128), BF16),
    l_y=pltpu.VMEM((NY - 1, 2, 192, 128), BF16),
    l_plane=pltpu.VMEM((NZ, 48, 128), BF16),
    l_z=pltpu.VMEM((NZ - 1, 48, 128), BF16),
    l_piece=pltpu.VMEM((48, 128), BF16),
    l_x=pltpu.VMEM((NC * NX, 48, 128), BF16),
)
PAIRS = dict(
    tk=(1, 12), ck=(2, 2), az=(1, 1), ay=(1, 1), my=(1, 1), mz=(1, 1), mx=(1, 1), gr=(2, 12), ot=(2, 2),
    ip=(1, 1), iz=(1, 1), iy=(1, 1), ic=(1, 1), ly=(1, 1), lz=(1, 1), lx=(1, 1), lg=(1, 1),
)
PLANES = dict(wy=(1, 1), wz=(1, 8), vz=(1, 8), vy=(1, 8), wc=(1, 8))
LOCAL = 8


def scratch_list():
    dma = pltpu.SemaphoreType.DMA
    out = list(SCRATCH.values())
    for send, recv in list(PAIRS.values()) + list(PLANES.values()):
        out += [dma((send,)), dma((recv,))]
    return out + [dma((LOCAL,))]


def named(refs):
    r = Refs()
    refs = list(refs)
    for name in SCRATCH:
        setattr(r, name, refs.pop(0))
    for name in PAIRS:
        setattr(r, name + "_s", refs.pop(0))
        setattr(r, name + "_r", refs.pop(0))
    for name in PLANES:
        setattr(r, name, [refs.pop(0), refs.pop(0)])
    r.local = refs.pop(0)
    return r


def whole_kernel(
    rows_ref, tok, cot, cond, wq, up_in, down_in, mm_in,
    attn_out, grad_out, mod, a_own, ig_all, f_all,
    *refs,
):
    r = named(refs)
    me = Place()
    s, y, z, c = me.s, me.y, me.z, me.c
    rows, width, att, heads = 192, 1536, 384, 3
    part = rows // 2
    image_rows = NX * part
    chunk = rows // 4
    scale = HEAD_SIZE ** (-0.5)
    right, left = me.at(dx=1), me.at(dx=NX - 1)
    sl, sr, so = (s + NX - 1) % NX, (s + 1) % NX, (s + 2) % NX
    c0, c1 = rows_ref[0, me.dp], rows_ref[1, me.dp]

    greet(me)
    offset = 48 * me.dp - 128 * ((96 * (me.dp // 2)) // 128)
    r.mm[...] = jnp.zeros_like(r.mm)
    raw_tok = pltpu.make_async_copy(tok, r.tok_raw, r.local.at[5])
    raw_tok.start()
    raw_cot = pltpu.make_async_copy(cot, r.cot_raw, r.local.at[6])
    raw_cot.start()
    locals_ = [
        pltpu.make_async_copy(
            mm_in.at[:, aligned(s * 768, 768)], r.mm.at[pl.ds(pl.multiple_of(offset, 16), 48)], r.local.at[0]
        ),
        pltpu.make_async_copy(down_in, r.down, r.local.at[1]),
    ]
    for b in range(3):
        locals_.append(
            pltpu.make_async_copy(
                up_in.at[:, aligned(b * width + s * att, att)], r.up.at[:, b * att : (b + 1) * att], r.local.at[2 + b]
            )
        )
    for copy in locals_:
        copy.start()
    pieces = []
    for b in range(3):
        block = wq[:, aligned(b * width + s * att, att)].astype(F32)
        pieces += [block[:, i * 128 : (i + 1) * 128] for i in range(3)]
    pieces.append(jnp.zeros((8, 128), F32))
    r.w_all[c, z, y] = jnp.concatenate(pieces, axis=0).astype(BF16)
    wide = cond[...].astype(F32)
    wide = (wide / (1.0 + jnp.exp(-wide))).astype(BF16).astype(F32)
    r.a_rows[...] = jnp.zeros_like(r.a_rows)
    for p in range(NZ * NY):
        j = (96 * p) // 128
        for img in range(2):
            for t in range(2):
                if j + t < 24:
                    at = 4 * (p // NZ) + 2 * img + t
                    r.a_rows[p % NZ, at : at + 1, :] = wide[img : img + 1, (j + t) * 128 : (j + t + 1) * 128]
    r.a_src[...] = r.a_rows[...].astype(BF16)
    r.a_z[z] = r.a_src[z]
    r.m_plane[...] = jnp.zeros_like(r.m_plane)
    perm = sorting(c0, c1, rows)
    raw_tok.wait()
    r.tok_all[s] = nn(perm, r.tok_raw[...]).astype(BF16)

    enter(me)

    batches = []

    def send(batch):
        batches.append(batch)
        return batch

    def row_chunk(i):
        return pl.ds(i * chunk, chunk)

    def token_copy(source, owner, i, slot, there):
        return remote(source, r.tok_all.at[owner, row_chunk(i)], r.tk_s.at[0], r.tk_r.at[slot], there)

    def own_tokens(img):
        i = 2 * img
        token_copy(r.tok_all.at[s, row_chunk(i)], s, i, i, right).start()
        token_copy(r.tok_all.at[s, row_chunk(i + 1)], s, i + 1, 4 + i + 1, left).start()
        token_copy(r.tok_all.at[s, row_chunk(i + 1)], s, i + 1, i + 1, right).start()
        token_copy(r.tok_all.at[s, row_chunk(i)], s, i, 4 + i, left).start()

    def forward(img):
        i = 2 * img
        token_copy(r.tok_all.at[s, row_chunk(i)], sl, i, i, right).wait_recv()
        token_copy(r.tok_all.at[sl, row_chunk(i)], sl, i, 8 + i, right).start()
        i = i + 1
        token_copy(r.tok_all.at[s, row_chunk(i)], sr, i, 4 + i, left).wait_recv()
        token_copy(r.tok_all.at[sr, row_chunk(i)], sr, i, 8 + i, left).start()

    def wait_tokens(img):
        i = 2 * img
        own = r.tok_all.at[s, row_chunk(i)]
        token_copy(own, sl, i + 1, i + 1, right).wait_recv()
        token_copy(own, sr, i, 4 + i, left).wait_recv()
        token_copy(own, so, i, 8 + i, right).wait_recv()
        token_copy(own, so, i + 1, 8 + i + 1, left).wait_recv()

    def own_cotangent(img):
        at = pl.ds(img * part, part)
        copies = [
            remote(
                r.cot_own.at[at, aligned(((s + i) % NX) * att, att)], r.cot_all.at[s, at],
                r.ck_s.at[img], r.ck_r.at[img], me.at(dx=i),
            )
            for i in range(1, NX)
        ]
        return send(Batch(me, copies, r.cot_all.at[pl.ds(0, 3), at], r.ck_s.at[img], r.ck_r.at[img]))

    az = send(
        exchange(
            me, "dz", NZ, lambda i: r.a_src.at[(z + i) % NZ], lambda i: r.a_z.at[z], r.a_z.at[pl.ds(0, 7)],
            r.az_s, r.az_r,
        )
    )
    weights = RowGather(me, r.w_all, *r.wy, *r.wz)
    weights.start_y()
    others = ColumnGather(me, r.w_all, *r.vz, *r.vy)
    others.step(1)
    swap = CoreSwap(me, r.w_all, *r.wc)
    own_tokens(0)
    raw_cot.wait()
    r.cot_own[...] = nn(perm, r.cot_raw[...]).astype(BF16)
    az.arrived()
    turned = r.a_z[...].astype(F32)
    for at_y in range(NY):
        for at_z in range(NZ):
            r.a_turn[at_y, 4 * at_z : 4 * at_z + 4, :] = turned[at_z, 4 * at_y : 4 * at_y + 4]
    r.a_low[...] = r.a_turn[...].astype(BF16)
    r.a_y[NY * c + y] = r.a_low[y]

    def plane_exchange(source, target, sample, send_sem, recv_sem):
        copies = []
        for i in range(1, 2 * NY):
            dy, flip = i // 2, i % 2 == 1
            there = (y + dy) % NY
            at = (1 - c) if flip else c
            copies.append(
                remote(source(at, there), target(i - 1), send_sem.at[0], recv_sem.at[0], me.at(dy=dy, flip=flip))
            )
        return send(Batch(me, copies, sample, send_sem.at[0], recv_sem.at[0]))

    ay = plane_exchange(
        lambda at, there: r.a_low.at[there], lambda i: r.a_y.at[NY * c + y], r.a_y.at[pl.ds(0, 7)], r.ay_s, r.ay_r
    )
    weights.first.arrived()
    weights.step(1)
    others.step(2)
    ay.arrived()
    locals_[0].wait()
    r.a_wide[...] = r.a_y[...].reshape(256, 128).astype(F32)
    for img in range(2):
        for t in range(2):
            r.a_pair[img * 64 : (img + 1) * 64, t * 128 : (t + 1) * 128] = r.a_wide[
                pl.ds(2 * img + t, 64, stride=4), :
            ].astype(BF16)
    for j in range(6):
        columns = nn(r.a_pair[...], r.mm[:, j * 128 : (j + 1) * 128])
        for img in range(2):
            r.part_wide[pl.ds(img * 6 + j, 64, stride=12), :] = columns[img * 64 : (img + 1) * 64]
    r.part_low[...] = r.part_wide[...].astype(BF16).reshape(r.part_low.shape)
    my = plane_exchange(
        lambda at, there: r.part_low.at[at, there], lambda i: r.m_in.at[i], r.m_in, r.my_s, r.my_r
    )
    forward(0)
    cot0 = own_cotangent(0)
    own_tokens(1)
    others.step(3)
    row = lax.broadcasted_iota(jnp.int32, (256, 128), 0)
    col = lax.broadcasted_iota(jnp.int32, (256, 128), 1)
    pick = jnp.where((row == col + offset) & (col < 48), 1.0, 0.0).astype(BF16)
    a_own[...] = nn(r.a_pair[...], pick).astype(BF16)
    weights.step(2)
    r.cot_all[s] = r.cot_own[:, aligned(s * att, att)]
    my.arrived()
    total = r.part_low[c, y].astype(F32)
    for i in range(7):
        total += r.m_in[i].astype(F32)
    for at_z in range(NZ):
        r.m_plane[at_z, 0:12, :] = total[12 * at_z : 12 * at_z + 12]
    mz = send(
        exchange(
            me, "dz", NZ, lambda i: r.m_plane.at[(z + i) % NZ], lambda i: r.m_z.at[i - 1], r.m_z, r.mz_s, r.mz_r
        )
    )
    def place(shift):
        swap.wait(shift)
        at_z = (z + shift) % NZ

        @pl.loop(0, NY)
        def _(at_y):
            first = r.w_all[0, at_z, at_y].astype(F32)
            other = r.w_all[1, at_z, at_y].astype(F32)
            at = pl.ds(pl.multiple_of(48 * (NZ * at_y + at_z), 16), 48)
            for t in range(9):
                both = jnp.concatenate([first[24 * t : 24 * t + 24], other[24 * t : 24 * t + 24]], axis=0)
                r.w[at, t * 128 : (t + 1) * 128] = both.astype(BF16)

    others.step(4)
    weights.step(3)
    for shift in (0, 1, NZ - 1):
        others.wait_spread(shift)
        swap.start(shift)
    mz.arrived()
    total = r.m_plane[z]
    for i in range(NZ - 1):
        total += r.m_z[i]
    r.m_own[...] = total
    r.m_all[s] = total
    mx = send(
        exchange(
            me, "dx", NX, lambda i: r.m_own, lambda i: r.m_all.at[s], r.m_all.at[pl.ds(0, 3)], r.mx_s, r.mx_r
        )
    )
    others.step(5)
    weights.step(4)
    for shift in (2, NZ - 2):
        others.wait_spread(shift)
        swap.start(shift)
    for shift in (0, 1, NZ - 1):
        place(shift)

    mx.arrived()
    mod[...] = jnp.zeros_like(mod)
    for k in range(NX):
        for img in range(2):
            for j in range(6):
                at = 768 * k + 128 * j
                mod[img : img + 1, at : at + 128] = r.m_all[k, img * 6 + j : img * 6 + j + 1, :]

    def normalize(img):
        @pl.loop(0, NX)
        def _(block):
            x = r.tok_all[block, img * part : (img + 1) * part, :].astype(F32)
            mean = jnp.mean(x, axis=1, keepdims=True)
            centred = x - mean
            inverse = lax.rsqrt(jnp.mean(centred * centred, axis=1, keepdims=True) + EPSILON)
            rank = lax.broadcasted_iota(jnp.int32, (part, 1), 0)
            gain = 1.0 + mod[img : img + 1, width:]
            value = gain * (centred * inverse) + mod[img : img + 1, :width]
            at = pl.ds(pl.multiple_of(img * image_rows + block * part, 32), part)
            r.modded[at, :] = jnp.where(rank < (c0, c1)[img], value, 0.0).astype(BF16)
            r.stats[at, 0:1] = mean
            r.stats[at, 1:2] = inverse

    weights.step(5)
    for shift in (3, 5, 4):
        others.wait_spread(shift)
        swap.start(shift)
    wait_tokens(0)
    normalize(0)
    forward(1)
    cot1 = own_cotangent(1)
    for shift in (2, NZ - 2, 3, 5, 4):
        place(shift)
    for copy in locals_[1:]:
        copy.wait()

    def project(img):
        at = slice(img * image_rows, (img + 1) * image_rows)
        r.low[at, :] = nt(r.modded[at, :], r.down[...]).astype(BF16)

        @pl.loop(0, 3)
        def _(n):
            cols = aligned(n * att, att)
            r.proj[at, cols] = (nn(r.modded[at, :], r.w[:, cols]) + nn(r.low[at, :], r.up[:, cols])).astype(BF16)

    lane = lax.broadcasted_iota(jnp.int32, (1, image_rows), 1)
    for _ in range(NX - 1):
        lane = jnp.where(lane >= part, lane - part, lane)

    def attend(img):
        at = slice(img * image_rows, (img + 1) * image_rows)
        allowed = lane < (c0, c1)[img]
        for h in range(heads):
            cols = slice(h * 128, (h + 1) * 128)
            key_cols = slice(att + h * 128, att + (h + 1) * 128)
            value_cols = slice(2 * att + h * 128, 2 * att + (h + 1) * 128)
            q, k, v = r.proj[at, cols], r.proj[at, key_cols], r.proj[at, value_cols]
            scores = jnp.where(allowed, nt(q, k), MASKED)
            largest = jnp.max(scores, axis=1, keepdims=True)
            raw = jnp.exp((scores - largest) * scale)
            probs = raw * (1.0 / jnp.sum(raw, axis=1, keepdims=True))
            probs_low = probs.astype(BF16)
            out = nn(probs_low, v).astype(BF16)
            r.attn[:, img, :, cols] = out.reshape(NX, part, 128)
            out_grad = r.cot_all[:, img * part : (img + 1) * part, cols].reshape(image_rows, 128)
            delta = jnp.sum(out_grad.astype(F32) * out.astype(F32), axis=1, keepdims=True)
            score_grads = (probs * (nt(out_grad, v) - delta)).astype(BF16)
            r.proj_grad[at, cols] = (nn(score_grads, k) * scale).astype(BF16)
            r.proj_grad[at, key_cols] = (tn(q, score_grads) * scale).T.astype(BF16)
            r.proj_grad[at, value_cols] = tn(out_grad, probs_low).T.astype(BF16)

    mine = aligned(s * att, att)

    def give(img):
        at = slice(img * part, (img + 1) * part)
        copies = [
            remote(
                r.attn.at[(s + i) % NX, img], attn_out.at[at, mine], r.ot_s.at[img], r.ot_r.at[img], me.at(dx=i)
            )
            for i in range(1, NX)
        ]
        attn_out[at, mine] = r.attn[s, img]
        return send(Batch(me, copies, attn_out.at[at, pl.ds(0, 3 * att)], r.ot_s.at[img], r.ot_r.at[img]))

    def low_grads(img):
        at = slice(img * image_rows, (img + 1) * image_rows)
        r.low_grad[at, :] = nt(r.proj_grad[at, :], r.up[...]).astype(BF16)

    def grads(img):
        at = slice(img * image_rows, (img + 1) * image_rows)

        @pl.loop(0, width // att)
        def _(n):
            f = aligned(n * att, att)
            grad = nt(r.proj_grad[at, :], r.w[f, :]) + nn(r.low_grad[at, :], r.down[:, f])
            r.pg[img, :, :, f] = grad.astype(BF16).reshape(NX, part, att)
            x = r.tok_all[:, img * part : (img + 1) * part, f].reshape(image_rows, att).astype(F32)
            normed = (x - r.stats[at, 0:1]) * r.stats[at, 1:2]
            r.ip[img : img + 1, f] = jnp.sum(grad, axis=0, keepdims=True)
            r.ip[img : img + 1, aligned(width + n * att, att)] = jnp.sum(grad * normed, axis=0, keepdims=True)

    half = part // 2
    first, second = pl.ds(0, half), pl.ds(half, half)

    def grad_copy(img, slot):
        src, dst, there = (
            (r.pg.at[img, so, first], r.half_l.at[img], right),
            (r.pg.at[img, so, second], r.half_r.at[img], left),
            (r.pg.at[img, sr, second], r.from_l.at[img, second], right),
            (r.pg.at[img, sl, first], r.from_r.at[img, first], left),
            (r.comb_r.at[img], r.from_l.at[img, first], right),
            (r.comb_l.at[img], r.from_r.at[img, second], left),
        )[slot]
        return remote(src, dst, r.gr_s.at[img], r.gr_r.at[6 * img + slot], there)

    def reduce_first(img):
        for slot in range(4):
            grad_copy(img, slot).start()

    def reduce_second(img):
        grad_copy(img, 0).wait_recv()
        r.comb_r[img] = (r.pg[img, sr, 0:half].astype(F32) + r.half_l[img].astype(F32)).astype(BF16)
        grad_copy(img, 4).start()
        grad_copy(img, 1).wait_recv()
        r.comb_l[img] = (r.pg[img, sl, half:part].astype(F32) + r.half_r[img].astype(F32)).astype(BF16)
        grad_copy(img, 5).start()

    project(0)
    cot0.arrived()
    attend(0)
    out0 = give(0)
    low_grads(0)
    grads(0)
    reduce_first(0)
    wait_tokens(1)
    normalize(1)
    project(1)
    cot1.arrived()
    attend(1)
    out1 = give(1)
    reduce_second(0)
    low_grads(1)

    r.lo[NX - 1 - s, 0] = jnp.zeros((192, 128), BF16)
    up_total = tn(r.low[...], r.proj_grad[...]).astype(BF16)
    for t in range(9):
        r.lo[(4 * (t // 3) + s) // 3, 0, (t % 3) * 64 : (t % 3 + 1) * 64, :] = up_total[:, t * 128 : (t + 1) * 128]
    down_total = tn(r.low_grad[...], r.modded[...]).astype(BF16)
    for t in range(12):
        r.lo[t // 3, 1, (t % 3) * 64 : (t % 3 + 1) * 64, :] = down_total[:, t * 128 : (t + 1) * 128]
    ly = send(
        exchange(me, "dy", NY, lambda i: r.lo.at[(y + i) % NY], lambda i: r.l_y.at[i - 1], r.l_y, r.ly_s, r.ly_r)
    )

    grads(1)
    reduce_first(1)
    for img in range(2):
        for j in range(24):
            at = img * 24 + j
            r.ip_own[at : at + 1, :] = r.ip[img : img + 1, j * 128 : (j + 1) * 128]
    ip = send(exchange(me, "dx", NX, lambda i: r.ip_own, lambda i: r.ip_in.at[i - 1], r.ip_in, r.ip_s, r.ip_r))

    ly.arrived()
    total = r.lo[y].astype(F32)
    for i in range(NY - 1):
        total += r.l_y[i].astype(F32)
    for i in range(NZ):
        at = slice(24 * i, 24 * i + 24)
        r.l_plane[i] = jnp.concatenate([total[0, at], total[1, at]], axis=0).astype(BF16)
    lz = send(
        exchange(
            me, "dz", NZ, lambda i: r.l_plane.at[(z + i) % NZ], lambda i: r.l_z.at[i - 1], r.l_z, r.lz_s, r.lz_r
        )
    )

    ip.arrived()
    ig_all[c, y, z] = (r.ip_own[...] + r.ip_in[0] + r.ip_in[1] + r.ip_in[2]).astype(BF16)
    own_ig = ig_all.at[c, y, z]
    iz = send(
        exchange(me, "dz", NZ, lambda i: own_ig, lambda i: own_ig, ig_all.at[c, y, pl.ds(0, 7)], r.iz_s, r.iz_r)
    )

    lz.arrived()
    total = r.l_plane[z].astype(F32)
    for i in range(NZ - 1):
        total += r.l_z[i].astype(F32)
    r.l_piece[...] = total.astype(BF16)
    r.l_x[NX * c + s] = r.l_piece[...]
    copies = [
        remote(
            r.l_piece, r.l_x.at[NX * c + s], r.lx_s.at[0], r.lx_r.at[0], me.at(dx=i // 2, flip=i % 2 == 1)
        )
        for i in range(1, 2 * NX)
    ]
    lx = send(Batch(me, copies, r.l_x.at[pl.ds(0, 7)], r.lx_s.at[0], r.lx_r.at[0]))

    iz.arrived()
    column = ig_all.at[c, y]
    iy = send(
        exchange(me, "dy", NY, lambda i: column, lambda i: column, ig_all.at[c, pl.ds(0, 3)], r.iy_s, r.iy_r)
    )
    reduce_second(1)

    lx.arrived()
    sums = [r.l_x[i].astype(F32) + r.l_x[NX + i].astype(F32) for i in range(NX)]
    pieces = []
    for i in range(3):
        k = (3 * y + i) % 4
        pieces.append((r.l_x[k].astype(F32) + r.l_x[NX + k].astype(F32))[0:24])
    pieces.append((sums[0] + sums[1] + sums[2] + sums[3])[24:48])
    f_all[z] = jnp.concatenate(pieces, axis=0).astype(BF16)
    lg = send(
        exchange(
            me, "dz", NZ, lambda i: f_all.at[z], lambda i: f_all.at[z], f_all.at[pl.ds(0, 7)], r.lg_s, r.lg_r
        )
    )

    iy.arrived()
    whole_core = ig_all.at[c]
    ic = send(
        Batch(
            me, [remote(whole_core, whole_core, r.ic_s.at[0], r.ic_r.at[0], me.at(flip=True))], whole_core,
            r.ic_s.at[0], r.ic_r.at[0],
        )
    )
    for img in range(2):
        for slot in range(2, 6):
            grad_copy(img, slot).wait_recv()
        grad_out[img * part : (img + 1) * part, :] = (
            r.pg[img, s].astype(F32) + r.from_l[img].astype(F32) + r.from_r[img].astype(F32)
        ).astype(BF16)
    ic.arrived()
    lg.arrived()
    out0.arrived()
    out1.arrived()

    for batch in batches:
        batch.left()
    tokens_sent = r.tok_all.at[pl.ds(0, 3)]
    remote(tokens_sent, tokens_sent, r.tk_s.at[0], r.tk_r.at[0], right).wait_send()
    for img in range(2):
        grads_sent = r.pg.at[img, pl.ds(0, 3)]
        remote(grads_sent, grads_sent, r.gr_s.at[img], r.gr_r.at[0], right).wait_send()
    weights.left()
    others.left()
    swap.left()


def whole(counts, tok, cot, cond, wq, up, down, mm):
    return pl.pallas_call(
        whole_kernel,
        out_shape=(
            jax.ShapeDtypeStruct((192, 1536), BF16),
            jax.ShapeDtypeStruct((192, 1536), BF16),
            jax.ShapeDtypeStruct((8, 3072), F32),
            jax.ShapeDtypeStruct((128, 128), BF16),
            jax.ShapeDtypeStruct((NC, NY, NZ, 48, 128), BF16),
            jax.ShapeDtypeStruct((NZ, 96, 128), BF16),
        ),
        in_specs=[pl.BlockSpec(memory_space=pltpu.SMEM), ANY, ANY, VM, VM, ANY, ANY, ANY],
        out_specs=(VM, VM, VM, VM, VM, VM),
        scratch_shapes=scratch_list(),
        compiler_params=pltpu.CompilerParams(
            collective_id=1, has_side_effects=True, vmem_limit_bytes=60 * 1024 * 1024
        ),
        name="whole",
    )(counts, tok, cot, cond, wq, up, down, mm)


def tail_kernel(
    counts, attn, grad, tok, mod, act, ig, pieces,
    attn_out, token_grad, down_out, up_out, mod_grad,
    ig_wide, sorted_grad,
):
    rows, width = tok.shape
    part = rows // 2
    dp = lax.axis_index("dp")
    perm = sorting(counts[0, dp], counts[1, dp], rows)
    attn_out[...] = tn(perm, attn[...]).astype(BF16)
    for img in range(2):
        at = slice(img * part, (img + 1) * part)
        x = nn(perm[at], tok[...])
        centred = x - jnp.mean(x, axis=1, keepdims=True)
        inverse = lax.rsqrt(jnp.mean(centred * centred, axis=1, keepdims=True) + EPSILON)
        normed = centred * inverse
        g = (1.0 + mod[img : img + 1, width:]) * grad[at, :].astype(F32)
        sorted_grad[at, :] = (
            inverse
            * (g - jnp.mean(g, axis=1, keepdims=True) - normed * jnp.mean(g * normed, axis=1, keepdims=True))
        ).astype(BF16)
    token_grad[...] = tn(perm, sorted_grad[...]).astype(BF16)

    ig_wide[...] = ig[...].reshape(3072, 128).astype(F32)
    for j in range(24):
        total = jnp.zeros((128, 128), F32)
        for img in range(2):
            part = ig_wide[pl.ds(img * 24 + j, 64, stride=48), :].astype(BF16)
            total += tn(act[img * 64 : (img + 1) * 64], part)
        mod_grad[:, j * 128 : (j + 1) * 128] = total[0:48]

    place = dp % (NZ * NC)
    flat = pieces[...].astype(F32)

    def tiles(i):
        triple = jnp.concatenate([flat[k, 24 * i : 24 * i + 24] for k in range(NZ)], axis=0).astype(BF16)
        return [triple[j * 64 : (j + 1) * 64] for j in range(3)]

    row = lax.broadcasted_iota(jnp.int32, (128, 128), 0)
    col = lax.broadcasted_iota(jnp.int32, (128, 128), 1)
    total = jnp.zeros((64, 128), F32)
    for i, tile in enumerate(tiles(0) + tiles(1) + tiles(2)):
        total += nn(tile, jnp.where(row + 128 * i == col + 72 * place, 1.0, 0.0).astype(BF16))
    up_out[...] = total[:, :72]
    total = jnp.zeros((128, 64), F32)
    for i, tile in enumerate(tiles(3)):
        total += nt(jnp.where(col + 128 * i == row + 24 * place, 1.0, 0.0).astype(BF16), tile)
    down_out[...] = total[:24]


def tail(counts, attn, grad, tok, mod, act, ig, pieces):
    return pl.pallas_call(
        tail_kernel,
        out_shape=(
            jax.ShapeDtypeStruct((192, 1536), BF16),
            jax.ShapeDtypeStruct((192, 1536), BF16),
            jax.ShapeDtypeStruct((24, 64), F32),
            jax.ShapeDtypeStruct((64, 72), F32),
            jax.ShapeDtypeStruct((48, 3072), F32),
        ),
        in_specs=[pl.BlockSpec(memory_space=pltpu.SMEM)] + [VM] * 7,
        out_specs=(VM, VM, VM, VM, VM),
        scratch_shapes=[pltpu.VMEM((3072, 128), F32), pltpu.VMEM((192, 1536), BF16)],
        compiler_params=pltpu.CompilerParams(vmem_limit_bytes=60 * 1024 * 1024),
        name="tail",
    )(counts, attn, grad, tok, mod, act, ig, pieces)


def body(
    tokens,
    cotangent,
    condition,
    per_image_rows,
    query_key_value_weight,
    adapter_down,
    adapter_up,
    modulation_matrix,
):
    counts = per_image_rows.T
    attn, grad, mod, act, ig, pieces = whole(
        counts,
        tokens[0],
        cotangent[0],
        condition[0],
        query_key_value_weight,
        adapter_up,
        adapter_down.T,
        modulation_matrix,
    )
    attention, token_grad, down_grad, up_grad, mod_grad = tail(
        counts, attn, grad, tokens[0], mod, act, ig, pieces
    )
    return attention[None], token_grad[None], down_grad, up_grad, mod_grad


def solution(mesh):
    in_specs = (
        P("dp", "seq", None),
        P("dp", "seq", None),
        P("dp", None, None),
        P(),
        P("dp", None),
        P(),
        P(),
        P("dp", None),
    )
    out_specs = (
        P("dp", "seq", None),
        P("dp", "seq", None),
        P("dp", None),
        P(None, "dp"),
        P("dp", None),
    )
    return jax.shard_map(body, mesh=mesh, in_specs=in_specs, out_specs=out_specs, check_vma=False)
```

```python
import jax
import jax.numpy as jnp
from jax import lax
from jax.experimental import pallas as pl
from jax.experimental.pallas import tpu as pltpu
from jax.sharding import PartitionSpec as P

HEAD_SIZE = 128
EPSILON = 1e-06
MASKED = -1e30
MESH = pl.DeviceIdType.MESH
NX, NY, NZ, NC = 4, 4, 8, 2
F32, BF16 = jnp.float32, jnp.bfloat16
ANY = pl.BlockSpec(memory_space=pl.ANY)
VM = pl.BlockSpec(memory_space=pltpu.VMEM)


def remote(src, dst, send_sem, recv_sem, device):
    return pltpu.make_async_remote_copy(
        src_ref=src,
        dst_ref=dst,
        send_sem=send_sem,
        recv_sem=recv_sem,
        device_id=device,
        device_id_type=MESH,
    )


class Place:
    def __init__(self):
        self.dp = lax.axis_index("dp")
        self.s = lax.axis_index("seq")
        self.y = self.dp // (NZ * NC)
        self.z = (self.dp // NC) % NZ
        self.c = self.dp % NC

    def at(self, dx=0, dy=0, dz=0, flip=False):
        s = (self.s + dx) % NX if dx else self.s
        y = (self.y + dy) % NY if dy else self.y
        z = (self.z + dz) % NZ if dz else self.z
        c = 1 - self.c if flip else self.c
        return (y * (NZ * NC) + z * NC + c, s)


def peers_of(me):
    peers = [me.at(dx=i) for i in range(1, NX)]
    peers += [me.at(dx=i, flip=True) for i in range(1, NX)]
    peers += [me.at(dy=i) for i in range(1, NY)]
    peers += [me.at(dz=i) for i in range(1, NZ)]
    peers += [me.at(dy=i, flip=True) for i in range(NY)]
    return peers


def greet(me):
    for peer in peers_of(me):
        pl.semaphore_signal(pltpu.get_barrier_semaphore(), inc=1, device_id=peer, device_id_type=MESH)


def enter(me):
    pl.semaphore_wait(pltpu.get_barrier_semaphore(), len(peers_of(me)))


SPLIT = 128


class Batch:
    def __init__(self, me, copies, sample, send, recv):
        self.all = remote(sample, sample, send, recv, me.at(dx=1))
        for copy in copies:
            copy.start()

    def arrived(self):
        self.all.wait_recv()

    def left(self):
        self.all.wait_send()


class RowGather:
    def __init__(self, me, buf, ysend, yrecv, zsend, zrecv):
        self.me, self.buf = me, buf
        self.ysend, self.yrecv = ysend.at[0], yrecv.at[0]
        self.zsend, self.zrecv = zsend.at[0], zrecv

    def start_y(self):
        me = self.me
        own = self.buf.at[me.c, 3, me.y, pl.ds(0, SPLIT)]
        copies = [remote(own, own, self.ysend, self.yrecv, me.at(dy=i)) for i in range(1, NY)]
        sample = self.buf.at[me.c, 3, pl.ds(0, 3), pl.ds(0, SPLIT)]
        self.first = Batch(me, copies, sample, self.ysend, self.yrecv)

    def ring(self, way, step):
        me = self.me
        here, there = (4 - step, 3 - step) if way == 0 else (2 + step, 3 + step)
        ys = pl.ds(0, NY) if step < 4 else pl.ds(2 * way, 2)
        source = self.buf.at[me.c, here, ys, pl.ds(0, SPLIT)]
        target = self.buf.at[me.c, there % NZ, ys, pl.ds(0, SPLIT)]
        device = me.at(dz=1) if way == 0 else me.at(dz=NZ - 1)
        return remote(source, target, self.zsend, self.zrecv.at[way * 4 + step - 1], device)

    def step(self, step):
        for way in (0, 1):
            if step > 1:
                self.ring(way, step - 1).wait_recv()
            if step <= 4:
                self.ring(way, step).start()

    def left(self):
        me = self.me
        self.first.left()
        sample = self.buf.at[me.c, pl.ds(0, 7), pl.ds(0, NY), pl.ds(0, SPLIT)]
        remote(sample, sample, self.zsend, self.zrecv.at[0], me.at(dz=1)).wait_send()


def rest_over_z(me, buf, send, recv):
    rows = pl.ds(SPLIT, buf.shape[3] - SPLIT)
    source = buf.at[me.c, 3, me.y, rows]
    copies = [
        remote(source, buf.at[me.c, (3 - i) % NZ, me.y, rows], send.at[0], recv.at[0], me.at(dz=i))
        for i in range(1, NZ)
    ]
    return Batch(me, copies, buf.at[me.c, pl.ds(0, 7), me.y, rows], send.at[0], recv.at[0])


def rest_over_y(me, buf, send, recv):
    rows = pl.ds(SPLIT, buf.shape[3] - SPLIT)
    block = buf.at[me.c, pl.ds(0, NZ), me.y, rows]
    copies = [remote(block, block, send.at[0], recv.at[0], me.at(dy=i)) for i in range(1, NY)]
    return Batch(me, copies, buf.at[me.c, pl.ds(0, NZ), pl.ds(0, 3), rows], send.at[0], recv.at[0])


def swap(me, buf, first, count, rows, send, recv):
    block = buf.at[me.c, pl.ds(first, count), pl.ds(0, NY), rows]
    return Batch(me, [remote(block, block, send, recv, me.at(flip=True))], block, send, recv)


def exchange(me, axis, count, source, target, sample, send, recv):
    copies = [
        remote(source(i), target(i), send.at[0], recv.at[0], me.at(**{axis: i})) for i in range(1, count)
    ]
    return Batch(me, copies, sample, send.at[0], recv.at[0])

def nt(a, b):
    return lax.dot_general(a, b, (((1,), (1,)), ((), ())), preferred_element_type=F32)


def tn(a, b):
    return lax.dot_general(a, b, (((0,), (0,)), ((), ())), preferred_element_type=F32)


def nn(a, b):
    return jnp.dot(a, b, preferred_element_type=F32)


def sorting(c0, c1, rows):
    here = lax.broadcasted_iota(jnp.int32, (rows, rows), 0)
    source = lax.broadcasted_iota(jnp.int32, (rows, rows), 1)
    later = here >= rows // 2
    rank = jnp.where(later, here - rows // 2, here)
    live = rank < jnp.where(later, c1, c0)
    return jnp.where((source == rank + jnp.where(later, c0, 0)) & live, 1.0, 0.0).astype(BF16)


def aligned(start, size):
    return pl.ds(pl.multiple_of(start, 128), size)


class Refs:
    pass


SCRATCH = dict(
    tok_raw=pltpu.VMEM((192, 1536), BF16),
    cot_raw=pltpu.VMEM((192, 1536), BF16),
    tok_all=pltpu.VMEM((NX, 192, 1536), BF16),
    cot_all=pltpu.VMEM((NX, 192, 384), BF16),
    w_all=pltpu.VMEM((NC, NZ, NY, 224, 128), BF16),
    w=pltpu.VMEM((1536, 1152), BF16),
    up=pltpu.VMEM((64, 1152), BF16),
    down=pltpu.VMEM((64, 1536), BF16),
    mm=pltpu.VMEM((256, 768), BF16),
    a_rows=pltpu.VMEM((NZ, 16, 128), F32),
    a_src=pltpu.VMEM((NZ, 16, 128), BF16),
    a_z=pltpu.VMEM((NZ, 16, 128), BF16),
    a_turn=pltpu.VMEM((NY, 32, 128), F32),
    a_low=pltpu.VMEM((NY, 32, 128), BF16),
    a_y=pltpu.VMEM((NC * NY, 32, 128), BF16),
    a_wide=pltpu.VMEM((256, 128), F32),
    a_pair=pltpu.VMEM((128, 256), BF16),
    part_wide=pltpu.VMEM((768, 128), F32),
    part_low=pltpu.VMEM((NC, NY, 96, 128), BF16),
    m_in=pltpu.VMEM((7, 96, 128), BF16),
    m_plane=pltpu.VMEM((NZ, 16, 128), F32),
    m_z=pltpu.VMEM((NZ - 1, 16, 128), F32),
    m_own=pltpu.VMEM((16, 128), F32),
    m_all=pltpu.VMEM((NX, 16, 128), F32),
    modded=pltpu.VMEM((768, 1536), BF16),
    stats=pltpu.VMEM((768, 128), F32),
    low=pltpu.VMEM((768, 64), BF16),
    proj=pltpu.VMEM((768, 1152), BF16),
    proj_grad=pltpu.VMEM((768, 1152), BF16),
    low_grad=pltpu.VMEM((768, 64), BF16),
    cot_own=pltpu.VMEM((192, 1536), BF16),
    attn=pltpu.VMEM((NX, 2, 96, 384), BF16),
    pg=pltpu.VMEM((2, NX, 96, 1536), BF16),
    ip=pltpu.VMEM((8, 3072), F32),
    half_l=pltpu.VMEM((2, 48, 1536), BF16),
    half_r=pltpu.VMEM((2, 48, 1536), BF16),
    comb_l=pltpu.VMEM((2, 48, 1536), BF16),
    comb_r=pltpu.VMEM((2, 48, 1536), BF16),
    from_l=pltpu.VMEM((2, 96, 1536), BF16),
    from_r=pltpu.VMEM((2, 96, 1536), BF16),
    ip_own=pltpu.VMEM((48, 128), F32),
    ip_in=pltpu.VMEM((3, 48, 128), F32),
    lo=pltpu.VMEM((NY, 2, 192, 128), BF16),
    l_y=pltpu.VMEM((NY - 1, 2, 192, 128), BF16),
    l_plane=pltpu.VMEM((NZ, 48, 128), BF16),
    l_z=pltpu.VMEM((NZ - 1, 48, 128), BF16),
    l_piece=pltpu.VMEM((48, 128), BF16),
    l_x=pltpu.VMEM((NC * NX, 48, 128), BF16),
)
PAIRS = dict(
    tk=(1, 8), ck=(2, 2), az=(1, 1), ay=(1, 1), my=(1, 1), mz=(1, 1), mx=(1, 1), gr=(2, 12), ot=(2, 2),
    ip=(1, 1), iz=(1, 1), iy=(1, 1), ic=(1, 1), ly=(1, 1), lz=(1, 1), lx=(1, 1), lg=(1, 1),
)
PLANES = dict(wy=(1, 1), wz=(1, 8), vz=(1, 1), vy=(1, 1), wc=(4, 4))
LOCAL = 8


def scratch_list():
    dma = pltpu.SemaphoreType.DMA
    out = list(SCRATCH.values())
    for send, recv in list(PAIRS.values()) + list(PLANES.values()):
        out += [dma((send,)), dma((recv,))]
    return out + [dma((LOCAL,))]


def named(refs):
    r = Refs()
    refs = list(refs)
    for name in SCRATCH:
        setattr(r, name, refs.pop(0))
    for name in PAIRS:
        setattr(r, name + "_s", refs.pop(0))
        setattr(r, name + "_r", refs.pop(0))
    for name in PLANES:
        setattr(r, name, [refs.pop(0), refs.pop(0)])
    r.local = refs.pop(0)
    return r


def whole_kernel(
    rows_ref, tok, cot, cond, wq, up_in, down_in, mm_in,
    attn_out, grad_out, mod, a_own, ig_all, f_all,
    *refs,
):
    r = named(refs)
    me = Place()
    s, y, z, c = me.s, me.y, me.z, me.c
    rows, width, att, heads = 192, 1536, 384, 3
    part = rows // 2
    image_rows = NX * part
    chunk = rows // 4
    scale = HEAD_SIZE ** (-0.5)
    right, left = me.at(dx=1), me.at(dx=NX - 1)
    sl, sr, so = (s + NX - 1) % NX, (s + 1) % NX, (s + 2) % NX
    c0, c1 = rows_ref[0, me.dp], rows_ref[1, me.dp]

    greet(me)
    offset = 48 * me.dp - 128 * ((96 * (me.dp // 2)) // 128)
    r.mm[...] = jnp.zeros_like(r.mm)
    raw_tok = pltpu.make_async_copy(tok, r.tok_raw, r.local.at[5])
    raw_tok.start()
    raw_cot = pltpu.make_async_copy(cot, r.cot_raw, r.local.at[6])
    raw_cot.start()
    locals_ = [
        pltpu.make_async_copy(
            mm_in.at[:, aligned(s * 768, 768)], r.mm.at[pl.ds(pl.multiple_of(offset, 16), 48)], r.local.at[0]
        ),
        pltpu.make_async_copy(down_in, r.down, r.local.at[1]),
    ]
    for b in range(3):
        locals_.append(
            pltpu.make_async_copy(
                up_in.at[:, aligned(b * width + s * att, att)], r.up.at[:, b * att : (b + 1) * att], r.local.at[2 + b]
            )
        )
    for copy in locals_:
        copy.start()
    pieces = []
    for b in range(3):
        block = wq[:, aligned(b * width + s * att, att)].astype(F32)
        pieces += [block[:, i * 128 : (i + 1) * 128] for i in range(3)]
    pieces.append(jnp.zeros((8, 128), F32))
    r.w_all[c, 3, y] = jnp.concatenate(pieces, axis=0).astype(BF16)
    wide = cond[...].astype(F32)
    wide = (wide / (1.0 + jnp.exp(-wide))).astype(BF16).astype(F32)
    r.a_rows[...] = jnp.zeros_like(r.a_rows)
    for p in range(NZ * NY):
        j = (96 * p) // 128
        for img in range(2):
            for t in range(2):
                if j + t < 24:
                    at = 4 * (p // NZ) + 2 * img + t
                    r.a_rows[p % NZ, at : at + 1, :] = wide[img : img + 1, (j + t) * 128 : (j + t + 1) * 128]
    r.a_src[...] = r.a_rows[...].astype(BF16)
    r.a_z[z] = r.a_src[z]
    r.m_plane[...] = jnp.zeros_like(r.m_plane)
    perm = sorting(c0, c1, rows)
    raw_tok.wait()
    r.tok_all[s] = nn(perm, r.tok_raw[...]).astype(BF16)

    enter(me)

    batches = []

    def send(batch):
        batches.append(batch)
        return batch

    quarter = part // 2

    def token_copy(img, slot):
        start = img * part
        owner, at, there = (
            (s, pl.ds(start, part), right),
            (s, pl.ds(start, part), left),
            (sl, pl.ds(start, quarter), right),
            (sr, pl.ds(start + quarter, quarter), left),
        )[slot]
        block = r.tok_all.at[owner, at]
        return remote(block, block, r.tk_s.at[0], r.tk_r.at[4 * img + slot], there)

    def own_tokens(img):
        token_copy(img, 0).start()
        token_copy(img, 1).start()

    def forward(img):
        for slot in (0, 1):
            token_copy(img, slot).wait_recv()
            token_copy(img, slot + 2).start()

    def wait_tokens(img):
        token_copy(img, 2).wait_recv()
        token_copy(img, 3).wait_recv()

    def own_cotangent(img):
        at = pl.ds(img * part, part)
        copies = [
            remote(
                r.cot_own.at[at, aligned(((s + i) % NX) * att, att)], r.cot_all.at[s, at],
                r.ck_s.at[img], r.ck_r.at[img], me.at(dx=i),
            )
            for i in range(1, NX)
        ]
        return send(Batch(me, copies, r.cot_all.at[pl.ds(0, 3), at], r.ck_s.at[img], r.ck_r.at[img]))

    az = send(
        exchange(
            me, "dz", NZ, lambda i: r.a_src.at[(z + i) % NZ], lambda i: r.a_z.at[z], r.a_z.at[pl.ds(0, 7)],
            r.az_s, r.az_r,
        )
    )
    weights = RowGather(me, r.w_all, *r.wy, *r.wz)
    weights.start_y()
    rest = send(rest_over_z(me, r.w_all, *r.vz))
    own_tokens(0)
    raw_cot.wait()
    r.cot_own[...] = nn(perm, r.cot_raw[...]).astype(BF16)
    az.arrived()
    turned = r.a_z[...].astype(F32)
    for at_y in range(NY):
        for at_z in range(NZ):
            r.a_turn[at_y, 4 * at_z : 4 * at_z + 4, :] = turned[at_z, 4 * at_y : 4 * at_y + 4]
    r.a_low[...] = r.a_turn[...].astype(BF16)
    r.a_y[NY * c + y] = r.a_low[y]

    def plane_exchange(source, target, sample, send_sem, recv_sem):
        copies = []
        for i in range(1, 2 * NY):
            dy, flip = i // 2, i % 2 == 1
            there = (y + dy) % NY
            at = (1 - c) if flip else c
            copies.append(
                remote(source(at, there), target(i - 1), send_sem.at[0], recv_sem.at[0], me.at(dy=dy, flip=flip))
            )
        return send(Batch(me, copies, sample, send_sem.at[0], recv_sem.at[0]))

    ay = plane_exchange(
        lambda at, there: r.a_low.at[there], lambda i: r.a_y.at[NY * c + y], r.a_y.at[pl.ds(0, 7)], r.ay_s, r.ay_r
    )
    weights.first.arrived()
    weights.step(1)
    ay.arrived()
    locals_[0].wait()
    r.a_wide[...] = r.a_y[...].reshape(256, 128).astype(F32)
    for img in range(2):
        for t in range(2):
            r.a_pair[img * 64 : (img + 1) * 64, t * 128 : (t + 1) * 128] = r.a_wide[
                pl.ds(2 * img + t, 64, stride=4), :
            ].astype(BF16)
    for j in range(6):
        columns = nn(r.a_pair[...], r.mm[:, j * 128 : (j + 1) * 128])
        for img in range(2):
            r.part_wide[pl.ds(img * 6 + j, 64, stride=12), :] = columns[img * 64 : (img + 1) * 64]
    r.part_low[...] = r.part_wide[...].astype(BF16).reshape(r.part_low.shape)
    my = plane_exchange(
        lambda at, there: r.part_low.at[at, there], lambda i: r.m_in.at[i], r.m_in, r.my_s, r.my_r
    )
    forward(0)
    cot0 = own_cotangent(0)
    own_tokens(1)
    rest.arrived()
    spread = send(rest_over_y(me, r.w_all, *r.vy))
    row = lax.broadcasted_iota(jnp.int32, (256, 128), 0)
    col = lax.broadcasted_iota(jnp.int32, (256, 128), 1)
    pick = jnp.where((row == col + offset) & (col < 48), 1.0, 0.0).astype(BF16)
    a_own[...] = nn(r.a_pair[...], pick).astype(BF16)
    weights.step(2)
    r.cot_all[s] = r.cot_own[:, aligned(s * att, att)]
    my.arrived()
    total = r.part_low[c, y].astype(F32)
    for i in range(7):
        total += r.m_in[i].astype(F32)
    for at_z in range(NZ):
        r.m_plane[at_z, 0:12, :] = total[12 * at_z : 12 * at_z + 12]
    mz = send(
        exchange(
            me, "dz", NZ, lambda i: r.m_plane.at[(z + i) % NZ], lambda i: r.m_z.at[i - 1], r.m_z, r.mz_s, r.mz_r
        )
    )
    def place(first, count):
        @pl.loop(0, NY * count)
        def _(i):
            at_y, at_d = i // count, first + i % count
            one = r.w_all[0, at_d, at_y].astype(F32)
            other = r.w_all[1, at_d, at_y].astype(F32)
            at_z = (z + at_d + NZ - 3) % NZ
            at = pl.ds(pl.multiple_of(48 * (NZ * at_y + at_z), 16), 48)
            for t in range(9):
                both = jnp.concatenate([one[24 * t : 24 * t + 24], other[24 * t : 24 * t + 24]], axis=0)
                r.w[at, t * 128 : (t + 1) * 128] = both.astype(BF16)

    def swap_part(index, first, count, rows):
        return send(swap(me, r.w_all, first, count, rows, r.wc[0].at[index], r.wc[1].at[index]))

    upper, lower = pl.ds(0, SPLIT), pl.ds(SPLIT, r.w_all.shape[3] - SPLIT)
    weights.step(3)
    near = swap_part(0, 1, 5, upper)
    mz.arrived()
    total = r.m_plane[z]
    for i in range(NZ - 1):
        total += r.m_z[i]
    r.m_own[...] = total
    r.m_all[s] = total
    mx = send(
        exchange(
            me, "dx", NX, lambda i: r.m_own, lambda i: r.m_all.at[s], r.m_all.at[pl.ds(0, 3)], r.mx_s, r.mx_r
        )
    )
    weights.step(4)
    left_end = swap_part(1, 0, 1, upper)
    spread.arrived()
    lower_part = swap_part(3, 0, NZ, lower)
    mx.arrived()
    mod[...] = jnp.zeros_like(mod)
    for k in range(NX):
        for img in range(2):
            for j in range(6):
                at = 768 * k + 128 * j
                mod[img : img + 1, at : at + 128] = r.m_all[k, img * 6 + j : img * 6 + j + 1, :]

    def normalize(img):
        @pl.loop(0, NX)
        def _(block):
            x = r.tok_all[block, img * part : (img + 1) * part, :].astype(F32)
            mean = jnp.mean(x, axis=1, keepdims=True)
            centred = x - mean
            inverse = lax.rsqrt(jnp.mean(centred * centred, axis=1, keepdims=True) + EPSILON)
            rank = lax.broadcasted_iota(jnp.int32, (part, 1), 0)
            gain = 1.0 + mod[img : img + 1, width:]
            value = gain * (centred * inverse) + mod[img : img + 1, :width]
            at = pl.ds(pl.multiple_of(img * image_rows + block * part, 32), part)
            r.modded[at, :] = jnp.where(rank < (c0, c1)[img], value, 0.0).astype(BF16)
            r.stats[at, 0:1] = mean
            r.stats[at, 1:2] = inverse

    weights.step(5)
    right_end = swap_part(2, 6, 2, upper)
    wait_tokens(0)
    normalize(0)
    forward(1)
    cot1 = own_cotangent(1)
    near.arrived()
    lower_part.arrived()
    place(1, 5)
    left_end.arrived()
    right_end.arrived()
    place(0, 1)
    place(6, 2)
    for copy in locals_[1:]:
        copy.wait()

    def project(img):
        at = slice(img * image_rows, (img + 1) * image_rows)
        r.low[at, :] = nt(r.modded[at, :], r.down[...]).astype(BF16)

        @pl.loop(0, 3)
        def _(n):
            cols = aligned(n * att, att)
            r.proj[at, cols] = (nn(r.modded[at, :], r.w[:, cols]) + nn(r.low[at, :], r.up[:, cols])).astype(BF16)

    lane = lax.broadcasted_iota(jnp.int32, (1, image_rows), 1)
    for _ in range(NX - 1):
        lane = jnp.where(lane >= part, lane - part, lane)

    def attend(img):
        at = slice(img * image_rows, (img + 1) * image_rows)
        allowed = lane < (c0, c1)[img]
        for h in range(heads):
            cols = slice(h * 128, (h + 1) * 128)
            key_cols = slice(att + h * 128, att + (h + 1) * 128)
            value_cols = slice(2 * att + h * 128, 2 * att + (h + 1) * 128)
            q, k, v = r.proj[at, cols], r.proj[at, key_cols], r.proj[at, value_cols]
            scores = jnp.where(allowed, nt(q, k), MASKED)
            largest = jnp.max(scores, axis=1, keepdims=True)
            raw = jnp.exp((scores - largest) * scale)
            probs = raw * (1.0 / jnp.sum(raw, axis=1, keepdims=True))
            probs_low = probs.astype(BF16)
            out = nn(probs_low, v).astype(BF16)
            r.attn[:, img, :, cols] = out.reshape(NX, part, 128)
            out_grad = r.cot_all[:, img * part : (img + 1) * part, cols].reshape(image_rows, 128)
            delta = jnp.sum(out_grad.astype(F32) * out.astype(F32), axis=1, keepdims=True)
            score_grads = (probs * (nt(out_grad, v) - delta)).astype(BF16)
            r.proj_grad[at, cols] = (nn(score_grads, k) * scale).astype(BF16)
            r.proj_grad[at, key_cols] = (tn(q, score_grads) * scale).T.astype(BF16)
            r.proj_grad[at, value_cols] = tn(out_grad, probs_low).T.astype(BF16)

    mine = aligned(s * att, att)

    def give(img):
        at = slice(img * part, (img + 1) * part)
        copies = [
            remote(
                r.attn.at[(s + i) % NX, img], attn_out.at[at, mine], r.ot_s.at[img], r.ot_r.at[img], me.at(dx=i)
            )
            for i in range(1, NX)
        ]
        attn_out[at, mine] = r.attn[s, img]
        return send(Batch(me, copies, attn_out.at[at, pl.ds(0, 3 * att)], r.ot_s.at[img], r.ot_r.at[img]))

    def low_grads(img):
        at = slice(img * image_rows, (img + 1) * image_rows)
        r.low_grad[at, :] = nt(r.proj_grad[at, :], r.up[...]).astype(BF16)

    def grads(img):
        at = slice(img * image_rows, (img + 1) * image_rows)

        @pl.loop(0, width // att)
        def _(n):
            f = aligned(n * att, att)
            grad = nt(r.proj_grad[at, :], r.w[f, :]) + nn(r.low_grad[at, :], r.down[:, f])
            r.pg[img, :, :, f] = grad.astype(BF16).reshape(NX, part, att)
            x = r.tok_all[:, img * part : (img + 1) * part, f].reshape(image_rows, att).astype(F32)
            normed = (x - r.stats[at, 0:1]) * r.stats[at, 1:2]
            r.ip[img : img + 1, f] = jnp.sum(grad, axis=0, keepdims=True)
            r.ip[img : img + 1, aligned(width + n * att, att)] = jnp.sum(grad * normed, axis=0, keepdims=True)

    half = part // 2
    first, second = pl.ds(0, half), pl.ds(half, half)

    def grad_copy(img, slot):
        src, dst, there = (
            (r.pg.at[img, so, first], r.half_l.at[img], right),
            (r.pg.at[img, so, second], r.half_r.at[img], left),
            (r.pg.at[img, sr, second], r.from_l.at[img, second], right),
            (r.pg.at[img, sl, first], r.from_r.at[img, first], left),
            (r.comb_r.at[img], r.from_l.at[img, first], right),
            (r.comb_l.at[img], r.from_r.at[img, second], left),
        )[slot]
        return remote(src, dst, r.gr_s.at[img], r.gr_r.at[6 * img + slot], there)

    def reduce_first(img):
        for slot in range(4):
            grad_copy(img, slot).start()

    def reduce_second(img):
        grad_copy(img, 0).wait_recv()
        r.comb_r[img] = (r.pg[img, sr, 0:half].astype(F32) + r.half_l[img].astype(F32)).astype(BF16)
        grad_copy(img, 4).start()
        grad_copy(img, 1).wait_recv()
        r.comb_l[img] = (r.pg[img, sl, half:part].astype(F32) + r.half_r[img].astype(F32)).astype(BF16)
        grad_copy(img, 5).start()

    project(0)
    cot0.arrived()
    attend(0)
    out0 = give(0)
    low_grads(0)
    grads(0)
    reduce_first(0)
    wait_tokens(1)
    normalize(1)
    project(1)
    cot1.arrived()
    attend(1)
    out1 = give(1)
    reduce_second(0)
    low_grads(1)

    r.lo[NX - 1 - s, 0] = jnp.zeros((192, 128), BF16)
    up_total = tn(r.low[...], r.proj_grad[...]).astype(BF16)
    for t in range(9):
        r.lo[(4 * (t // 3) + s) // 3, 0, (t % 3) * 64 : (t % 3 + 1) * 64, :] = up_total[:, t * 128 : (t + 1) * 128]
    down_total = tn(r.low_grad[...], r.modded[...]).astype(BF16)
    for t in range(12):
        r.lo[t // 3, 1, (t % 3) * 64 : (t % 3 + 1) * 64, :] = down_total[:, t * 128 : (t + 1) * 128]
    ly = send(
        exchange(me, "dy", NY, lambda i: r.lo.at[(y + i) % NY], lambda i: r.l_y.at[i - 1], r.l_y, r.ly_s, r.ly_r)
    )

    grads(1)
    reduce_first(1)
    for img in range(2):
        for j in range(24):
            at = img * 24 + j
            r.ip_own[at : at + 1, :] = r.ip[img : img + 1, j * 128 : (j + 1) * 128]
    ip = send(exchange(me, "dx", NX, lambda i: r.ip_own, lambda i: r.ip_in.at[i - 1], r.ip_in, r.ip_s, r.ip_r))

    ly.arrived()
    total = r.lo[y].astype(F32)
    for i in range(NY - 1):
        total += r.l_y[i].astype(F32)
    for i in range(NZ):
        at = slice(24 * i, 24 * i + 24)
        r.l_plane[i] = jnp.concatenate([total[0, at], total[1, at]], axis=0).astype(BF16)
    lz = send(
        exchange(
            me, "dz", NZ, lambda i: r.l_plane.at[(z + i) % NZ], lambda i: r.l_z.at[i - 1], r.l_z, r.lz_s, r.lz_r
        )
    )

    ip.arrived()
    ig_all[c, y, z] = (r.ip_own[...] + r.ip_in[0] + r.ip_in[1] + r.ip_in[2]).astype(BF16)
    own_ig = ig_all.at[c, y, z]
    iz = send(
        exchange(me, "dz", NZ, lambda i: own_ig, lambda i: own_ig, ig_all.at[c, y, pl.ds(0, 7)], r.iz_s, r.iz_r)
    )

    lz.arrived()
    total = r.l_plane[z].astype(F32)
    for i in range(NZ - 1):
        total += r.l_z[i].astype(F32)
    r.l_piece[...] = total.astype(BF16)
    r.l_x[NX * c + s] = r.l_piece[...]
    copies = [
        remote(
            r.l_piece, r.l_x.at[NX * c + s], r.lx_s.at[0], r.lx_r.at[0], me.at(dx=i // 2, flip=i % 2 == 1)
        )
        for i in range(1, 2 * NX)
    ]
    lx = send(Batch(me, copies, r.l_x.at[pl.ds(0, 7)], r.lx_s.at[0], r.lx_r.at[0]))

    iz.arrived()
    column = ig_all.at[c, y]
    iy = send(
        exchange(me, "dy", NY, lambda i: column, lambda i: column, ig_all.at[c, pl.ds(0, 3)], r.iy_s, r.iy_r)
    )
    reduce_second(1)

    lx.arrived()
    sums = [r.l_x[i].astype(F32) + r.l_x[NX + i].astype(F32) for i in range(NX)]
    pieces = []
    for i in range(3):
        k = (3 * y + i) % 4
        pieces.append((r.l_x[k].astype(F32) + r.l_x[NX + k].astype(F32))[0:24])
    pieces.append((sums[0] + sums[1] + sums[2] + sums[3])[24:48])
    f_all[z] = jnp.concatenate(pieces, axis=0).astype(BF16)
    lg = send(
        exchange(
            me, "dz", NZ, lambda i: f_all.at[z], lambda i: f_all.at[z], f_all.at[pl.ds(0, 7)], r.lg_s, r.lg_r
        )
    )

    iy.arrived()
    whole_core = ig_all.at[c]
    ic = send(
        Batch(
            me, [remote(whole_core, whole_core, r.ic_s.at[0], r.ic_r.at[0], me.at(flip=True))], whole_core,
            r.ic_s.at[0], r.ic_r.at[0],
        )
    )
    for img in range(2):
        for slot in range(2, 6):
            grad_copy(img, slot).wait_recv()
        grad_out[img * part : (img + 1) * part, :] = (
            r.pg[img, s].astype(F32) + r.from_l[img].astype(F32) + r.from_r[img].astype(F32)
        ).astype(BF16)
    ic.arrived()
    lg.arrived()
    out0.arrived()
    out1.arrived()

    for batch in batches:
        batch.left()
    tokens_sent = r.tok_all.at[pl.ds(0, 3)]
    remote(tokens_sent, tokens_sent, r.tk_s.at[0], r.tk_r.at[0], right).wait_send()
    for img in range(2):
        grads_sent = r.pg.at[img, pl.ds(0, 3)]
        remote(grads_sent, grads_sent, r.gr_s.at[img], r.gr_r.at[0], right).wait_send()
    weights.left()


def whole(counts, tok, cot, cond, wq, up, down, mm):
    return pl.pallas_call(
        whole_kernel,
        out_shape=(
            jax.ShapeDtypeStruct((192, 1536), BF16),
            jax.ShapeDtypeStruct((192, 1536), BF16),
            jax.ShapeDtypeStruct((8, 3072), F32),
            jax.ShapeDtypeStruct((128, 128), BF16),
            jax.ShapeDtypeStruct((NC, NY, NZ, 48, 128), BF16),
            jax.ShapeDtypeStruct((NZ, 96, 128), BF16),
        ),
        in_specs=[pl.BlockSpec(memory_space=pltpu.SMEM), ANY, ANY, VM, VM, ANY, ANY, ANY],
        out_specs=(VM, VM, VM, VM, VM, VM),
        scratch_shapes=scratch_list(),
        compiler_params=pltpu.CompilerParams(
            collective_id=1, has_side_effects=True, vmem_limit_bytes=60 * 1024 * 1024
        ),
        name="whole",
    )(counts, tok, cot, cond, wq, up, down, mm)


def tail_kernel(
    counts, attn, grad, tok, mod, act, ig, pieces,
    attn_out, token_grad, down_out, up_out, mod_grad,
    ig_wide, sorted_grad,
):
    rows, width = tok.shape
    part = rows // 2
    dp = lax.axis_index("dp")
    perm = sorting(counts[0, dp], counts[1, dp], rows)
    attn_out[...] = tn(perm, attn[...]).astype(BF16)
    for img in range(2):
        at = slice(img * part, (img + 1) * part)
        x = nn(perm[at], tok[...])
        centred = x - jnp.mean(x, axis=1, keepdims=True)
        inverse = lax.rsqrt(jnp.mean(centred * centred, axis=1, keepdims=True) + EPSILON)
        normed = centred * inverse
        g = (1.0 + mod[img : img + 1, width:]) * grad[at, :].astype(F32)
        sorted_grad[at, :] = (
            inverse
            * (g - jnp.mean(g, axis=1, keepdims=True) - normed * jnp.mean(g * normed, axis=1, keepdims=True))
        ).astype(BF16)
    token_grad[...] = tn(perm, sorted_grad[...]).astype(BF16)

    ig_wide[...] = ig[...].reshape(3072, 128).astype(F32)
    turned = act[...].astype(F32).T.astype(BF16)[:48]
    for j in range(24):
        parts = [ig_wide[pl.ds(img * 24 + j, 64, stride=48), :].astype(BF16) for img in range(2)]
        mod_grad[:, j * 128 : (j + 1) * 128] = nn(turned, jnp.concatenate(parts, axis=0))

    place = dp % (NZ * NC)
    flat = pieces[...].astype(F32)

    def tiles(i):
        triple = jnp.concatenate([flat[k, 24 * i : 24 * i + 24] for k in range(NZ)], axis=0).astype(BF16)
        return [triple[j * 64 : (j + 1) * 64] for j in range(3)]

    row = lax.broadcasted_iota(jnp.int32, (128, 128), 0)
    col = lax.broadcasted_iota(jnp.int32, (128, 128), 1)
    total = jnp.zeros((64, 128), F32)
    for i, tile in enumerate(tiles(0) + tiles(1) + tiles(2)):
        total += nn(tile, jnp.where(row + 128 * i == col + 72 * place, 1.0, 0.0).astype(BF16))
    up_out[...] = total[:, :72]
    total = jnp.zeros((128, 64), F32)
    for i, tile in enumerate(tiles(3)):
        total += nt(jnp.where(col + 128 * i == row + 24 * place, 1.0, 0.0).astype(BF16), tile)
    down_out[...] = total[:24]


def tail(counts, attn, grad, tok, mod, act, ig, pieces):
    return pl.pallas_call(
        tail_kernel,
        out_shape=(
            jax.ShapeDtypeStruct((192, 1536), BF16),
            jax.ShapeDtypeStruct((192, 1536), BF16),
            jax.ShapeDtypeStruct((24, 64), F32),
            jax.ShapeDtypeStruct((64, 72), F32),
            jax.ShapeDtypeStruct((48, 3072), F32),
        ),
        in_specs=[pl.BlockSpec(memory_space=pltpu.SMEM)] + [VM] * 7,
        out_specs=(VM, VM, VM, VM, VM),
        scratch_shapes=[pltpu.VMEM((3072, 128), F32), pltpu.VMEM((192, 1536), BF16)],
        compiler_params=pltpu.CompilerParams(vmem_limit_bytes=60 * 1024 * 1024),
        name="tail",
    )(counts, attn, grad, tok, mod, act, ig, pieces)


def body(
    tokens,
    cotangent,
    condition,
    per_image_rows,
    query_key_value_weight,
    adapter_down,
    adapter_up,
    modulation_matrix,
):
    counts = per_image_rows.T
    attn, grad, mod, act, ig, pieces = whole(
        counts,
        tokens[0],
        cotangent[0],
        condition[0],
        query_key_value_weight,
        adapter_up,
        adapter_down.T,
        modulation_matrix,
    )
    attention, token_grad, down_grad, up_grad, mod_grad = tail(
        counts, attn, grad, tokens[0], mod, act, ig, pieces
    )
    return attention[None], token_grad[None], down_grad, up_grad, mod_grad


def solution(mesh):
    in_specs = (
        P("dp", "seq", None),
        P("dp", "seq", None),
        P("dp", None, None),
        P(),
        P("dp", None),
        P(),
        P(),
        P("dp", None),
    )
    out_specs = (
        P("dp", "seq", None),
        P("dp", "seq", None),
        P("dp", None),
        P(None, "dp"),
        P("dp", None),
    )
    return jax.shard_map(body, mesh=mesh, in_specs=in_specs, out_specs=out_specs, check_vma=False)
```

```python
import jax
import jax.numpy as jnp
from jax import lax
from jax.experimental import pallas as pl
from jax.experimental.pallas import tpu as pltpu
from jax.sharding import PartitionSpec as P

HEAD_SIZE = 128
EPSILON = 1e-06
MASKED = -1e30
MESH = pl.DeviceIdType.MESH
NX, NY, NZ, NC = 4, 4, 8, 2
F32, BF16 = jnp.float32, jnp.bfloat16
ANY = pl.BlockSpec(memory_space=pl.ANY)
VM = pl.BlockSpec(memory_space=pltpu.VMEM)


def remote(src, dst, send_sem, recv_sem, device):
    return pltpu.make_async_remote_copy(
        src_ref=src,
        dst_ref=dst,
        send_sem=send_sem,
        recv_sem=recv_sem,
        device_id=device,
        device_id_type=MESH,
    )


class Place:
    def __init__(self):
        self.dp = lax.axis_index("dp")
        self.s = lax.axis_index("seq")
        self.y = self.dp // (NZ * NC)
        self.z = (self.dp // NC) % NZ
        self.c = self.dp % NC

    def at(self, dx=0, dy=0, dz=0, flip=False):
        s = (self.s + dx) % NX if dx else self.s
        y = (self.y + dy) % NY if dy else self.y
        z = (self.z + dz) % NZ if dz else self.z
        c = 1 - self.c if flip else self.c
        return (y * (NZ * NC) + z * NC + c, s)


def peers_of(me):
    peers = [me.at(dx=i) for i in range(1, NX)]
    peers += [me.at(dx=i, flip=True) for i in range(1, NX)]
    peers += [me.at(dy=i) for i in range(1, NY)]
    peers += [me.at(dz=i) for i in range(1, NZ)]
    peers += [me.at(dy=i, flip=True) for i in range(NY)]
    return peers


def greet(me):
    for peer in peers_of(me):
        pl.semaphore_signal(pltpu.get_barrier_semaphore(), inc=1, device_id=peer, device_id_type=MESH)


def enter(me):
    pl.semaphore_wait(pltpu.get_barrier_semaphore(), len(peers_of(me)))


SPLIT = 96


class Batch:
    def __init__(self, me, copies, sample, send, recv):
        self.all = remote(sample, sample, send, recv, me.at(dx=1))
        for copy in copies:
            copy.start()

    def arrived(self):
        self.all.wait_recv()

    def left(self):
        self.all.wait_send()


class RowGather:
    def __init__(self, me, buf, ysend, yrecv, zsend, zrecv):
        self.me, self.buf = me, buf
        self.ysend, self.yrecv = ysend.at[0], yrecv.at[0]
        self.zsend, self.zrecv = zsend.at[0], zrecv

    def start_y(self):
        me = self.me
        own = self.buf.at[me.c, 3, me.y, pl.ds(0, SPLIT)]
        copies = [remote(own, own, self.ysend, self.yrecv, me.at(dy=i)) for i in range(1, NY)]
        sample = self.buf.at[me.c, 3, pl.ds(0, 3), pl.ds(0, SPLIT)]
        self.first = Batch(me, copies, sample, self.ysend, self.yrecv)

    def ring(self, way, step):
        me = self.me
        here, there = (4 - step, 3 - step) if way == 0 else (2 + step, 3 + step)
        ys = pl.ds(0, NY) if step < 4 else pl.ds(2 * way, 2)
        source = self.buf.at[me.c, here, ys, pl.ds(0, SPLIT)]
        target = self.buf.at[me.c, there % NZ, ys, pl.ds(0, SPLIT)]
        device = me.at(dz=1) if way == 0 else me.at(dz=NZ - 1)
        return remote(source, target, self.zsend, self.zrecv.at[way * 4 + step - 1], device)

    def step(self, step):
        for way in (0, 1):
            if step > 1:
                self.ring(way, step - 1).wait_recv()
            if step <= 4:
                self.ring(way, step).start()

    def left(self):
        me = self.me
        self.first.left()
        sample = self.buf.at[me.c, pl.ds(0, 7), pl.ds(0, NY), pl.ds(0, SPLIT)]
        remote(sample, sample, self.zsend, self.zrecv.at[0], me.at(dz=1)).wait_send()


def rest_over_z(me, buf, send, recv):
    rows = pl.ds(SPLIT, buf.shape[3] - SPLIT)
    source = buf.at[me.c, 3, me.y, rows]
    copies = [
        remote(source, buf.at[me.c, (3 - i) % NZ, me.y, rows], send.at[0], recv.at[0], me.at(dz=i))
        for i in range(1, NZ)
    ]
    return Batch(me, copies, buf.at[me.c, pl.ds(0, 7), me.y, rows], send.at[0], recv.at[0])


def rest_over_y(me, buf, send, recv):
    rows = pl.ds(SPLIT, buf.shape[3] - SPLIT)
    block = buf.at[me.c, pl.ds(0, NZ), me.y, rows]
    copies = [remote(block, block, send.at[0], recv.at[0], me.at(dy=i)) for i in range(1, NY)]
    return Batch(me, copies, buf.at[me.c, pl.ds(0, NZ), pl.ds(0, 3), rows], send.at[0], recv.at[0])


def swap(me, buf, first, count, rows, send, recv):
    block = buf.at[me.c, pl.ds(first, count), pl.ds(0, NY), rows]
    return Batch(me, [remote(block, block, send, recv, me.at(flip=True))], block, send, recv)


def exchange(me, axis, count, source, target, sample, send, recv):
    copies = [
        remote(source(i), target(i), send.at[0], recv.at[0], me.at(**{axis: i})) for i in range(1, count)
    ]
    return Batch(me, copies, sample, send.at[0], recv.at[0])

def nt(a, b):
    return lax.dot_general(a, b, (((1,), (1,)), ((), ())), preferred_element_type=F32)


def tn(a, b):
    return lax.dot_general(a, b, (((0,), (0,)), ((), ())), preferred_element_type=F32)


def nn(a, b):
    return jnp.dot(a, b, preferred_element_type=F32)


def sorting(c0, c1, rows):
    here = lax.broadcasted_iota(jnp.int32, (rows, rows), 0)
    source = lax.broadcasted_iota(jnp.int32, (rows, rows), 1)
    later = here >= rows // 2
    rank = jnp.where(later, here - rows // 2, here)
    live = rank < jnp.where(later, c1, c0)
    return jnp.where((source == rank + jnp.where(later, c0, 0)) & live, 1.0, 0.0).astype(BF16)


def aligned(start, size):
    return pl.ds(pl.multiple_of(start, 128), size)


class Refs:
    pass


SCRATCH = dict(
    tok_raw=pltpu.VMEM((192, 1536), BF16),
    cot_raw=pltpu.VMEM((192, 1536), BF16),
    tok_all=pltpu.VMEM((NX, 192, 1536), BF16),
    cot_all=pltpu.VMEM((NX, 192, 384), BF16),
    w_all=pltpu.VMEM((NC, NZ, NY, 224, 128), BF16),
    w=pltpu.VMEM((1536, 1152), BF16),
    up=pltpu.VMEM((64, 1152), BF16),
    down=pltpu.VMEM((64, 1536), BF16),
    mm=pltpu.VMEM((256, 768), BF16),
    a_rows=pltpu.VMEM((NZ, 16, 128), F32),
    a_src=pltpu.VMEM((NZ, 16, 128), BF16),
    a_z=pltpu.VMEM((NZ, 16, 128), BF16),
    a_turn=pltpu.VMEM((NY, 32, 128), F32),
    a_low=pltpu.VMEM((NY, 32, 128), BF16),
    a_y=pltpu.VMEM((NC * NY, 32, 128), BF16),
    a_wide=pltpu.VMEM((256, 128), F32),
    a_pair=pltpu.VMEM((128, 256), BF16),
    part_wide=pltpu.VMEM((768, 128), F32),
    part_low=pltpu.VMEM((NC, NY, 96, 128), BF16),
    m_in=pltpu.VMEM((7, 96, 128), BF16),
    m_plane=pltpu.VMEM((NZ, 16, 128), F32),
    m_z=pltpu.VMEM((NZ - 1, 16, 128), F32),
    m_own=pltpu.VMEM((16, 128), F32),
    m_all=pltpu.VMEM((NX, 16, 128), F32),
    modded=pltpu.VMEM((768, 1536), BF16),
    stats=pltpu.VMEM((768, 128), F32),
    low=pltpu.VMEM((768, 64), BF16),
    proj=pltpu.VMEM((768, 1152), BF16),
    proj_grad=pltpu.VMEM((768, 1152), BF16),
    low_grad=pltpu.VMEM((768, 64), BF16),
    cot_own=pltpu.VMEM((192, 1536), BF16),
    attn=pltpu.VMEM((NX, 2, 96, 384), BF16),
    pg=pltpu.VMEM((2, NX, 96, 1536), BF16),
    ip=pltpu.VMEM((8, 3072), F32),
    half_l=pltpu.VMEM((2, 48, 1536), BF16),
    half_r=pltpu.VMEM((2, 48, 1536), BF16),
    comb_l=pltpu.VMEM((2, 48, 1536), BF16),
    comb_r=pltpu.VMEM((2, 48, 1536), BF16),
    from_l=pltpu.VMEM((2, 96, 1536), BF16),
    from_r=pltpu.VMEM((2, 96, 1536), BF16),
    ip_own=pltpu.VMEM((48, 128), F32),
    ip_in=pltpu.VMEM((3, 48, 128), F32),
    lo=pltpu.VMEM((NY, 2, 192, 128), BF16),
    l_y=pltpu.VMEM((NY - 1, 2, 192, 128), BF16),
    l_plane=pltpu.VMEM((NZ, 48, 128), BF16),
    l_z=pltpu.VMEM((NZ - 1, 48, 128), BF16),
    l_piece=pltpu.VMEM((48, 128), BF16),
    l_x=pltpu.VMEM((NC * NX, 48, 128), BF16),
)
PAIRS = dict(
    tk=(1, 8), ck=(2, 2), az=(1, 1), ay=(1, 1), my=(1, 1), mz=(1, 1), mx=(1, 1), gr=(2, 12), ot=(2, 2),
    ip=(1, 1), iz=(1, 1), iy=(1, 1), ic=(1, 1), ly=(1, 1), lz=(1, 1), lx=(1, 1), lg=(1, 1),
)
PLANES = dict(wy=(1, 1), wz=(1, 8), vz=(1, 1), vy=(1, 1), wc=(4, 4))
LOCAL = 8


def scratch_list():
    dma = pltpu.SemaphoreType.DMA
    out = list(SCRATCH.values())
    for send, recv in list(PAIRS.values()) + list(PLANES.values()):
        out += [dma((send,)), dma((recv,))]
    return out + [dma((LOCAL,))]


def named(refs):
    r = Refs()
    refs = list(refs)
    for name in SCRATCH:
        setattr(r, name, refs.pop(0))
    for name in PAIRS:
        setattr(r, name + "_s", refs.pop(0))
        setattr(r, name + "_r", refs.pop(0))
    for name in PLANES:
        setattr(r, name, [refs.pop(0), refs.pop(0)])
    r.local = refs.pop(0)
    return r


def whole_kernel(
    rows_ref, tok, cot, cond, wq, up_in, down_in, mm_in,
    attn_out, grad_out, mod, a_own, ig_all, f_all,
    *refs,
):
    r = named(refs)
    me = Place()
    s, y, z, c = me.s, me.y, me.z, me.c
    rows, width, att, heads = 192, 1536, 384, 3
    part = rows // 2
    image_rows = NX * part
    chunk = rows // 4
    scale = HEAD_SIZE ** (-0.5)
    right, left = me.at(dx=1), me.at(dx=NX - 1)
    sl, sr, so = (s + NX - 1) % NX, (s + 1) % NX, (s + 2) % NX
    c0, c1 = rows_ref[0, me.dp], rows_ref[1, me.dp]

    greet(me)
    offset = 48 * me.dp - 128 * ((96 * (me.dp // 2)) // 128)
    r.mm[...] = jnp.zeros_like(r.mm)
    raw_tok = pltpu.make_async_copy(tok, r.tok_raw, r.local.at[5])
    raw_tok.start()
    raw_cot = pltpu.make_async_copy(cot, r.cot_raw, r.local.at[6])
    raw_cot.start()
    locals_ = [
        pltpu.make_async_copy(
            mm_in.at[:, aligned(s * 768, 768)], r.mm.at[pl.ds(pl.multiple_of(offset, 16), 48)], r.local.at[0]
        ),
        pltpu.make_async_copy(down_in, r.down, r.local.at[1]),
    ]
    for b in range(3):
        locals_.append(
            pltpu.make_async_copy(
                up_in.at[:, aligned(b * width + s * att, att)], r.up.at[:, b * att : (b + 1) * att], r.local.at[2 + b]
            )
        )
    for copy in locals_:
        copy.start()
    pieces = []
    for b in range(3):
        block = wq[:, aligned(b * width + s * att, att)].astype(F32)
        pieces += [block[:, i * 128 : (i + 1) * 128] for i in range(3)]
    pieces.append(jnp.zeros((8, 128), F32))
    r.w_all[c, 3, y] = jnp.concatenate(pieces, axis=0).astype(BF16)
    wide = cond[...].astype(F32)
    wide = (wide / (1.0 + jnp.exp(-wide))).astype(BF16).astype(F32)
    r.a_rows[...] = jnp.zeros_like(r.a_rows)
    for p in range(NZ * NY):
        j = (96 * p) // 128
        for img in range(2):
            for t in range(2):
                if j + t < 24:
                    at = 4 * (p // NZ) + 2 * img + t
                    r.a_rows[p % NZ, at : at + 1, :] = wide[img : img + 1, (j + t) * 128 : (j + t + 1) * 128]
    r.a_src[...] = r.a_rows[...].astype(BF16)
    r.a_z[z] = r.a_src[z]
    r.m_plane[...] = jnp.zeros_like(r.m_plane)
    perm = sorting(c0, c1, rows)
    raw_tok.wait()
    r.tok_all[s] = nn(perm, r.tok_raw[...]).astype(BF16)

    enter(me)

    batches = []

    def send(batch):
        batches.append(batch)
        return batch

    quarter = part // 2

    def token_copy(img, slot):
        start = img * part
        owner, at, there = (
            (s, pl.ds(start, part), right),
            (s, pl.ds(start, part), left),
            (sl, pl.ds(start, quarter), right),
            (sr, pl.ds(start + quarter, quarter), left),
        )[slot]
        block = r.tok_all.at[owner, at]
        return remote(block, block, r.tk_s.at[0], r.tk_r.at[4 * img + slot], there)

    def own_tokens(img):
        token_copy(img, 0).start()
        token_copy(img, 1).start()

    def forward(img):
        for slot in (0, 1):
            token_copy(img, slot).wait_recv()
            token_copy(img, slot + 2).start()

    def wait_tokens(img):
        token_copy(img, 2).wait_recv()
        token_copy(img, 3).wait_recv()

    def own_cotangent(img):
        at = pl.ds(img * part, part)
        copies = [
            remote(
                r.cot_own.at[at, aligned(((s + i) % NX) * att, att)], r.cot_all.at[s, at],
                r.ck_s.at[img], r.ck_r.at[img], me.at(dx=i),
            )
            for i in range(1, NX)
        ]
        return send(Batch(me, copies, r.cot_all.at[pl.ds(0, 3), at], r.ck_s.at[img], r.ck_r.at[img]))

    az = send(
        exchange(
            me, "dz", NZ, lambda i: r.a_src.at[(z + i) % NZ], lambda i: r.a_z.at[z], r.a_z.at[pl.ds(0, 7)],
            r.az_s, r.az_r,
        )
    )
    weights = RowGather(me, r.w_all, *r.wy, *r.wz)
    weights.start_y()
    rest = send(rest_over_z(me, r.w_all, *r.vz))
    own_tokens(0)
    raw_cot.wait()
    r.cot_own[...] = nn(perm, r.cot_raw[...]).astype(BF16)
    cot0 = own_cotangent(0)
    az.arrived()
    turned = r.a_z[...].astype(F32)
    for at_y in range(NY):
        for at_z in range(NZ):
            r.a_turn[at_y, 4 * at_z : 4 * at_z + 4, :] = turned[at_z, 4 * at_y : 4 * at_y + 4]
    r.a_low[...] = r.a_turn[...].astype(BF16)
    r.a_y[NY * c + y] = r.a_low[y]

    def plane_exchange(source, target, sample, send_sem, recv_sem):
        copies = []
        for i in range(1, 2 * NY):
            dy, flip = i // 2, i % 2 == 1
            there = (y + dy) % NY
            at = (1 - c) if flip else c
            copies.append(
                remote(source(at, there), target(i - 1), send_sem.at[0], recv_sem.at[0], me.at(dy=dy, flip=flip))
            )
        return send(Batch(me, copies, sample, send_sem.at[0], recv_sem.at[0]))

    ay = plane_exchange(
        lambda at, there: r.a_low.at[there], lambda i: r.a_y.at[NY * c + y], r.a_y.at[pl.ds(0, 7)], r.ay_s, r.ay_r
    )
    weights.first.arrived()
    weights.step(1)
    ay.arrived()
    locals_[0].wait()
    r.a_wide[...] = r.a_y[...].reshape(256, 128).astype(F32)
    for img in range(2):
        for t in range(2):
            r.a_pair[img * 64 : (img + 1) * 64, t * 128 : (t + 1) * 128] = r.a_wide[
                pl.ds(2 * img + t, 64, stride=4), :
            ].astype(BF16)
    for j in range(6):
        columns = nn(r.a_pair[...], r.mm[:, j * 128 : (j + 1) * 128])
        for img in range(2):
            r.part_wide[pl.ds(img * 6 + j, 64, stride=12), :] = columns[img * 64 : (img + 1) * 64]
    r.part_low[...] = r.part_wide[...].astype(BF16).reshape(r.part_low.shape)
    my = plane_exchange(
        lambda at, there: r.part_low.at[at, there], lambda i: r.m_in.at[i], r.m_in, r.my_s, r.my_r
    )
    rest.arrived()
    spread = send(rest_over_y(me, r.w_all, *r.vy))
    my.arrived()
    total = r.part_low[c, y].astype(F32)
    for i in range(7):
        total += r.m_in[i].astype(F32)
    for at_z in range(NZ):
        r.m_plane[at_z, 0:12, :] = total[12 * at_z : 12 * at_z + 12]
    mz = send(
        exchange(
            me, "dz", NZ, lambda i: r.m_plane.at[(z + i) % NZ], lambda i: r.m_z.at[i - 1], r.m_z, r.mz_s, r.mz_r
        )
    )
    weights.step(2)
    forward(0)
    own_tokens(1)
    row = lax.broadcasted_iota(jnp.int32, (256, 128), 0)
    col = lax.broadcasted_iota(jnp.int32, (256, 128), 1)
    pick = jnp.where((row == col + offset) & (col < 48), 1.0, 0.0).astype(BF16)
    a_own[...] = nn(r.a_pair[...], pick).astype(BF16)
    r.cot_all[s] = r.cot_own[:, aligned(s * att, att)]

    def place(first, count, tiles, start):
        @pl.loop(0, NY * count)
        def _(i):
            at_y, at_d = i // count, first + i % count
            rows_at = pl.ds(start, 24 * len(tiles))
            one = r.w_all[0, at_d, at_y, rows_at].astype(F32)
            other = r.w_all[1, at_d, at_y, rows_at].astype(F32)
            at_z = (z + at_d + NZ - 3) % NZ
            at = pl.ds(pl.multiple_of(48 * (NZ * at_y + at_z), 16), 48)
            for k, t in enumerate(tiles):
                both = jnp.concatenate([one[24 * k : 24 * k + 24], other[24 * k : 24 * k + 24]], axis=0)
                r.w[at, t * 128 : (t + 1) * 128] = both.astype(BF16)

    upper_tiles, lower_tiles = range(4), range(4, 9)

    def swap_part(index, first, count, rows):
        return send(swap(me, r.w_all, first, count, rows, r.wc[0].at[index], r.wc[1].at[index]))

    upper, lower = pl.ds(0, SPLIT), pl.ds(SPLIT, r.w_all.shape[3] - SPLIT)
    def normalize(img):
        @pl.loop(0, NX)
        def _(block):
            x = r.tok_all[block, img * part : (img + 1) * part, :].astype(F32)
            mean = jnp.mean(x, axis=1, keepdims=True)
            centred = x - mean
            inverse = lax.rsqrt(jnp.mean(centred * centred, axis=1, keepdims=True) + EPSILON)
            rank = lax.broadcasted_iota(jnp.int32, (part, 1), 0)
            gain = 1.0 + mod[img : img + 1, width:]
            value = gain * (centred * inverse) + mod[img : img + 1, :width]
            at = pl.ds(pl.multiple_of(img * image_rows + block * part, 32), part)
            r.modded[at, :] = jnp.where(rank < (c0, c1)[img], value, 0.0).astype(BF16)
            r.stats[at, 0:1] = mean
            r.stats[at, 1:2] = inverse

    mz.arrived()
    total = r.m_plane[z]
    for i in range(NZ - 1):
        total += r.m_z[i]
    r.m_own[...] = total
    r.m_all[s] = total
    mx = send(
        exchange(
            me, "dx", NX, lambda i: r.m_own, lambda i: r.m_all.at[s], r.m_all.at[pl.ds(0, 3)], r.mx_s, r.mx_r
        )
    )
    weights.step(3)
    near = swap_part(0, 1, 5, upper)
    mx.arrived()
    mod[...] = jnp.zeros_like(mod)
    for k in range(NX):
        for img in range(2):
            for j in range(6):
                at = 768 * k + 128 * j
                mod[img : img + 1, at : at + 128] = r.m_all[k, img * 6 + j : img * 6 + j + 1, :]

    wait_tokens(0)
    normalize(0)
    weights.step(4)
    left_end = swap_part(1, 0, 1, upper)
    near.arrived()
    place(1, 5, upper_tiles, 0)
    spread.arrived()
    lower_part = swap_part(3, 0, NZ, lower)
    weights.step(5)
    right_end = swap_part(2, 6, 2, upper)
    forward(1)
    cot1 = own_cotangent(1)
    left_end.arrived()
    place(0, 1, upper_tiles, 0)
    right_end.arrived()
    place(6, 2, upper_tiles, 0)
    lower_part.arrived()
    place(0, NZ, lower_tiles, SPLIT)
    for copy in locals_[1:]:
        copy.wait()

    def project(img):
        at = slice(img * image_rows, (img + 1) * image_rows)
        r.low[at, :] = nt(r.modded[at, :], r.down[...]).astype(BF16)

        @pl.loop(0, 3)
        def _(n):
            cols = aligned(n * att, att)
            r.proj[at, cols] = (nn(r.modded[at, :], r.w[:, cols]) + nn(r.low[at, :], r.up[:, cols])).astype(BF16)

    lane = lax.broadcasted_iota(jnp.int32, (1, image_rows), 1)
    for _ in range(NX - 1):
        lane = jnp.where(lane >= part, lane - part, lane)

    def attend(img):
        at = slice(img * image_rows, (img + 1) * image_rows)
        allowed = lane < (c0, c1)[img]
        for h in range(heads):
            cols = slice(h * 128, (h + 1) * 128)
            key_cols = slice(att + h * 128, att + (h + 1) * 128)
            value_cols = slice(2 * att + h * 128, 2 * att + (h + 1) * 128)
            q, k, v = r.proj[at, cols], r.proj[at, key_cols], r.proj[at, value_cols]
            scores = jnp.where(allowed, nt(q, k), MASKED)
            largest = jnp.max(scores, axis=1, keepdims=True)
            raw = jnp.exp((scores - largest) * scale)
            probs = raw * (1.0 / jnp.sum(raw, axis=1, keepdims=True))
            probs_low = probs.astype(BF16)
            out = nn(probs_low, v).astype(BF16)
            r.attn[:, img, :, cols] = out.reshape(NX, part, 128)
            out_grad = r.cot_all[:, img * part : (img + 1) * part, cols].reshape(image_rows, 128)
            delta = jnp.sum(out_grad.astype(F32) * out.astype(F32), axis=1, keepdims=True)
            score_grads = (probs * (nt(out_grad, v) - delta)).astype(BF16)
            r.proj_grad[at, cols] = (nn(score_grads, k) * scale).astype(BF16)
            r.proj_grad[at, key_cols] = (tn(q, score_grads) * scale).T.astype(BF16)
            r.proj_grad[at, value_cols] = tn(out_grad, probs_low).T.astype(BF16)

    mine = aligned(s * att, att)

    def give(img):
        at = slice(img * part, (img + 1) * part)
        copies = [
            remote(
                r.attn.at[(s + i) % NX, img], attn_out.at[at, mine], r.ot_s.at[img], r.ot_r.at[img], me.at(dx=i)
            )
            for i in range(1, NX)
        ]
        attn_out[at, mine] = r.attn[s, img]
        return send(Batch(me, copies, attn_out.at[at, pl.ds(0, 3 * att)], r.ot_s.at[img], r.ot_r.at[img]))

    def low_grads(img):
        at = slice(img * image_rows, (img + 1) * image_rows)
        r.low_grad[at, :] = nt(r.proj_grad[at, :], r.up[...]).astype(BF16)

    def grads(img):
        at = slice(img * image_rows, (img + 1) * image_rows)

        @pl.loop(0, width // att)
        def _(n):
            f = aligned(n * att, att)
            grad = nt(r.proj_grad[at, :], r.w[f, :]) + nn(r.low_grad[at, :], r.down[:, f])
            r.pg[img, :, :, f] = grad.astype(BF16).reshape(NX, part, att)
            x = r.tok_all[:, img * part : (img + 1) * part, f].reshape(image_rows, att).astype(F32)
            normed = (x - r.stats[at, 0:1]) * r.stats[at, 1:2]
            r.ip[img : img + 1, f] = jnp.sum(grad, axis=0, keepdims=True)
            r.ip[img : img + 1, aligned(width + n * att, att)] = jnp.sum(grad * normed, axis=0, keepdims=True)

    half = part // 2
    first, second = pl.ds(0, half), pl.ds(half, half)

    def grad_copy(img, slot):
        src, dst, there = (
            (r.pg.at[img, so, first], r.half_l.at[img], right),
            (r.pg.at[img, so, second], r.half_r.at[img], left),
            (r.pg.at[img, sr, second], r.from_l.at[img, second], right),
            (r.pg.at[img, sl, first], r.from_r.at[img, first], left),
            (r.comb_r.at[img], r.from_l.at[img, first], right),
            (r.comb_l.at[img], r.from_r.at[img, second], left),
        )[slot]
        return remote(src, dst, r.gr_s.at[img], r.gr_r.at[6 * img + slot], there)

    def reduce_first(img):
        for slot in range(4):
            grad_copy(img, slot).start()

    def reduce_second(img):
        grad_copy(img, 0).wait_recv()
        r.comb_r[img] = (r.pg[img, sr, 0:half].astype(F32) + r.half_l[img].astype(F32)).astype(BF16)
        grad_copy(img, 4).start()
        grad_copy(img, 1).wait_recv()
        r.comb_l[img] = (r.pg[img, sl, half:part].astype(F32) + r.half_r[img].astype(F32)).astype(BF16)
        grad_copy(img, 5).start()

    project(0)
    cot0.arrived()
    attend(0)
    out0 = give(0)
    low_grads(0)
    grads(0)
    reduce_first(0)
    wait_tokens(1)
    normalize(1)
    project(1)
    cot1.arrived()
    attend(1)
    out1 = give(1)
    reduce_second(0)
    low_grads(1)

    r.lo[NX - 1 - s, 0] = jnp.zeros((192, 128), BF16)
    up_total = tn(r.low[...], r.proj_grad[...]).astype(BF16)
    for t in range(9):
        r.lo[(4 * (t // 3) + s) // 3, 0, (t % 3) * 64 : (t % 3 + 1) * 64, :] = up_total[:, t * 128 : (t + 1) * 128]
    down_total = tn(r.low_grad[...], r.modded[...]).astype(BF16)
    for t in range(12):
        r.lo[t // 3, 1, (t % 3) * 64 : (t % 3 + 1) * 64, :] = down_total[:, t * 128 : (t + 1) * 128]
    ly = send(
        exchange(me, "dy", NY, lambda i: r.lo.at[(y + i) % NY], lambda i: r.l_y.at[i - 1], r.l_y, r.ly_s, r.ly_r)
    )

    grads(1)
    reduce_first(1)
    for img in range(2):
        for j in range(24):
            at = img * 24 + j
            r.ip_own[at : at + 1, :] = r.ip[img : img + 1, j * 128 : (j + 1) * 128]
    ip = send(exchange(me, "dx", NX, lambda i: r.ip_own, lambda i: r.ip_in.at[i - 1], r.ip_in, r.ip_s, r.ip_r))

    ly.arrived()
    total = r.lo[y].astype(F32)
    for i in range(NY - 1):
        total += r.l_y[i].astype(F32)
    for i in range(NZ):
        at = slice(24 * i, 24 * i + 24)
        r.l_plane[i] = jnp.concatenate([total[0, at], total[1, at]], axis=0).astype(BF16)
    lz = send(
        exchange(
            me, "dz", NZ, lambda i: r.l_plane.at[(z + i) % NZ], lambda i: r.l_z.at[i - 1], r.l_z, r.lz_s, r.lz_r
        )
    )

    ip.arrived()
    ig_all[c, y, z] = (r.ip_own[...] + r.ip_in[0] + r.ip_in[1] + r.ip_in[2]).astype(BF16)
    own_ig = ig_all.at[c, y, z]
    iz = send(
        exchange(me, "dz", NZ, lambda i: own_ig, lambda i: own_ig, ig_all.at[c, y, pl.ds(0, 7)], r.iz_s, r.iz_r)
    )

    lz.arrived()
    total = r.l_plane[z].astype(F32)
    for i in range(NZ - 1):
        total += r.l_z[i].astype(F32)
    r.l_piece[...] = total.astype(BF16)
    r.l_x[NX * c + s] = r.l_piece[...]
    copies = [
        remote(
            r.l_piece, r.l_x.at[NX * c + s], r.lx_s.at[0], r.lx_r.at[0], me.at(dx=i // 2, flip=i % 2 == 1)
        )
        for i in range(1, 2 * NX)
    ]
    lx = send(Batch(me, copies, r.l_x.at[pl.ds(0, 7)], r.lx_s.at[0], r.lx_r.at[0]))

    iz.arrived()
    column = ig_all.at[c, y]
    iy = send(
        exchange(me, "dy", NY, lambda i: column, lambda i: column, ig_all.at[c, pl.ds(0, 3)], r.iy_s, r.iy_r)
    )
    reduce_second(1)

    lx.arrived()
    sums = [r.l_x[i].astype(F32) + r.l_x[NX + i].astype(F32) for i in range(NX)]
    pieces = []
    for i in range(3):
        k = (3 * y + i) % 4
        pieces.append((r.l_x[k].astype(F32) + r.l_x[NX + k].astype(F32))[0:24])
    pieces.append((sums[0] + sums[1] + sums[2] + sums[3])[24:48])
    f_all[z] = jnp.concatenate(pieces, axis=0).astype(BF16)
    lg = send(
        exchange(
            me, "dz", NZ, lambda i: f_all.at[z], lambda i: f_all.at[z], f_all.at[pl.ds(0, 7)], r.lg_s, r.lg_r
        )
    )

    iy.arrived()
    whole_core = ig_all.at[c]
    ic = send(
        Batch(
            me, [remote(whole_core, whole_core, r.ic_s.at[0], r.ic_r.at[0], me.at(flip=True))], whole_core,
            r.ic_s.at[0], r.ic_r.at[0],
        )
    )
    for img in range(2):
        for slot in range(2, 6):
            grad_copy(img, slot).wait_recv()
        grad_out[img * part : (img + 1) * part, :] = (
            r.pg[img, s].astype(F32) + r.from_l[img].astype(F32) + r.from_r[img].astype(F32)
        ).astype(BF16)
    ic.arrived()
    lg.arrived()
    out0.arrived()
    out1.arrived()

    for batch in batches:
        batch.left()
    tokens_sent = r.tok_all.at[pl.ds(0, 3)]
    remote(tokens_sent, tokens_sent, r.tk_s.at[0], r.tk_r.at[0], right).wait_send()
    for img in range(2):
        grads_sent = r.pg.at[img, pl.ds(0, 3)]
        remote(grads_sent, grads_sent, r.gr_s.at[img], r.gr_r.at[0], right).wait_send()
    weights.left()


def whole(counts, tok, cot, cond, wq, up, down, mm):
    return pl.pallas_call(
        whole_kernel,
        out_shape=(
            jax.ShapeDtypeStruct((192, 1536), BF16),
            jax.ShapeDtypeStruct((192, 1536), BF16),
            jax.ShapeDtypeStruct((8, 3072), F32),
            jax.ShapeDtypeStruct((128, 128), BF16),
            jax.ShapeDtypeStruct((NC, NY, NZ, 48, 128), BF16),
            jax.ShapeDtypeStruct((NZ, 96, 128), BF16),
        ),
        in_specs=[pl.BlockSpec(memory_space=pltpu.SMEM), ANY, ANY, VM, VM, ANY, ANY, ANY],
        out_specs=(VM, VM, VM, VM, VM, VM),
        scratch_shapes=scratch_list(),
        compiler_params=pltpu.CompilerParams(
            collective_id=1, has_side_effects=True, vmem_limit_bytes=60 * 1024 * 1024
        ),
        name="whole",
    )(counts, tok, cot, cond, wq, up, down, mm)


def tail_kernel(
    counts, attn, grad, tok, mod, act, ig, pieces,
    attn_out, token_grad, down_out, up_out, mod_grad,
    ig_wide, sorted_grad,
):
    rows, width = tok.shape
    part = rows // 2
    dp = lax.axis_index("dp")
    perm = sorting(counts[0, dp], counts[1, dp], rows)
    attn_out[...] = tn(perm, attn[...]).astype(BF16)
    for img in range(2):
        at = slice(img * part, (img + 1) * part)
        x = nn(perm[at], tok[...])
        centred = x - jnp.mean(x, axis=1, keepdims=True)
        inverse = lax.rsqrt(jnp.mean(centred * centred, axis=1, keepdims=True) + EPSILON)
        normed = centred * inverse
        g = (1.0 + mod[img : img + 1, width:]) * grad[at, :].astype(F32)
        sorted_grad[at, :] = (
            inverse
            * (g - jnp.mean(g, axis=1, keepdims=True) - normed * jnp.mean(g * normed, axis=1, keepdims=True))
        ).astype(BF16)
    token_grad[...] = tn(perm, sorted_grad[...]).astype(BF16)

    ig_wide[...] = ig[...].reshape(3072, 128).astype(F32)
    turned = act[...].astype(F32).T.astype(BF16)[:48]
    for j in range(24):
        parts = [ig_wide[pl.ds(img * 24 + j, 64, stride=48), :].astype(BF16) for img in range(2)]
        mod_grad[:, j * 128 : (j + 1) * 128] = nn(turned, jnp.concatenate(parts, axis=0))

    place = dp % (NZ * NC)
    flat = pieces[...].astype(F32)

    def tiles(i):
        triple = jnp.concatenate([flat[k, 24 * i : 24 * i + 24] for k in range(NZ)], axis=0).astype(BF16)
        return [triple[j * 64 : (j + 1) * 64] for j in range(3)]

    row = lax.broadcasted_iota(jnp.int32, (128, 128), 0)
    col = lax.broadcasted_iota(jnp.int32, (128, 128), 1)
    total = jnp.zeros((64, 128), F32)
    for i, tile in enumerate(tiles(0) + tiles(1) + tiles(2)):
        total += nn(tile, jnp.where(row + 128 * i == col + 72 * place, 1.0, 0.0).astype(BF16))
    up_out[...] = total[:, :72]
    total = jnp.zeros((128, 64), F32)
    for i, tile in enumerate(tiles(3)):
        total += nt(jnp.where(col + 128 * i == row + 24 * place, 1.0, 0.0).astype(BF16), tile)
    down_out[...] = total[:24]


def tail(counts, attn, grad, tok, mod, act, ig, pieces):
    return pl.pallas_call(
        tail_kernel,
        out_shape=(
            jax.ShapeDtypeStruct((192, 1536), BF16),
            jax.ShapeDtypeStruct((192, 1536), BF16),
            jax.ShapeDtypeStruct((24, 64), F32),
            jax.ShapeDtypeStruct((64, 72), F32),
            jax.ShapeDtypeStruct((48, 3072), F32),
        ),
        in_specs=[pl.BlockSpec(memory_space=pltpu.SMEM)] + [VM] * 7,
        out_specs=(VM, VM, VM, VM, VM),
        scratch_shapes=[pltpu.VMEM((3072, 128), F32), pltpu.VMEM((192, 1536), BF16)],
        compiler_params=pltpu.CompilerParams(vmem_limit_bytes=60 * 1024 * 1024),
        name="tail",
    )(counts, attn, grad, tok, mod, act, ig, pieces)


def body(
    tokens,
    cotangent,
    condition,
    per_image_rows,
    query_key_value_weight,
    adapter_down,
    adapter_up,
    modulation_matrix,
):
    counts = per_image_rows.T
    attn, grad, mod, act, ig, pieces = whole(
        counts,
        tokens[0],
        cotangent[0],
        condition[0],
        query_key_value_weight,
        adapter_up,
        adapter_down.T,
        modulation_matrix,
    )
    attention, token_grad, down_grad, up_grad, mod_grad = tail(
        counts, attn, grad, tokens[0], mod, act, ig, pieces
    )
    return attention[None], token_grad[None], down_grad, up_grad, mod_grad


def solution(mesh):
    in_specs = (
        P("dp", "seq", None),
        P("dp", "seq", None),
        P("dp", None, None),
        P(),
        P("dp", None),
        P(),
        P(),
        P("dp", None),
    )
    out_specs = (
        P("dp", "seq", None),
        P("dp", "seq", None),
        P("dp", None),
        P(None, "dp"),
        P("dp", None),
    )
    return jax.shard_map(body, mesh=mesh, in_specs=in_specs, out_specs=out_specs, check_vma=False)
```

```python
import jax
import jax.numpy as jnp
from jax import lax
from jax.experimental import pallas as pl
from jax.experimental.pallas import tpu as pltpu
from jax.sharding import PartitionSpec as P

HEAD_SIZE = 128
EPSILON = 1e-06
MASKED = -1e30
MESH = pl.DeviceIdType.MESH
NX, NY, NZ, NC = 4, 4, 8, 2
F32, BF16 = jnp.float32, jnp.bfloat16
ANY = pl.BlockSpec(memory_space=pl.ANY)
VM = pl.BlockSpec(memory_space=pltpu.VMEM)


def remote(src, dst, send_sem, recv_sem, device):
    return pltpu.make_async_remote_copy(
        src_ref=src,
        dst_ref=dst,
        send_sem=send_sem,
        recv_sem=recv_sem,
        device_id=device,
        device_id_type=MESH,
    )


class Place:
    def __init__(self):
        self.dp = lax.axis_index("dp")
        self.s = lax.axis_index("seq")
        self.y = self.dp // (NZ * NC)
        self.z = (self.dp // NC) % NZ
        self.c = self.dp % NC

    def at(self, dx=0, dy=0, dz=0, flip=False):
        s = (self.s + dx) % NX if dx else self.s
        y = (self.y + dy) % NY if dy else self.y
        z = (self.z + dz) % NZ if dz else self.z
        c = 1 - self.c if flip else self.c
        return (y * (NZ * NC) + z * NC + c, s)


def peers_of(me):
    peers = [me.at(dx=i) for i in range(1, NX)]
    peers += [me.at(dx=i, flip=True) for i in range(1, NX)]
    peers += [me.at(dy=i) for i in range(1, NY)]
    peers += [me.at(dz=i) for i in range(1, NZ)]
    peers += [me.at(dy=i, flip=True) for i in range(NY)]
    return peers


def greet(me):
    for peer in peers_of(me):
        pl.semaphore_signal(pltpu.get_barrier_semaphore(), inc=1, device_id=peer, device_id_type=MESH)


def enter(me):
    pl.semaphore_wait(pltpu.get_barrier_semaphore(), len(peers_of(me)))


SPLIT = 96


class Batch:
    def __init__(self, me, copies, sample, send, recv):
        self.all = remote(sample, sample, send, recv, me.at(dx=1))
        for copy in copies:
            copy.start()

    def arrived(self):
        self.all.wait_recv()

    def left(self):
        self.all.wait_send()


class RowGather:
    def __init__(self, me, buf, ysend, yrecv, zsend, zrecv):
        self.me, self.buf = me, buf
        self.ysend, self.yrecv = ysend.at[0], yrecv.at[0]
        self.zsend, self.zrecv = zsend.at[0], zrecv

    def start_y(self):
        me = self.me
        own = self.buf.at[me.c, 3, me.y, pl.ds(0, SPLIT)]
        copies = [remote(own, own, self.ysend, self.yrecv, me.at(dy=i)) for i in range(1, NY)]
        sample = self.buf.at[me.c, 3, pl.ds(0, 3), pl.ds(0, SPLIT)]
        self.first = Batch(me, copies, sample, self.ysend, self.yrecv)

    def ring(self, way, step):
        me = self.me
        here, there = (4 - step, 3 - step) if way == 0 else (2 + step, 3 + step)
        ys = pl.ds(0, NY) if step < 4 else pl.ds(2 * way, 2)
        source = self.buf.at[me.c, here, ys, pl.ds(0, SPLIT)]
        target = self.buf.at[me.c, there % NZ, ys, pl.ds(0, SPLIT)]
        device = me.at(dz=1) if way == 0 else me.at(dz=NZ - 1)
        return remote(source, target, self.zsend, self.zrecv.at[way * 4 + step - 1], device)

    def step(self, step):
        for way in (0, 1):
            if step > 1:
                self.ring(way, step - 1).wait_recv()
            if step <= 4:
                self.ring(way, step).start()

    def left(self):
        me = self.me
        self.first.left()
        sample = self.buf.at[me.c, pl.ds(0, 7), pl.ds(0, NY), pl.ds(0, SPLIT)]
        remote(sample, sample, self.zsend, self.zrecv.at[0], me.at(dz=1)).wait_send()


def rest_over_z(me, buf, send, recv):
    rows = pl.ds(SPLIT, buf.shape[3] - SPLIT)
    source = buf.at[me.c, 3, me.y, rows]
    copies = [
        remote(source, buf.at[me.c, (3 - i) % NZ, me.y, rows], send.at[0], recv.at[0], me.at(dz=i))
        for i in range(1, NZ)
    ]
    return Batch(me, copies, buf.at[me.c, pl.ds(0, 7), me.y, rows], send.at[0], recv.at[0])


class Spread:
    def __init__(self, me, buf, send, recv):
        self.me, self.buf, self.send, self.recv = me, buf, send.at[0], recv
        self.rows = pl.ds(SPLIT, buf.shape[3] - SPLIT)

    def copy(self, slot):
        me = self.me
        owner, blocks, there = (
            (me.y, pl.ds(0, NZ), 1),
            (me.y, pl.ds(0, NZ), NY - 1),
            ((me.y + NY - 1) % NY, pl.ds(0, NZ // 2), 1),
            ((me.y + 1) % NY, pl.ds(NZ // 2, NZ // 2), NY - 1),
        )[slot]
        block = self.buf.at[me.c, blocks, owner, self.rows]
        return remote(block, block, self.send, self.recv.at[slot], me.at(dy=there))

    def start(self):
        self.copy(0).start()
        self.copy(1).start()

    def forward(self):
        for slot in (0, 1):
            self.copy(slot).wait_recv()
            self.copy(slot + 2).start()

    def arrived(self):
        self.copy(2).wait_recv()
        self.copy(3).wait_recv()

    def left(self):
        sample = self.buf.at[self.me.c, pl.ds(0, NZ), pl.ds(0, 3), self.rows]
        remote(sample, sample, self.send, self.recv.at[0], self.me.at(dy=1)).wait_send()


def swap(me, buf, first, count, rows, send, recv):
    block = buf.at[me.c, pl.ds(first, count), pl.ds(0, NY), rows]
    return Batch(me, [remote(block, block, send, recv, me.at(flip=True))], block, send, recv)


def exchange(me, axis, count, source, target, sample, send, recv):
    copies = [
        remote(source(i), target(i), send.at[0], recv.at[0], me.at(**{axis: i})) for i in range(1, count)
    ]
    return Batch(me, copies, sample, send.at[0], recv.at[0])

def nt(a, b):
    return lax.dot_general(a, b, (((1,), (1,)), ((), ())), preferred_element_type=F32)


def tn(a, b):
    return lax.dot_general(a, b, (((0,), (0,)), ((), ())), preferred_element_type=F32)


def nn(a, b):
    return jnp.dot(a, b, preferred_element_type=F32)


def sorting(c0, c1, rows):
    here = lax.broadcasted_iota(jnp.int32, (rows, rows), 0)
    source = lax.broadcasted_iota(jnp.int32, (rows, rows), 1)
    later = here >= rows // 2
    rank = jnp.where(later, here - rows // 2, here)
    live = rank < jnp.where(later, c1, c0)
    return jnp.where((source == rank + jnp.where(later, c0, 0)) & live, 1.0, 0.0).astype(BF16)


def aligned(start, size):
    return pl.ds(pl.multiple_of(start, 128), size)


class Refs:
    pass


SCRATCH = dict(
    tok_raw=pltpu.VMEM((192, 1536), BF16),
    cot_raw=pltpu.VMEM((192, 1536), BF16),
    tok_all=pltpu.VMEM((NX, 192, 1536), BF16),
    cot_all=pltpu.VMEM((NX, 192, 384), BF16),
    w_all=pltpu.VMEM((NC, NZ, NY, 224, 128), BF16),
    w=pltpu.VMEM((1536, 1152), BF16),
    up=pltpu.VMEM((64, 1152), BF16),
    down=pltpu.VMEM((64, 1536), BF16),
    mm=pltpu.VMEM((256, 768), BF16),
    a_rows=pltpu.VMEM((NZ, 16, 128), F32),
    a_src=pltpu.VMEM((NZ, 16, 128), BF16),
    a_z=pltpu.VMEM((NZ, 16, 128), BF16),
    a_turn=pltpu.VMEM((NY, 32, 128), F32),
    a_low=pltpu.VMEM((NY, 32, 128), BF16),
    a_y=pltpu.VMEM((NC * NY, 32, 128), BF16),
    a_wide=pltpu.VMEM((256, 128), F32),
    a_pair=pltpu.VMEM((128, 256), BF16),
    part_wide=pltpu.VMEM((768, 128), F32),
    part_low=pltpu.VMEM((NC, NY, 96, 128), BF16),
    m_in=pltpu.VMEM((7, 96, 128), BF16),
    m_plane=pltpu.VMEM((NZ, 16, 128), F32),
    m_z=pltpu.VMEM((NZ - 1, 16, 128), F32),
    m_own=pltpu.VMEM((16, 128), F32),
    m_all=pltpu.VMEM((NX, 16, 128), F32),
    modded=pltpu.VMEM((768, 1536), BF16),
    stats=pltpu.VMEM((768, 128), F32),
    low=pltpu.VMEM((768, 64), BF16),
    proj=pltpu.VMEM((768, 1152), BF16),
    proj_grad=pltpu.VMEM((768, 1152), BF16),
    low_grad=pltpu.VMEM((768, 64), BF16),
    cot_own=pltpu.VMEM((192, 1536), BF16),
    attn=pltpu.VMEM((NX, 2, 96, 384), BF16),
    stage_l=pltpu.VMEM((2, 48, 384), BF16),
    stage_r=pltpu.VMEM((2, 48, 384), BF16),
    pg=pltpu.VMEM((2, NX, 96, 1536), BF16),
    ip=pltpu.VMEM((8, 3072), F32),
    half_l=pltpu.VMEM((2, 48, 1536), BF16),
    half_r=pltpu.VMEM((2, 48, 1536), BF16),
    comb_l=pltpu.VMEM((2, 48, 1536), BF16),
    comb_r=pltpu.VMEM((2, 48, 1536), BF16),
    from_l=pltpu.VMEM((2, 96, 1536), BF16),
    from_r=pltpu.VMEM((2, 96, 1536), BF16),
    ip_own=pltpu.VMEM((48, 128), F32),
    ip_in=pltpu.VMEM((3, 48, 128), F32),
    lo=pltpu.VMEM((NY, 2, 192, 128), BF16),
    l_y=pltpu.VMEM((NY - 1, 2, 192, 128), BF16),
    l_plane=pltpu.VMEM((NZ, 48, 128), BF16),
    l_z=pltpu.VMEM((NZ - 1, 48, 128), BF16),
    l_piece=pltpu.VMEM((48, 128), BF16),
    l_x=pltpu.VMEM((NC * NX, 48, 128), BF16),
)
PAIRS = dict(
    tk=(1, 8), ck=(2, 2), az=(1, 1), ay=(1, 1), my=(1, 1), mz=(1, 1), mx=(1, 1), gr=(2, 12), ot=(2, 12),
    ip=(1, 1), iz=(1, 1), iy=(1, 1), ic=(1, 1), ly=(1, 1), lz=(1, 1), lx=(1, 1), lg=(1, 1),
)
PLANES = dict(wy=(1, 1), wz=(1, 8), vz=(1, 1), vy=(1, 4), wc=(4, 4))
LOCAL = 8


def scratch_list():
    dma = pltpu.SemaphoreType.DMA
    out = list(SCRATCH.values())
    for send, recv in list(PAIRS.values()) + list(PLANES.values()):
        out += [dma((send,)), dma((recv,))]
    return out + [dma((LOCAL,))]


def named(refs):
    r = Refs()
    refs = list(refs)
    for name in SCRATCH:
        setattr(r, name, refs.pop(0))
    for name in PAIRS:
        setattr(r, name + "_s", refs.pop(0))
        setattr(r, name + "_r", refs.pop(0))
    for name in PLANES:
        setattr(r, name, [refs.pop(0), refs.pop(0)])
    r.local = refs.pop(0)
    return r


def whole_kernel(
    rows_ref, tok, cot, cond, wq, up_in, down_in, mm_in,
    attn_out, grad_out, mod, a_own, ig_all, f_all,
    *refs,
):
    r = named(refs)
    me = Place()
    s, y, z, c = me.s, me.y, me.z, me.c
    rows, width, att, heads = 192, 1536, 384, 3
    part = rows // 2
    image_rows = NX * part
    chunk = rows // 4
    scale = HEAD_SIZE ** (-0.5)
    right, left = me.at(dx=1), me.at(dx=NX - 1)
    sl, sr, so = (s + NX - 1) % NX, (s + 1) % NX, (s + 2) % NX
    c0, c1 = rows_ref[0, me.dp], rows_ref[1, me.dp]

    greet(me)
    offset = 48 * me.dp - 128 * ((96 * (me.dp // 2)) // 128)
    r.mm[...] = jnp.zeros_like(r.mm)
    raw_tok = pltpu.make_async_copy(tok, r.tok_raw, r.local.at[5])
    raw_tok.start()
    raw_cot = pltpu.make_async_copy(cot, r.cot_raw, r.local.at[6])
    raw_cot.start()
    locals_ = [
        pltpu.make_async_copy(
            mm_in.at[:, aligned(s * 768, 768)], r.mm.at[pl.ds(pl.multiple_of(offset, 16), 48)], r.local.at[0]
        ),
        pltpu.make_async_copy(down_in, r.down, r.local.at[1]),
    ]
    for b in range(3):
        locals_.append(
            pltpu.make_async_copy(
                up_in.at[:, aligned(b * width + s * att, att)], r.up.at[:, b * att : (b + 1) * att], r.local.at[2 + b]
            )
        )
    for copy in locals_:
        copy.start()
    pieces = []
    for b in range(3):
        block = wq[:, aligned(b * width + s * att, att)].astype(F32)
        pieces += [block[:, i * 128 : (i + 1) * 128] for i in range(3)]
    pieces.append(jnp.zeros((8, 128), F32))
    r.w_all[c, 3, y] = jnp.concatenate(pieces, axis=0).astype(BF16)
    wide = cond[...].astype(F32)
    wide = (wide / (1.0 + jnp.exp(-wide))).astype(BF16).astype(F32)
    r.a_rows[...] = jnp.zeros_like(r.a_rows)
    for p in range(NZ * NY):
        j = (96 * p) // 128
        for img in range(2):
            for t in range(2):
                if j + t < 24:
                    at = 4 * (p // NZ) + 2 * img + t
                    r.a_rows[p % NZ, at : at + 1, :] = wide[img : img + 1, (j + t) * 128 : (j + t + 1) * 128]
    r.a_src[...] = r.a_rows[...].astype(BF16)
    r.a_z[z] = r.a_src[z]
    r.m_plane[...] = jnp.zeros_like(r.m_plane)
    perm = sorting(c0, c1, rows)
    raw_tok.wait()
    r.tok_all[s] = nn(perm, r.tok_raw[...]).astype(BF16)

    enter(me)

    batches = []

    def send(batch):
        batches.append(batch)
        return batch

    quarter = part // 2

    def token_copy(img, slot):
        start = img * part
        owner, at, there = (
            (s, pl.ds(start, part), right),
            (s, pl.ds(start, part), left),
            (sl, pl.ds(start, quarter), right),
            (sr, pl.ds(start + quarter, quarter), left),
        )[slot]
        block = r.tok_all.at[owner, at]
        return remote(block, block, r.tk_s.at[0], r.tk_r.at[4 * img + slot], there)

    def own_tokens(img):
        token_copy(img, 0).start()
        token_copy(img, 1).start()

    def forward(img):
        for slot in (0, 1):
            token_copy(img, slot).wait_recv()
            token_copy(img, slot + 2).start()

    def wait_tokens(img):
        token_copy(img, 2).wait_recv()
        token_copy(img, 3).wait_recv()

    def own_cotangent(img):
        at = pl.ds(img * part, part)
        copies = [
            remote(
                r.cot_own.at[at, aligned(((s + i) % NX) * att, att)], r.cot_all.at[s, at],
                r.ck_s.at[img], r.ck_r.at[img], me.at(dx=i),
            )
            for i in range(1, NX)
        ]
        return send(Batch(me, copies, r.cot_all.at[pl.ds(0, 3), at], r.ck_s.at[img], r.ck_r.at[img]))

    az = send(
        exchange(
            me, "dz", NZ, lambda i: r.a_src.at[(z + i) % NZ], lambda i: r.a_z.at[z], r.a_z.at[pl.ds(0, 7)],
            r.az_s, r.az_r,
        )
    )
    weights = RowGather(me, r.w_all, *r.wy, *r.wz)
    weights.start_y()
    rest = send(rest_over_z(me, r.w_all, *r.vz))
    own_tokens(0)
    raw_cot.wait()
    r.cot_own[...] = nn(perm, r.cot_raw[...]).astype(BF16)
    cot0 = own_cotangent(0)
    az.arrived()
    turned = r.a_z[...].astype(F32)
    for at_y in range(NY):
        for at_z in range(NZ):
            r.a_turn[at_y, 4 * at_z : 4 * at_z + 4, :] = turned[at_z, 4 * at_y : 4 * at_y + 4]
    r.a_low[...] = r.a_turn[...].astype(BF16)
    r.a_y[NY * c + y] = r.a_low[y]

    def plane_exchange(source, target, sample, send_sem, recv_sem):
        copies = []
        for i in range(1, 2 * NY):
            dy, flip = i // 2, i % 2 == 1
            there = (y + dy) % NY
            at = (1 - c) if flip else c
            copies.append(
                remote(source(at, there), target(i - 1), send_sem.at[0], recv_sem.at[0], me.at(dy=dy, flip=flip))
            )
        return send(Batch(me, copies, sample, send_sem.at[0], recv_sem.at[0]))

    ay = plane_exchange(
        lambda at, there: r.a_low.at[there], lambda i: r.a_y.at[NY * c + y], r.a_y.at[pl.ds(0, 7)], r.ay_s, r.ay_r
    )
    weights.first.arrived()
    weights.step(1)
    ay.arrived()
    locals_[0].wait()
    r.a_wide[...] = r.a_y[...].reshape(256, 128).astype(F32)
    for img in range(2):
        for t in range(2):
            r.a_pair[img * 64 : (img + 1) * 64, t * 128 : (t + 1) * 128] = r.a_wide[
                pl.ds(2 * img + t, 64, stride=4), :
            ].astype(BF16)
    for j in range(6):
        columns = nn(r.a_pair[...], r.mm[:, j * 128 : (j + 1) * 128])
        for img in range(2):
            r.part_wide[pl.ds(img * 6 + j, 64, stride=12), :] = columns[img * 64 : (img + 1) * 64]
    r.part_low[...] = r.part_wide[...].astype(BF16).reshape(r.part_low.shape)
    my = plane_exchange(
        lambda at, there: r.part_low.at[at, there], lambda i: r.m_in.at[i], r.m_in, r.my_s, r.my_r
    )
    rest.arrived()
    spread = send(Spread(me, r.w_all, *r.vy))
    spread.start()
    my.arrived()
    total = r.part_low[c, y].astype(F32)
    for i in range(7):
        total += r.m_in[i].astype(F32)
    for at_z in range(NZ):
        r.m_plane[at_z, 0:12, :] = total[12 * at_z : 12 * at_z + 12]
    mz = send(
        exchange(
            me, "dz", NZ, lambda i: r.m_plane.at[(z + i) % NZ], lambda i: r.m_z.at[i - 1], r.m_z, r.mz_s, r.mz_r
        )
    )
    weights.step(2)
    forward(0)
    own_tokens(1)
    row = lax.broadcasted_iota(jnp.int32, (256, 128), 0)
    col = lax.broadcasted_iota(jnp.int32, (256, 128), 1)
    pick = jnp.where((row == col + offset) & (col < 48), 1.0, 0.0).astype(BF16)
    a_own[...] = nn(r.a_pair[...], pick).astype(BF16)
    r.cot_all[s] = r.cot_own[:, aligned(s * att, att)]

    def place(first, count, tiles, start):
        @pl.loop(0, NY * count)
        def _(i):
            at_y, at_d = i // count, first + i % count
            rows_at = pl.ds(start, 24 * len(tiles))
            one = r.w_all[0, at_d, at_y, rows_at].astype(F32)
            other = r.w_all[1, at_d, at_y, rows_at].astype(F32)
            at_z = (z + at_d + NZ - 3) % NZ
            at = pl.ds(pl.multiple_of(48 * (NZ * at_y + at_z), 16), 48)
            for k, t in enumerate(tiles):
                both = jnp.concatenate([one[24 * k : 24 * k + 24], other[24 * k : 24 * k + 24]], axis=0)
                r.w[at, t * 128 : (t + 1) * 128] = both.astype(BF16)

    upper_tiles, lower_tiles = range(4), range(4, 9)

    def swap_part(index, first, count, rows):
        return send(swap(me, r.w_all, first, count, rows, r.wc[0].at[index], r.wc[1].at[index]))

    upper, lower = pl.ds(0, SPLIT), pl.ds(SPLIT, r.w_all.shape[3] - SPLIT)
    def normalize(img):
        @pl.loop(0, NX)
        def _(block):
            x = r.tok_all[block, img * part : (img + 1) * part, :].astype(F32)
            mean = jnp.mean(x, axis=1, keepdims=True)
            centred = x - mean
            inverse = lax.rsqrt(jnp.mean(centred * centred, axis=1, keepdims=True) + EPSILON)
            rank = lax.broadcasted_iota(jnp.int32, (part, 1), 0)
            gain = 1.0 + mod[img : img + 1, width:]
            value = gain * (centred * inverse) + mod[img : img + 1, :width]
            at = pl.ds(pl.multiple_of(img * image_rows + block * part, 32), part)
            r.modded[at, :] = jnp.where(rank < (c0, c1)[img], value, 0.0).astype(BF16)
            r.stats[at, 0:1] = mean
            r.stats[at, 1:2] = inverse

    mz.arrived()
    total = r.m_plane[z]
    for i in range(NZ - 1):
        total += r.m_z[i]
    r.m_own[...] = total
    r.m_all[s] = total
    mx = send(
        exchange(
            me, "dx", NX, lambda i: r.m_own, lambda i: r.m_all.at[s], r.m_all.at[pl.ds(0, 3)], r.mx_s, r.mx_r
        )
    )
    weights.step(3)
    near = swap_part(0, 1, 5, upper)
    mx.arrived()
    mod[...] = jnp.zeros_like(mod)
    for k in range(NX):
        for img in range(2):
            for j in range(6):
                at = 768 * k + 128 * j
                mod[img : img + 1, at : at + 128] = r.m_all[k, img * 6 + j : img * 6 + j + 1, :]

    spread.forward()
    wait_tokens(0)
    normalize(0)
    weights.step(4)
    left_end = swap_part(1, 0, 1, upper)
    near.arrived()
    place(1, 5, upper_tiles, 0)
    spread.arrived()
    lower_part = swap_part(3, 0, NZ, lower)
    weights.step(5)
    right_end = swap_part(2, 6, 2, upper)
    forward(1)
    cot1 = own_cotangent(1)
    left_end.arrived()
    place(0, 1, upper_tiles, 0)
    right_end.arrived()
    place(6, 2, upper_tiles, 0)
    lower_part.arrived()
    place(0, NZ, lower_tiles, SPLIT)
    for copy in locals_[1:]:
        copy.wait()

    def project(img):
        at = slice(img * image_rows, (img + 1) * image_rows)
        r.low[at, :] = nt(r.modded[at, :], r.down[...]).astype(BF16)

        @pl.loop(0, 3)
        def _(n):
            cols = aligned(n * att, att)
            r.proj[at, cols] = (nn(r.modded[at, :], r.w[:, cols]) + nn(r.low[at, :], r.up[:, cols])).astype(BF16)

    lane = lax.broadcasted_iota(jnp.int32, (1, image_rows), 1)
    for _ in range(NX - 1):
        lane = jnp.where(lane >= part, lane - part, lane)

    def attend(img):
        at = slice(img * image_rows, (img + 1) * image_rows)
        allowed = lane < (c0, c1)[img]
        for h in range(heads):
            cols = slice(h * 128, (h + 1) * 128)
            key_cols = slice(att + h * 128, att + (h + 1) * 128)
            value_cols = slice(2 * att + h * 128, 2 * att + (h + 1) * 128)
            q, k, v = r.proj[at, cols], r.proj[at, key_cols], r.proj[at, value_cols]
            scores = jnp.where(allowed, nt(q, k), MASKED)
            largest = jnp.max(scores, axis=1, keepdims=True)
            raw = jnp.exp((scores - largest) * scale)
            probs = raw * (1.0 / jnp.sum(raw, axis=1, keepdims=True))
            probs_low = probs.astype(BF16)
            out = nn(probs_low, v).astype(BF16)
            r.attn[:, img, :, cols] = out.reshape(NX, part, 128)
            out_grad = r.cot_all[:, img * part : (img + 1) * part, cols].reshape(image_rows, 128)
            delta = jnp.sum(out_grad.astype(F32) * out.astype(F32), axis=1, keepdims=True)
            score_grads = (probs * (nt(out_grad, v) - delta)).astype(BF16)
            r.proj_grad[at, cols] = (nn(score_grads, k) * scale).astype(BF16)
            r.proj_grad[at, key_cols] = (tn(q, score_grads) * scale).T.astype(BF16)
            r.proj_grad[at, value_cols] = tn(out_grad, probs_low).T.astype(BF16)

    mine = aligned(s * att, att)

    def attn_copy(img, slot):
        start, half = img * part, part // 2
        upper_half, lower_half = pl.ds(start, half), pl.ds(start + half, half)
        source, target, there = (
            (r.attn.at[sr, img], attn_out.at[pl.ds(start, part), mine], right),
            (r.attn.at[sl, img], attn_out.at[pl.ds(start, part), mine], left),
            (r.attn.at[so, img, pl.ds(0, half)], r.stage_l.at[img], right),
            (r.attn.at[so, img, pl.ds(half, half)], r.stage_r.at[img], left),
            (r.stage_l.at[img], attn_out.at[upper_half, aligned(sl * att, att)], right),
            (r.stage_r.at[img], attn_out.at[lower_half, aligned(sr * att, att)], left),
        )[slot]
        return remote(source, target, r.ot_s.at[img], r.ot_r.at[6 * img + slot], there)

    def give(img):
        for slot in (2, 3, 0, 1):
            attn_copy(img, slot).start()
        attn_out[img * part : (img + 1) * part, mine] = r.attn[s, img]

    def pass_on(img):
        for slot in (2, 3):
            attn_copy(img, slot).wait_recv()
            attn_copy(img, slot + 2).start()

    def low_grads(img):
        at = slice(img * image_rows, (img + 1) * image_rows)
        r.low_grad[at, :] = nt(r.proj_grad[at, :], r.up[...]).astype(BF16)

    def grads(img):
        at = slice(img * image_rows, (img + 1) * image_rows)

        @pl.loop(0, width // att)
        def _(n):
            f = aligned(n * att, att)
            grad = nt(r.proj_grad[at, :], r.w[f, :]) + nn(r.low_grad[at, :], r.down[:, f])
            r.pg[img, :, :, f] = grad.astype(BF16).reshape(NX, part, att)
            x = r.tok_all[:, img * part : (img + 1) * part, f].reshape(image_rows, att).astype(F32)
            normed = (x - r.stats[at, 0:1]) * r.stats[at, 1:2]
            r.ip[img : img + 1, f] = jnp.sum(grad, axis=0, keepdims=True)
            r.ip[img : img + 1, aligned(width + n * att, att)] = jnp.sum(grad * normed, axis=0, keepdims=True)

    half = part // 2
    first, second = pl.ds(0, half), pl.ds(half, half)

    def grad_copy(img, slot):
        src, dst, there = (
            (r.pg.at[img, so, first], r.half_l.at[img], right),
            (r.pg.at[img, so, second], r.half_r.at[img], left),
            (r.pg.at[img, sr, second], r.from_l.at[img, second], right),
            (r.pg.at[img, sl, first], r.from_r.at[img, first], left),
            (r.comb_r.at[img], r.from_l.at[img, first], right),
            (r.comb_l.at[img], r.from_r.at[img, second], left),
        )[slot]
        return remote(src, dst, r.gr_s.at[img], r.gr_r.at[6 * img + slot], there)

    def reduce_first(img):
        for slot in range(4):
            grad_copy(img, slot).start()

    def reduce_second(img):
        grad_copy(img, 0).wait_recv()
        r.comb_r[img] = (r.pg[img, sr, 0:half].astype(F32) + r.half_l[img].astype(F32)).astype(BF16)
        grad_copy(img, 4).start()
        grad_copy(img, 1).wait_recv()
        r.comb_l[img] = (r.pg[img, sl, half:part].astype(F32) + r.half_r[img].astype(F32)).astype(BF16)
        grad_copy(img, 5).start()

    project(0)
    cot0.arrived()
    attend(0)
    give(0)
    low_grads(0)
    grads(0)
    reduce_first(0)
    pass_on(0)
    wait_tokens(1)
    normalize(1)
    project(1)
    cot1.arrived()
    attend(1)
    give(1)
    reduce_second(0)
    low_grads(1)

    r.lo[NX - 1 - s, 0] = jnp.zeros((192, 128), BF16)
    up_total = tn(r.low[...], r.proj_grad[...]).astype(BF16)
    for t in range(9):
        r.lo[(4 * (t // 3) + s) // 3, 0, (t % 3) * 64 : (t % 3 + 1) * 64, :] = up_total[:, t * 128 : (t + 1) * 128]
    down_total = tn(r.low_grad[...], r.modded[...]).astype(BF16)
    for t in range(12):
        r.lo[t // 3, 1, (t % 3) * 64 : (t % 3 + 1) * 64, :] = down_total[:, t * 128 : (t + 1) * 128]
    ly = send(
        exchange(me, "dy", NY, lambda i: r.lo.at[(y + i) % NY], lambda i: r.l_y.at[i - 1], r.l_y, r.ly_s, r.ly_r)
    )

    grads(1)
    reduce_first(1)
    pass_on(1)
    for img in range(2):
        for j in range(24):
            at = img * 24 + j
            r.ip_own[at : at + 1, :] = r.ip[img : img + 1, j * 128 : (j + 1) * 128]
    ip = send(exchange(me, "dx", NX, lambda i: r.ip_own, lambda i: r.ip_in.at[i - 1], r.ip_in, r.ip_s, r.ip_r))

    ly.arrived()
    total = r.lo[y].astype(F32)
    for i in range(NY - 1):
        total += r.l_y[i].astype(F32)
    for i in range(NZ):
        at = slice(24 * i, 24 * i + 24)
        r.l_plane[i] = jnp.concatenate([total[0, at], total[1, at]], axis=0).astype(BF16)
    lz = send(
        exchange(
            me, "dz", NZ, lambda i: r.l_plane.at[(z + i) % NZ], lambda i: r.l_z.at[i - 1], r.l_z, r.lz_s, r.lz_r
        )
    )

    ip.arrived()
    ig_all[c, y, z] = (r.ip_own[...] + r.ip_in[0] + r.ip_in[1] + r.ip_in[2]).astype(BF16)
    own_ig = ig_all.at[c, y, z]
    iz = send(
        exchange(me, "dz", NZ, lambda i: own_ig, lambda i: own_ig, ig_all.at[c, y, pl.ds(0, 7)], r.iz_s, r.iz_r)
    )

    lz.arrived()
    total = r.l_plane[z].astype(F32)
    for i in range(NZ - 1):
        total += r.l_z[i].astype(F32)
    r.l_piece[...] = total.astype(BF16)
    r.l_x[NX * c + s] = r.l_piece[...]
    copies = [
        remote(
            r.l_piece, r.l_x.at[NX * c + s], r.lx_s.at[0], r.lx_r.at[0], me.at(dx=i // 2, flip=i % 2 == 1)
        )
        for i in range(1, 2 * NX)
    ]
    lx = send(Batch(me, copies, r.l_x.at[pl.ds(0, 7)], r.lx_s.at[0], r.lx_r.at[0]))

    iz.arrived()
    column = ig_all.at[c, y]
    iy = send(
        exchange(me, "dy", NY, lambda i: column, lambda i: column, ig_all.at[c, pl.ds(0, 3)], r.iy_s, r.iy_r)
    )
    reduce_second(1)

    lx.arrived()
    sums = [r.l_x[i].astype(F32) + r.l_x[NX + i].astype(F32) for i in range(NX)]
    pieces = []
    for i in range(3):
        k = (3 * y + i) % 4
        pieces.append((r.l_x[k].astype(F32) + r.l_x[NX + k].astype(F32))[0:24])
    pieces.append((sums[0] + sums[1] + sums[2] + sums[3])[24:48])
    f_all[z] = jnp.concatenate(pieces, axis=0).astype(BF16)
    lg = send(
        exchange(
            me, "dz", NZ, lambda i: f_all.at[z], lambda i: f_all.at[z], f_all.at[pl.ds(0, 7)], r.lg_s, r.lg_r
        )
    )

    iy.arrived()
    whole_core = ig_all.at[c]
    ic = send(
        Batch(
            me, [remote(whole_core, whole_core, r.ic_s.at[0], r.ic_r.at[0], me.at(flip=True))], whole_core,
            r.ic_s.at[0], r.ic_r.at[0],
        )
    )
    for img in range(2):
        for slot in range(2, 6):
            grad_copy(img, slot).wait_recv()
        grad_out[img * part : (img + 1) * part, :] = (
            r.pg[img, s].astype(F32) + r.from_l[img].astype(F32) + r.from_r[img].astype(F32)
        ).astype(BF16)
    ic.arrived()
    lg.arrived()
    for img in range(2):
        for slot in (0, 1, 4, 5):
            attn_copy(img, slot).wait_recv()
        sent = attn_out.at[pl.ds(img * part, part)]
        remote(sent, sent, r.ot_s.at[img], r.ot_r.at[0], right).wait_send()

    for batch in batches:
        batch.left()
    tokens_sent = r.tok_all.at[pl.ds(0, 3)]
    remote(tokens_sent, tokens_sent, r.tk_s.at[0], r.tk_r.at[0], right).wait_send()
    for img in range(2):
        grads_sent = r.pg.at[img, pl.ds(0, 3)]
        remote(grads_sent, grads_sent, r.gr_s.at[img], r.gr_r.at[0], right).wait_send()
    weights.left()


def whole(counts, tok, cot, cond, wq, up, down, mm):
    return pl.pallas_call(
        whole_kernel,
        out_shape=(
            jax.ShapeDtypeStruct((192, 1536), BF16),
            jax.ShapeDtypeStruct((192, 1536), BF16),
            jax.ShapeDtypeStruct((8, 3072), F32),
            jax.ShapeDtypeStruct((128, 128), BF16),
            jax.ShapeDtypeStruct((NC, NY, NZ, 48, 128), BF16),
            jax.ShapeDtypeStruct((NZ, 96, 128), BF16),
        ),
        in_specs=[pl.BlockSpec(memory_space=pltpu.SMEM), ANY, ANY, VM, VM, ANY, ANY, ANY],
        out_specs=(VM, VM, VM, VM, VM, VM),
        scratch_shapes=scratch_list(),
        compiler_params=pltpu.CompilerParams(
            collective_id=1, has_side_effects=True, vmem_limit_bytes=60 * 1024 * 1024
        ),
        name="whole",
    )(counts, tok, cot, cond, wq, up, down, mm)


def tail_kernel(
    counts, attn, grad, tok, mod, act, ig, pieces,
    attn_out, token_grad, down_out, up_out, mod_grad,
    ig_wide, sorted_grad,
):
    rows, width = tok.shape
    part = rows // 2
    dp = lax.axis_index("dp")
    perm = sorting(counts[0, dp], counts[1, dp], rows)
    attn_out[...] = tn(perm, attn[...]).astype(BF16)
    for img in range(2):
        at = slice(img * part, (img + 1) * part)
        x = nn(perm[at], tok[...])
        centred = x - jnp.mean(x, axis=1, keepdims=True)
        inverse = lax.rsqrt(jnp.mean(centred * centred, axis=1, keepdims=True) + EPSILON)
        normed = centred * inverse
        g = (1.0 + mod[img : img + 1, width:]) * grad[at, :].astype(F32)
        sorted_grad[at, :] = (
            inverse
            * (g - jnp.mean(g, axis=1, keepdims=True) - normed * jnp.mean(g * normed, axis=1, keepdims=True))
        ).astype(BF16)
    token_grad[...] = tn(perm, sorted_grad[...]).astype(BF16)

    ig_wide[...] = ig[...].reshape(3072, 128).astype(F32)
    turned = act[...].astype(F32).T.astype(BF16)[:48]
    for j in range(24):
        parts = [ig_wide[pl.ds(img * 24 + j, 64, stride=48), :].astype(BF16) for img in range(2)]
        mod_grad[:, j * 128 : (j + 1) * 128] = nn(turned, jnp.concatenate(parts, axis=0))

    place = dp % (NZ * NC)
    flat = pieces[...].astype(F32)

    def tiles(i):
        triple = jnp.concatenate([flat[k, 24 * i : 24 * i + 24] for k in range(NZ)], axis=0).astype(BF16)
        return [triple[j * 64 : (j + 1) * 64] for j in range(3)]

    row = lax.broadcasted_iota(jnp.int32, (128, 128), 0)
    col = lax.broadcasted_iota(jnp.int32, (128, 128), 1)
    total = jnp.zeros((64, 128), F32)
    for i, tile in enumerate(tiles(0) + tiles(1) + tiles(2)):
        total += nn(tile, jnp.where(row + 128 * i == col + 72 * place, 1.0, 0.0).astype(BF16))
    up_out[...] = total[:, :72]
    total = jnp.zeros((128, 64), F32)
    for i, tile in enumerate(tiles(3)):
        total += nt(jnp.where(col + 128 * i == row + 24 * place, 1.0, 0.0).astype(BF16), tile)
    down_out[...] = total[:24]


def tail(counts, attn, grad, tok, mod, act, ig, pieces):
    return pl.pallas_call(
        tail_kernel,
        out_shape=(
            jax.ShapeDtypeStruct((192, 1536), BF16),
            jax.ShapeDtypeStruct((192, 1536), BF16),
            jax.ShapeDtypeStruct((24, 64), F32),
            jax.ShapeDtypeStruct((64, 72), F32),
            jax.ShapeDtypeStruct((48, 3072), F32),
        ),
        in_specs=[pl.BlockSpec(memory_space=pltpu.SMEM)] + [VM] * 7,
        out_specs=(VM, VM, VM, VM, VM),
        scratch_shapes=[pltpu.VMEM((3072, 128), F32), pltpu.VMEM((192, 1536), BF16)],
        compiler_params=pltpu.CompilerParams(vmem_limit_bytes=60 * 1024 * 1024),
        name="tail",
    )(counts, attn, grad, tok, mod, act, ig, pieces)


def body(
    tokens,
    cotangent,
    condition,
    per_image_rows,
    query_key_value_weight,
    adapter_down,
    adapter_up,
    modulation_matrix,
):
    counts = per_image_rows.T
    attn, grad, mod, act, ig, pieces = whole(
        counts,
        tokens[0],
        cotangent[0],
        condition[0],
        query_key_value_weight,
        adapter_up,
        adapter_down.T,
        modulation_matrix,
    )
    attention, token_grad, down_grad, up_grad, mod_grad = tail(
        counts, attn, grad, tokens[0], mod, act, ig, pieces
    )
    return attention[None], token_grad[None], down_grad, up_grad, mod_grad


def solution(mesh):
    in_specs = (
        P("dp", "seq", None),
        P("dp", "seq", None),
        P("dp", None, None),
        P(),
        P("dp", None),
        P(),
        P(),
        P("dp", None),
    )
    out_specs = (
        P("dp", "seq", None),
        P("dp", "seq", None),
        P("dp", None),
        P(None, "dp"),
        P("dp", None),
    )
    return jax.shard_map(body, mesh=mesh, in_specs=in_specs, out_specs=out_specs, check_vma=False)
```

```python
import jax
import jax.numpy as jnp
from jax import lax
from jax.experimental import pallas as pl
from jax.experimental.pallas import tpu as pltpu
from jax.sharding import PartitionSpec as P

HEAD_SIZE = 128
EPSILON = 1e-06
MASKED = -1e30
MESH = pl.DeviceIdType.MESH
NX, NY, NZ, NC = 4, 4, 8, 2
F32, BF16 = jnp.float32, jnp.bfloat16
ANY = pl.BlockSpec(memory_space=pl.ANY)
VM = pl.BlockSpec(memory_space=pltpu.VMEM)


def remote(src, dst, send_sem, recv_sem, device):
    return pltpu.make_async_remote_copy(
        src_ref=src,
        dst_ref=dst,
        send_sem=send_sem,
        recv_sem=recv_sem,
        device_id=device,
        device_id_type=MESH,
    )


class Place:
    def __init__(self):
        self.dp = lax.axis_index("dp")
        self.s = lax.axis_index("seq")
        self.y = self.dp // (NZ * NC)
        self.z = (self.dp // NC) % NZ
        self.c = self.dp % NC

    def at(self, dx=0, dy=0, dz=0, flip=False):
        s = (self.s + dx) % NX if dx else self.s
        y = (self.y + dy) % NY if dy else self.y
        z = (self.z + dz) % NZ if dz else self.z
        c = 1 - self.c if flip else self.c
        return (y * (NZ * NC) + z * NC + c, s)


def peers_of(me):
    peers = [me.at(dx=i) for i in range(1, NX)]
    peers += [me.at(dx=i, flip=True) for i in range(1, NX)]
    peers += [me.at(dy=i) for i in range(1, NY)]
    peers += [me.at(dz=i) for i in range(1, NZ)]
    peers += [me.at(dy=i, flip=True) for i in range(NY)]
    return peers


def greet(me):
    for peer in peers_of(me):
        pl.semaphore_signal(pltpu.get_barrier_semaphore(), inc=1, device_id=peer, device_id_type=MESH)


def enter(me):
    pl.semaphore_wait(pltpu.get_barrier_semaphore(), len(peers_of(me)))


HALF = 112


class Batch:
    def __init__(self, me, copies, sample, send, recv):
        self.all = remote(sample, sample, send, recv, me.at(dx=1))
        for copy in copies:
            copy.start()

    def arrived(self):
        self.all.wait_recv()

    def left(self):
        self.all.wait_send()


class RowGather:
    def __init__(self, me, buf, ysend, yrecv, zsend, zrecv):
        self.me, self.buf = me, buf
        self.ysend, self.yrecv = ysend.at[0], yrecv.at[0]
        self.zsend, self.zrecv = zsend.at[0], zrecv

    def start_y(self):
        me = self.me
        own = self.buf.at[me.c, me.z, me.y, pl.ds(0, HALF)]
        copies = [remote(own, own, self.ysend, self.yrecv, me.at(dy=i)) for i in range(1, NY)]
        sample = self.buf.at[me.c, me.z, pl.ds(0, 3), pl.ds(0, HALF)]
        self.first = Batch(me, copies, sample, self.ysend, self.yrecv)

    def ring(self, way, step, arriving):
        me = self.me
        far = step if arriving else step - 1
        source = (me.z + NZ - far) % NZ if way == 0 else (me.z + far) % NZ
        ys = pl.ds(0, NY) if step < 4 else pl.ds(2 * way, 2)
        block = self.buf.at[me.c, source, ys, pl.ds(0, HALF)]
        there = me.at(dz=1) if way == 0 else me.at(dz=NZ - 1)
        return remote(block, block, self.zsend, self.zrecv.at[way * 4 + step - 1], there)

    def step(self, step):
        for way in (0, 1):
            if step > 1:
                self.ring(way, step - 1, True).wait_recv()
            if step <= 4:
                self.ring(way, step, False).start()

    def left(self):
        me = self.me
        self.first.left()
        sample = self.buf.at[me.c, pl.ds(0, 7), pl.ds(0, NY), pl.ds(0, HALF)]
        remote(sample, sample, self.zsend, self.zrecv.at[0], me.at(dz=1)).wait_send()


class ColumnGather:
    def __init__(self, me, buf, zsend, zrecv, ysend, yrecv):
        self.me, self.buf = me, buf
        self.ysend, self.yrecv = ysend.at[0], yrecv
        self.zsend, self.zrecv = zsend.at[0], zrecv

    def block(self, shift, ys):
        return self.buf.at[self.me.c, (self.me.z + shift) % NZ, ys, pl.ds(HALF, HALF)]

    def ring(self, way, step, arriving):
        far = step if arriving else step - 1
        block = self.block((NZ - far) % NZ if way == 0 else far, self.me.y)
        there = self.me.at(dz=1) if way == 0 else self.me.at(dz=NZ - 1)
        return remote(block, block, self.zsend, self.zrecv.at[way * 4 + step - 1], there)

    def spread(self, shift):
        block = self.block(shift, self.me.y)
        for i in range(1, NY):
            remote(block, block, self.ysend, self.yrecv.at[shift], self.me.at(dy=i)).start()

    def wait_spread(self, shift):
        sample = self.block(shift, pl.ds(0, 3))
        remote(sample, sample, self.ysend, self.yrecv.at[shift], self.me.at(dy=1)).wait_recv()

    def step(self, step):
        for way in (0, 1):
            last = 4 - way
            if 1 < step <= last + 1:
                self.ring(way, step - 1, True).wait_recv()
            if step <= last:
                self.ring(way, step, False).start()
        if step == 1:
            self.spread(0)
        else:
            self.spread(NZ - step + 1)
            if step < 5:
                self.spread(step - 1)

    def left(self):
        me = self.me
        sample = self.buf.at[me.c, pl.ds(0, 7), 0, pl.ds(HALF, HALF)]
        remote(sample, sample, self.zsend, self.zrecv.at[0], me.at(dz=1)).wait_send()
        sample = self.buf.at[me.c, pl.ds(0, NZ), pl.ds(0, 3), pl.ds(HALF, HALF)]
        remote(sample, sample, self.ysend, self.yrecv.at[0], me.at(dy=1)).wait_send()


class CoreSwap:
    def __init__(self, me, buf, send, recv):
        self.me, self.buf, self.send, self.recv = me, buf, send.at[0], recv

    def copy(self, at_c, shift):
        block = self.buf.at[at_c, (self.me.z + shift) % NZ]
        return remote(block, block, self.send, self.recv.at[shift], self.me.at(flip=True))

    def start(self, shift):
        self.copy(self.me.c, shift).start()

    def wait(self, shift):
        self.copy(1 - self.me.c, shift).wait_recv()

    def left(self):
        block = self.buf.at[self.me.c]
        remote(block, block, self.send, self.recv.at[0], self.me.at(flip=True)).wait_send()


def exchange(me, axis, count, source, target, sample, send, recv):
    copies = [
        remote(source(i), target(i), send.at[0], recv.at[0], me.at(**{axis: i})) for i in range(1, count)
    ]
    return Batch(me, copies, sample, send.at[0], recv.at[0])

def nt(a, b):
    return lax.dot_general(a, b, (((1,), (1,)), ((), ())), preferred_element_type=F32)


def tn(a, b):
    return lax.dot_general(a, b, (((0,), (0,)), ((), ())), preferred_element_type=F32)


def nn(a, b):
    return jnp.dot(a, b, preferred_element_type=F32)


def sorting(c0, c1, rows):
    here = lax.broadcasted_iota(jnp.int32, (rows, rows), 0)
    source = lax.broadcasted_iota(jnp.int32, (rows, rows), 1)
    later = here >= rows // 2
    rank = jnp.where(later, here - rows // 2, here)
    live = rank < jnp.where(later, c1, c0)
    return jnp.where((source == rank + jnp.where(later, c0, 0)) & live, 1.0, 0.0).astype(BF16)


def aligned(start, size):
    return pl.ds(pl.multiple_of(start, 128), size)


class Refs:
    pass


SCRATCH = dict(
    tok_raw=pltpu.VMEM((192, 1536), BF16),
    cot_raw=pltpu.VMEM((192, 1536), BF16),
    tok_all=pltpu.VMEM((NX, 192, 1536), BF16),
    cot_all=pltpu.VMEM((NX, 192, 384), BF16),
    w_all=pltpu.VMEM((NC, NZ, NY, 224, 128), BF16),
    w=pltpu.VMEM((1536, 1152), BF16),
    up=pltpu.VMEM((64, 1152), BF16),
    down=pltpu.VMEM((64, 1536), BF16),
    mm=pltpu.VMEM((256, 768), BF16),
    a_rows=pltpu.VMEM((NZ, 16, 128), F32),
    a_src=pltpu.VMEM((NZ, 16, 128), BF16),
    a_z=pltpu.VMEM((NZ, 16, 128), BF16),
    a_turn=pltpu.VMEM((NY, 32, 128), F32),
    a_low=pltpu.VMEM((NY, 32, 128), BF16),
    a_y=pltpu.VMEM((NC * NY, 32, 128), BF16),
    a_wide=pltpu.VMEM((256, 128), F32),
    a_pair=pltpu.VMEM((128, 256), BF16),
    part_wide=pltpu.VMEM((768, 128), F32),
    part_low=pltpu.VMEM((NC, NY, 96, 128), BF16),
    m_in=pltpu.VMEM((7, 96, 128), BF16),
    m_plane=pltpu.VMEM((NZ, 16, 128), F32),
    m_z=pltpu.VMEM((NZ - 1, 16, 128), F32),
    m_own=pltpu.VMEM((16, 128), F32),
    m_all=pltpu.VMEM((NX, 16, 128), F32),
    modded=pltpu.VMEM((768, 1536), BF16),
    stats=pltpu.VMEM((768, 128), F32),
    low=pltpu.VMEM((768, 64), BF16),
    proj=pltpu.VMEM((768, 1152), BF16),
    proj_grad=pltpu.VMEM((768, 1152), BF16),
    low_grad=pltpu.VMEM((768, 64), BF16),
    cot_own=pltpu.VMEM((192, 1536), BF16),
    attn=pltpu.VMEM((NX, 2, 96, 384), BF16),
    pg=pltpu.VMEM((2, NX, 96, 1536), BF16),
    ip=pltpu.VMEM((8, 3072), F32),
    half_l=pltpu.VMEM((2, 48, 1536), BF16),
    half_r=pltpu.VMEM((2, 48, 1536), BF16),
    comb_l=pltpu.VMEM((2, 48, 1536), BF16),
    comb_r=pltpu.VMEM((2, 48, 1536), BF16),
    from_l=pltpu.VMEM((2, 96, 1536), BF16),
    from_r=pltpu.VMEM((2, 96, 1536), BF16),
    ip_own=pltpu.VMEM((48, 128), F32),
    ip_in=pltpu.VMEM((3, 48, 128), F32),
    lo=pltpu.VMEM((NY, 2, 192, 128), BF16),
    l_y=pltpu.VMEM((NY - 1, 2, 192, 128), BF16),
    l_plane=pltpu.VMEM((NZ, 48, 128), BF16),
    l_z=pltpu.VMEM((NZ - 1, 48, 128), BF16),
    l_piece=pltpu.VMEM((48, 128), BF16),
    l_x=pltpu.VMEM((NC * NX, 48, 128), BF16),
)
PAIRS = dict(
    tk=(1, 12), ck=(2, 2), az=(1, 1), ay=(1, 1), my=(1, 1), mz=(1, 1), mx=(1, 1), gr=(2, 12), ot=(2, 2),
    ip=(1, 1), iz=(1, 1), iy=(1, 1), ic=(1, 1), ly=(1, 1), lz=(1, 1), lx=(1, 1), lg=(1, 1),
)
PLANES = dict(wy=(1, 1), wz=(1, 8), vz=(1, 8), vy=(1, 8), wc=(1, 8))
LOCAL = 8


def scratch_list():
    dma = pltpu.SemaphoreType.DMA
    out = list(SCRATCH.values())
    for send, recv in list(PAIRS.values()) + list(PLANES.values()):
        out += [dma((send,)), dma((recv,))]
    return out + [dma((LOCAL,))]


def named(refs):
    r = Refs()
    refs = list(refs)
    for name in SCRATCH:
        setattr(r, name, refs.pop(0))
    for name in PAIRS:
        setattr(r, name + "_s", refs.pop(0))
        setattr(r, name + "_r", refs.pop(0))
    for name in PLANES:
        setattr(r, name, [refs.pop(0), refs.pop(0)])
    r.local = refs.pop(0)
    return r


def whole_kernel(
    rows_ref, tok, cot, cond, wq, up_in, down_in, mm_in,
    attn_out, grad_out, mod, a_own, ig_all, f_all,
    *refs,
):
    r = named(refs)
    me = Place()
    s, y, z, c = me.s, me.y, me.z, me.c
    rows, width, att, heads = 192, 1536, 384, 3
    part = rows // 2
    image_rows = NX * part
    chunk = rows // 4
    scale = HEAD_SIZE ** (-0.5)
    right, left = me.at(dx=1), me.at(dx=NX - 1)
    sl, sr, so = (s + NX - 1) % NX, (s + 1) % NX, (s + 2) % NX
    c0, c1 = rows_ref[0, me.dp], rows_ref[1, me.dp]

    greet(me)
    offset = 48 * me.dp - 128 * ((96 * (me.dp // 2)) // 128)
    r.mm[...] = jnp.zeros_like(r.mm)
    raw_tok = pltpu.make_async_copy(tok, r.tok_raw, r.local.at[5])
    raw_tok.start()
    raw_cot = pltpu.make_async_copy(cot, r.cot_raw, r.local.at[6])
    raw_cot.start()
    locals_ = [
        pltpu.make_async_copy(
            mm_in.at[:, aligned(s * 768, 768)], r.mm.at[pl.ds(pl.multiple_of(offset, 16), 48)], r.local.at[0]
        ),
        pltpu.make_async_copy(down_in, r.down, r.local.at[1]),
    ]
    for b in range(3):
        locals_.append(
            pltpu.make_async_copy(
                up_in.at[:, aligned(b * width + s * att, att)], r.up.at[:, b * att : (b + 1) * att], r.local.at[2 + b]
            )
        )
    for copy in locals_:
        copy.start()
    pieces = []
    for b in range(3):
        block = wq[:, aligned(b * width + s * att, att)].astype(F32)
        pieces += [block[:, i * 128 : (i + 1) * 128] for i in range(3)]
    pieces.append(jnp.zeros((8, 128), F32))
    r.w_all[c, z, y] = jnp.concatenate(pieces, axis=0).astype(BF16)
    wide = cond[...].astype(F32)
    wide = (wide / (1.0 + jnp.exp(-wide))).astype(BF16).astype(F32)
    r.a_rows[...] = jnp.zeros_like(r.a_rows)
    for p in range(NZ * NY):
        j = (96 * p) // 128
        for img in range(2):
            for t in range(2):
                if j + t < 24:
                    at = 4 * (p // NZ) + 2 * img + t
                    r.a_rows[p % NZ, at : at + 1, :] = wide[img : img + 1, (j + t) * 128 : (j + t + 1) * 128]
    r.a_src[...] = r.a_rows[...].astype(BF16)
    r.a_z[z] = r.a_src[z]
    r.m_plane[...] = jnp.zeros_like(r.m_plane)
    perm = sorting(c0, c1, rows)
    raw_tok.wait()
    r.tok_all[s] = nn(perm, r.tok_raw[...]).astype(BF16)

    enter(me)

    batches = []

    def send(batch):
        batches.append(batch)
        return batch

    def row_chunk(i):
        return pl.ds(i * chunk, chunk)

    def token_copy(source, owner, i, slot, there):
        return remote(source, r.tok_all.at[owner, row_chunk(i)], r.tk_s.at[0], r.tk_r.at[slot], there)

    def own_tokens(img):
        i = 2 * img
        token_copy(r.tok_all.at[s, row_chunk(i)], s, i, i, right).start()
        token_copy(r.tok_all.at[s, row_chunk(i + 1)], s, i + 1, 4 + i + 1, left).start()
        token_copy(r.tok_all.at[s, row_chunk(i + 1)], s, i + 1, i + 1, right).start()
        token_copy(r.tok_all.at[s, row_chunk(i)], s, i, 4 + i, left).start()

    def forward(img):
        i = 2 * img
        token_copy(r.tok_all.at[s, row_chunk(i)], sl, i, i, right).wait_recv()
        token_copy(r.tok_all.at[sl, row_chunk(i)], sl, i, 8 + i, right).start()
        i = i + 1
        token_copy(r.tok_all.at[s, row_chunk(i)], sr, i, 4 + i, left).wait_recv()
        token_copy(r.tok_all.at[sr, row_chunk(i)], sr, i, 8 + i, left).start()

    def wait_tokens(img):
        i = 2 * img
        own = r.tok_all.at[s, row_chunk(i)]
        token_copy(own, sl, i + 1, i + 1, right).wait_recv()
        token_copy(own, sr, i, 4 + i, left).wait_recv()
        token_copy(own, so, i, 8 + i, right).wait_recv()
        token_copy(own, so, i + 1, 8 + i + 1, left).wait_recv()

    def own_cotangent(img):
        at = pl.ds(img * part, part)
        copies = [
            remote(
                r.cot_own.at[at, aligned(((s + i) % NX) * att, att)], r.cot_all.at[s, at],
                r.ck_s.at[img], r.ck_r.at[img], me.at(dx=i),
            )
            for i in range(1, NX)
        ]
        return send(Batch(me, copies, r.cot_all.at[pl.ds(0, 3), at], r.ck_s.at[img], r.ck_r.at[img]))

    weights = RowGather(me, r.w_all, *r.wy, *r.wz)
    weights.start_y()
    az = send(
        exchange(
            me, "dz", NZ, lambda i: r.a_src.at[(z + i) % NZ], lambda i: r.a_z.at[z], r.a_z.at[pl.ds(0, 7)],
            r.az_s, r.az_r,
        )
    )
    others = ColumnGather(me, r.w_all, *r.vz, *r.vy)
    others.step(1)
    swap = CoreSwap(me, r.w_all, *r.wc)
    own_tokens(0)
    raw_cot.wait()
    r.cot_own[...] = nn(perm, r.cot_raw[...]).astype(BF16)
    weights.first.arrived()
    weights.step(1)
    az.arrived()
    turned = r.a_z[...].astype(F32)
    for at_y in range(NY):
        for at_z in range(NZ):
            r.a_turn[at_y, 4 * at_z : 4 * at_z + 4, :] = turned[at_z, 4 * at_y : 4 * at_y + 4]
    r.a_low[...] = r.a_turn[...].astype(BF16)
    r.a_y[NY * c + y] = r.a_low[y]

    def plane_exchange(source, target, sample, send_sem, recv_sem):
        copies = []
        for i in range(1, 2 * NY):
            dy, flip = i // 2, i % 2 == 1
            there = (y + dy) % NY
            at = (1 - c) if flip else c
            copies.append(
                remote(source(at, there), target(i - 1), send_sem.at[0], recv_sem.at[0], me.at(dy=dy, flip=flip))
            )
        return send(Batch(me, copies, sample, send_sem.at[0], recv_sem.at[0]))

    ay = plane_exchange(
        lambda at, there: r.a_low.at[there], lambda i: r.a_y.at[NY * c + y], r.a_y.at[pl.ds(0, 7)], r.ay_s, r.ay_r
    )
    others.step(2)
    ay.arrived()
    locals_[0].wait()
    r.a_wide[...] = r.a_y[...].reshape(256, 128).astype(F32)
    for img in range(2):
        for t in range(2):
            r.a_pair[img * 64 : (img + 1) * 64, t * 128 : (t + 1) * 128] = r.a_wide[
                pl.ds(2 * img + t, 64, stride=4), :
            ].astype(BF16)
    for j in range(6):
        columns = nn(r.a_pair[...], r.mm[:, j * 128 : (j + 1) * 128])
        for img in range(2):
            r.part_wide[pl.ds(img * 6 + j, 64, stride=12), :] = columns[img * 64 : (img + 1) * 64]
    r.part_low[...] = r.part_wide[...].astype(BF16).reshape(r.part_low.shape)
    my = plane_exchange(
        lambda at, there: r.part_low.at[at, there], lambda i: r.m_in.at[i], r.m_in, r.my_s, r.my_r
    )
    weights.step(2)
    forward(0)
    cot0 = own_cotangent(0)
    own_tokens(1)
    others.step(3)
    row = lax.broadcasted_iota(jnp.int32, (256, 128), 0)
    col = lax.broadcasted_iota(jnp.int32, (256, 128), 1)
    pick = jnp.where((row == col + offset) & (col < 48), 1.0, 0.0).astype(BF16)
    a_own[...] = nn(r.a_pair[...], pick).astype(BF16)
    r.cot_all[s] = r.cot_own[:, aligned(s * att, att)]
    my.arrived()
    total = r.part_low[c, y].astype(F32)
    for i in range(7):
        total += r.m_in[i].astype(F32)
    for at_z in range(NZ):
        r.m_plane[at_z, 0:12, :] = total[12 * at_z : 12 * at_z + 12]
    mz = send(
        exchange(
            me, "dz", NZ, lambda i: r.m_plane.at[(z + i) % NZ], lambda i: r.m_z.at[i - 1], r.m_z, r.mz_s, r.mz_r
        )
    )
    def place(shift):
        swap.wait(shift)
        at_z = (z + shift) % NZ

        @pl.loop(0, NY)
        def _(at_y):
            first = r.w_all[0, at_z, at_y].astype(F32)
            other = r.w_all[1, at_z, at_y].astype(F32)
            at = pl.ds(pl.multiple_of(48 * (NZ * at_y + at_z), 16), 48)
            for t in range(9):
                both = jnp.concatenate([first[24 * t : 24 * t + 24], other[24 * t : 24 * t + 24]], axis=0)
                r.w[at, t * 128 : (t + 1) * 128] = both.astype(BF16)

    weights.step(3)
    others.step(4)
    for shift in (0, 1, NZ - 1):
        others.wait_spread(shift)
        swap.start(shift)
    mz.arrived()
    total = r.m_plane[z]
    for i in range(NZ - 1):
        total += r.m_z[i]
    r.m_own[...] = total
    r.m_all[s] = total
    mx = send(
        exchange(
            me, "dx", NX, lambda i: r.m_own, lambda i: r.m_all.at[s], r.m_all.at[pl.ds(0, 3)], r.mx_s, r.mx_r
        )
    )
    weights.step(4)
    others.step(5)
    for shift in (2, NZ - 2):
        others.wait_spread(shift)
        swap.start(shift)
    for shift in (0, 1, NZ - 1):
        place(shift)

    mx.arrived()
    mod[...] = jnp.zeros_like(mod)
    for k in range(NX):
        for img in range(2):
            for j in range(6):
                at = 768 * k + 128 * j
                mod[img : img + 1, at : at + 128] = r.m_all[k, img * 6 + j : img * 6 + j + 1, :]

    def normalize(img):
        @pl.loop(0, NX)
        def _(block):
            x = r.tok_all[block, img * part : (img + 1) * part, :].astype(F32)
            mean = jnp.mean(x, axis=1, keepdims=True)
            centred = x - mean
            inverse = lax.rsqrt(jnp.mean(centred * centred, axis=1, keepdims=True) + EPSILON)
            rank = lax.broadcasted_iota(jnp.int32, (part, 1), 0)
            gain = 1.0 + mod[img : img + 1, width:]
            value = gain * (centred * inverse) + mod[img : img + 1, :width]
            at = pl.ds(pl.multiple_of(img * image_rows + block * part, 32), part)
            r.modded[at, :] = jnp.where(rank < (c0, c1)[img], value, 0.0).astype(BF16)
            r.stats[at, 0:1] = mean
            r.stats[at, 1:2] = inverse

    weights.step(5)
    for shift in (3, 5, 4):
        others.wait_spread(shift)
        swap.start(shift)
    wait_tokens(0)
    normalize(0)
    forward(1)
    cot1 = own_cotangent(1)
    for shift in (2, NZ - 2, 3, 5, 4):
        place(shift)
    for copy in locals_[1:]:
        copy.wait()

    def project(img):
        at = slice(img * image_rows, (img + 1) * image_rows)
        r.low[at, :] = nt(r.modded[at, :], r.down[...]).astype(BF16)

        @pl.loop(0, 3)
        def _(n):
            cols = aligned(n * att, att)
            r.proj[at, cols] = (nn(r.modded[at, :], r.w[:, cols]) + nn(r.low[at, :], r.up[:, cols])).astype(BF16)

    lane = lax.broadcasted_iota(jnp.int32, (1, image_rows), 1)
    for _ in range(NX - 1):
        lane = jnp.where(lane >= part, lane - part, lane)

    def attend(img):
        at = slice(img * image_rows, (img + 1) * image_rows)
        allowed = lane < (c0, c1)[img]
        for h in range(heads):
            cols = slice(h * 128, (h + 1) * 128)
            key_cols = slice(att + h * 128, att + (h + 1) * 128)
            value_cols = slice(2 * att + h * 128, 2 * att + (h + 1) * 128)
            q, k, v = r.proj[at, cols], r.proj[at, key_cols], r.proj[at, value_cols]
            scores = jnp.where(allowed, nt(q, k), MASKED)
            largest = jnp.max(scores, axis=1, keepdims=True)
            raw = jnp.exp((scores - largest) * scale)
            probs = raw * (1.0 / jnp.sum(raw, axis=1, keepdims=True))
            probs_low = probs.astype(BF16)
            out = nn(probs_low, v).astype(BF16)
            r.attn[:, img, :, cols] = out.reshape(NX, part, 128)
            out_grad = r.cot_all[:, img * part : (img + 1) * part, cols].reshape(image_rows, 128)
            delta = jnp.sum(out_grad.astype(F32) * out.astype(F32), axis=1, keepdims=True)
            score_grads = (probs * (nt(out_grad, v) - delta)).astype(BF16)
            r.proj_grad[at, cols] = (nn(score_grads, k) * scale).astype(BF16)
            r.proj_grad[at, key_cols] = (tn(q, score_grads) * scale).T.astype(BF16)
            r.proj_grad[at, value_cols] = tn(out_grad, probs_low).T.astype(BF16)

    mine = aligned(s * att, att)

    def give(img):
        at = slice(img * part, (img + 1) * part)
        copies = [
            remote(
                r.attn.at[(s + i) % NX, img], attn_out.at[at, mine], r.ot_s.at[img], r.ot_r.at[img], me.at(dx=i)
            )
            for i in range(1, NX)
        ]
        attn_out[at, mine] = r.attn[s, img]
        return send(Batch(me, copies, attn_out.at[at, pl.ds(0, 3 * att)], r.ot_s.at[img], r.ot_r.at[img]))

    def low_grads(img):
        at = slice(img * image_rows, (img + 1) * image_rows)
        r.low_grad[at, :] = nt(r.proj_grad[at, :], r.up[...]).astype(BF16)

    def grads(img):
        at = slice(img * image_rows, (img + 1) * image_rows)

        @pl.loop(0, width // att)
        def _(n):
            f = aligned(n * att, att)
            grad = nt(r.proj_grad[at, :], r.w[f, :]) + nn(r.low_grad[at, :], r.down[:, f])
            r.pg[img, :, :, f] = grad.astype(BF16).reshape(NX, part, att)
            x = r.tok_all[:, img * part : (img + 1) * part, f].reshape(image_rows, att).astype(F32)
            normed = (x - r.stats[at, 0:1]) * r.stats[at, 1:2]
            r.ip[img : img + 1, f] = jnp.sum(grad, axis=0, keepdims=True)
            r.ip[img : img + 1, aligned(width + n * att, att)] = jnp.sum(grad * normed, axis=0, keepdims=True)

    half = part // 2
    first, second = pl.ds(0, half), pl.ds(half, half)

    def grad_copy(img, slot):
        src, dst, there = (
            (r.pg.at[img, so, first], r.half_l.at[img], right),
            (r.pg.at[img, so, second], r.half_r.at[img], left),
            (r.pg.at[img, sr, second], r.from_l.at[img, second], right),
            (r.pg.at[img, sl, first], r.from_r.at[img, first], left),
            (r.comb_r.at[img], r.from_l.at[img, first], right),
            (r.comb_l.at[img], r.from_r.at[img, second], left),
        )[slot]
        return remote(src, dst, r.gr_s.at[img], r.gr_r.at[6 * img + slot], there)

    def reduce_first(img):
        for slot in range(4):
            grad_copy(img, slot).start()

    def reduce_second(img):
        grad_copy(img, 0).wait_recv()
        r.comb_r[img] = (r.pg[img, sr, 0:half].astype(F32) + r.half_l[img].astype(F32)).astype(BF16)
        grad_copy(img, 4).start()
        grad_copy(img, 1).wait_recv()
        r.comb_l[img] = (r.pg[img, sl, half:part].astype(F32) + r.half_r[img].astype(F32)).astype(BF16)
        grad_copy(img, 5).start()

    project(0)
    cot0.arrived()
    attend(0)
    out0 = give(0)
    low_grads(0)
    grads(0)
    reduce_first(0)
    wait_tokens(1)
    normalize(1)
    project(1)
    cot1.arrived()
    attend(1)
    out1 = give(1)
    reduce_second(0)
    low_grads(1)

    r.lo[NX - 1 - s, 0] = jnp.zeros((192, 128), BF16)
    up_total = tn(r.low[...], r.proj_grad[...]).astype(BF16)
    for t in range(9):
        r.lo[(4 * (t // 3) + s) // 3, 0, (t % 3) * 64 : (t % 3 + 1) * 64, :] = up_total[:, t * 128 : (t + 1) * 128]
    down_total = tn(r.low_grad[...], r.modded[...]).astype(BF16)
    for t in range(12):
        r.lo[t // 3, 1, (t % 3) * 64 : (t % 3 + 1) * 64, :] = down_total[:, t * 128 : (t + 1) * 128]
    ly = send(
        exchange(me, "dy", NY, lambda i: r.lo.at[(y + i) % NY], lambda i: r.l_y.at[i - 1], r.l_y, r.ly_s, r.ly_r)
    )

    grads(1)
    reduce_first(1)
    for img in range(2):
        for j in range(24):
            at = img * 24 + j
            r.ip_own[at : at + 1, :] = r.ip[img : img + 1, j * 128 : (j + 1) * 128]
    ip = send(exchange(me, "dx", NX, lambda i: r.ip_own, lambda i: r.ip_in.at[i - 1], r.ip_in, r.ip_s, r.ip_r))

    ly.arrived()
    total = r.lo[y].astype(F32)
    for i in range(NY - 1):
        total += r.l_y[i].astype(F32)
    for i in range(NZ):
        at = slice(24 * i, 24 * i + 24)
        r.l_plane[i] = jnp.concatenate([total[0, at], total[1, at]], axis=0).astype(BF16)
    lz = send(
        exchange(
            me, "dz", NZ, lambda i: r.l_plane.at[(z + i) % NZ], lambda i: r.l_z.at[i - 1], r.l_z, r.lz_s, r.lz_r
        )
    )

    ip.arrived()
    ig_all[c, y, z] = (r.ip_own[...] + r.ip_in[0] + r.ip_in[1] + r.ip_in[2]).astype(BF16)
    own_ig = ig_all.at[c, y, z]
    iz = send(
        exchange(me, "dz", NZ, lambda i: own_ig, lambda i: own_ig, ig_all.at[c, y, pl.ds(0, 7)], r.iz_s, r.iz_r)
    )

    reduce_second(1)
    lz.arrived()
    total = r.l_plane[z].astype(F32)
    for i in range(NZ - 1):
        total += r.l_z[i].astype(F32)
    r.l_piece[...] = total.astype(BF16)
    r.l_x[NX * c + s] = r.l_piece[...]
    copies = [
        remote(
            r.l_piece, r.l_x.at[NX * c + s], r.lx_s.at[0], r.lx_r.at[0], me.at(dx=i // 2, flip=i % 2 == 1)
        )
        for i in range(1, 2 * NX)
    ]
    lx = send(Batch(me, copies, r.l_x.at[pl.ds(0, 7)], r.lx_s.at[0], r.lx_r.at[0]))

    iz.arrived()
    column = ig_all.at[c, y]
    iy = send(
        exchange(me, "dy", NY, lambda i: column, lambda i: column, ig_all.at[c, pl.ds(0, 3)], r.iy_s, r.iy_r)
    )
    lx.arrived()
    sums = [r.l_x[i].astype(F32) + r.l_x[NX + i].astype(F32) for i in range(NX)]
    pieces = []
    for i in range(3):
        k = (3 * y + i) % 4
        pieces.append((r.l_x[k].astype(F32) + r.l_x[NX + k].astype(F32))[0:24])
    pieces.append((sums[0] + sums[1] + sums[2] + sums[3])[24:48])
    f_all[z] = jnp.concatenate(pieces, axis=0).astype(BF16)
    lg = send(
        exchange(
            me, "dz", NZ, lambda i: f_all.at[z], lambda i: f_all.at[z], f_all.at[pl.ds(0, 7)], r.lg_s, r.lg_r
        )
    )

    iy.arrived()
    whole_core = ig_all.at[c]
    ic = send(
        Batch(
            me, [remote(whole_core, whole_core, r.ic_s.at[0], r.ic_r.at[0], me.at(flip=True))], whole_core,
            r.ic_s.at[0], r.ic_r.at[0],
        )
    )
    for img in range(2):
        for slot in range(2, 6):
            grad_copy(img, slot).wait_recv()
        grad_out[img * part : (img + 1) * part, :] = (
            r.pg[img, s].astype(F32) + r.from_l[img].astype(F32) + r.from_r[img].astype(F32)
        ).astype(BF16)
    ic.arrived()
    lg.arrived()
    out0.arrived()
    out1.arrived()

    for batch in batches:
        batch.left()
    tokens_sent = r.tok_all.at[pl.ds(0, 3)]
    remote(tokens_sent, tokens_sent, r.tk_s.at[0], r.tk_r.at[0], right).wait_send()
    for img in range(2):
        grads_sent = r.pg.at[img, pl.ds(0, 3)]
        remote(grads_sent, grads_sent, r.gr_s.at[img], r.gr_r.at[0], right).wait_send()
    weights.left()
    others.left()
    swap.left()


def whole(counts, tok, cot, cond, wq, up, down, mm):
    return pl.pallas_call(
        whole_kernel,
        out_shape=(
            jax.ShapeDtypeStruct((192, 1536), BF16),
            jax.ShapeDtypeStruct((192, 1536), BF16),
            jax.ShapeDtypeStruct((8, 3072), F32),
            jax.ShapeDtypeStruct((128, 128), BF16),
            jax.ShapeDtypeStruct((NC, NY, NZ, 48, 128), BF16),
            jax.ShapeDtypeStruct((NZ, 96, 128), BF16),
        ),
        in_specs=[pl.BlockSpec(memory_space=pltpu.SMEM), ANY, ANY, VM, VM, ANY, ANY, ANY],
        out_specs=(VM, VM, VM, VM, VM, VM),
        scratch_shapes=scratch_list(),
        compiler_params=pltpu.CompilerParams(
            collective_id=1, has_side_effects=True, vmem_limit_bytes=60 * 1024 * 1024
        ),
        name="whole",
    )(counts, tok, cot, cond, wq, up, down, mm)


def tail_kernel(
    counts, attn, grad, tok, mod, act, ig, pieces,
    attn_out, token_grad, down_out, up_out, mod_grad,
    ig_wide, sorted_grad,
):
    rows, width = tok.shape
    part = rows // 2
    dp = lax.axis_index("dp")
    perm = sorting(counts[0, dp], counts[1, dp], rows)
    attn_out[...] = tn(perm, attn[...]).astype(BF16)
    for img in range(2):
        at = slice(img * part, (img + 1) * part)
        x = nn(perm[at], tok[...])
        centred = x - jnp.mean(x, axis=1, keepdims=True)
        inverse = lax.rsqrt(jnp.mean(centred * centred, axis=1, keepdims=True) + EPSILON)
        normed = centred * inverse
        g = (1.0 + mod[img : img + 1, width:]) * grad[at, :].astype(F32)
        sorted_grad[at, :] = (
            inverse
            * (g - jnp.mean(g, axis=1, keepdims=True) - normed * jnp.mean(g * normed, axis=1, keepdims=True))
        ).astype(BF16)
    token_grad[...] = tn(perm, sorted_grad[...]).astype(BF16)

    ig_wide[...] = ig[...].reshape(3072, 128).astype(F32)
    for j in range(24):
        total = jnp.zeros((128, 128), F32)
        for img in range(2):
            part = ig_wide[pl.ds(img * 24 + j, 64, stride=48), :].astype(BF16)
            total += tn(act[img * 64 : (img + 1) * 64], part)
        mod_grad[:, j * 128 : (j + 1) * 128] = total[0:48]

    place = dp % (NZ * NC)
    flat = pieces[...].astype(F32)

    def tiles(i):
        triple = jnp.concatenate([flat[k, 24 * i : 24 * i + 24] for k in range(NZ)], axis=0).astype(BF16)
        return [triple[j * 64 : (j + 1) * 64] for j in range(3)]

    row = lax.broadcasted_iota(jnp.int32, (128, 128), 0)
    col = lax.broadcasted_iota(jnp.int32, (128, 128), 1)
    total = jnp.zeros((64, 128), F32)
    for i, tile in enumerate(tiles(0) + tiles(1) + tiles(2)):
        total += nn(tile, jnp.where(row + 128 * i == col + 72 * place, 1.0, 0.0).astype(BF16))
    up_out[...] = total[:, :72]
    total = jnp.zeros((128, 64), F32)
    for i, tile in enumerate(tiles(3)):
        total += nt(jnp.where(col + 128 * i == row + 24 * place, 1.0, 0.0).astype(BF16), tile)
    down_out[...] = total[:24]


def tail(counts, attn, grad, tok, mod, act, ig, pieces):
    return pl.pallas_call(
        tail_kernel,
        out_shape=(
            jax.ShapeDtypeStruct((192, 1536), BF16),
            jax.ShapeDtypeStruct((192, 1536), BF16),
            jax.ShapeDtypeStruct((24, 64), F32),
            jax.ShapeDtypeStruct((64, 72), F32),
            jax.ShapeDtypeStruct((48, 3072), F32),
        ),
        in_specs=[pl.BlockSpec(memory_space=pltpu.SMEM)] + [VM] * 7,
        out_specs=(VM, VM, VM, VM, VM),
        scratch_shapes=[pltpu.VMEM((3072, 128), F32), pltpu.VMEM((192, 1536), BF16)],
        compiler_params=pltpu.CompilerParams(vmem_limit_bytes=60 * 1024 * 1024),
        name="tail",
    )(counts, attn, grad, tok, mod, act, ig, pieces)


def body(
    tokens,
    cotangent,
    condition,
    per_image_rows,
    query_key_value_weight,
    adapter_down,
    adapter_up,
    modulation_matrix,
):
    counts = per_image_rows.T
    attn, grad, mod, act, ig, pieces = whole(
        counts,
        tokens[0],
        cotangent[0],
        condition[0],
        query_key_value_weight,
        adapter_up,
        adapter_down.T,
        modulation_matrix,
    )
    attention, token_grad, down_grad, up_grad, mod_grad = tail(
        counts, attn, grad, tokens[0], mod, act, ig, pieces
    )
    return attention[None], token_grad[None], down_grad, up_grad, mod_grad


def solution(mesh):
    in_specs = (
        P("dp", "seq", None),
        P("dp", "seq", None),
        P("dp", None, None),
        P(),
        P("dp", None),
        P(),
        P(),
        P("dp", None),
    )
    out_specs = (
        P("dp", "seq", None),
        P("dp", "seq", None),
        P("dp", None),
        P(None, "dp"),
        P("dp", None),
    )
    return jax.shard_map(body, mesh=mesh, in_specs=in_specs, out_specs=out_specs, check_vma=False)
```
